32 devices in a mesh: seq: 2 (over y), row: 4 (over z), col: 4 (over x, core).
Axes of the slice: x: 2, y: 2, z: 4, core: 2. Of those that a mesh axis runs over, the one named last changes fastest.
Arguments:
- tokens: bfloat16 [4, 2048, 1088], P('row', 'seq', 'col'), may hold values from -6 to 6
- prefix: int32 [4], P('row'), may hold values from 204 to 1024, as said below
- ln1_gain: bfloat16 [1088], P('col'), may hold values from 0.5 to 1.5
- ln1_bias: bfloat16 [1088], P('col'), may hold values from -3 to 3
- w_qkv: bfloat16 [1088, 3, 1088], P('row', None, 'col'), may hold values from -1 to 1
- b_qv: bfloat16 [2, 1088], P(None, 'col'), may hold values from -3 to 3
- w_out: bfloat16 [1088, 1088], P('row'), may hold values from -1 to 1
- b_out: bfloat16 [1088], replicated, may hold values from -3 to 3
- ln2_gain: bfloat16 [1088], P('col'), may hold values from 0.5 to 1.5
- ln2_bias: bfloat16 [1088], P('col'), may hold values from -3 to 3
- w_up: bfloat16 [1088, 4352], P('row', 'col'), may hold values from -0.1875 to 0.1875
- b_up: bfloat16 [4352], P('col'), may hold values from -3 to 3
- w_down: bfloat16 [4352, 1088], P('col', 'row'), may hold values from -0.09375 to 0.09375
- b_down: bfloat16 [1088], P('col'), may hold values from -3 to 3
- cotangent: bfloat16 [4, 2048, 1088], P('row', 'seq', 'col'), may hold values from -6 to 6
Outputs:
- block_out: bfloat16 [4, 2048, 1088], P('row', 'seq', 'col')
- grad_tokens: float32 [4, 2048, 1088], P('row', 'seq', 'col')
- grad_ln1_gain: float32 [1088], P('col')
- grad_ln1_bias: float32 [1088], P('col')
- grad_w_qkv: float32 [1088, 3, 1088], P(('seq', 'row'), None, 'col')
- grad_b_qv: float32 [2, 1088], P(None, 'col')
- grad_w_out: float32 [1088, 1088], P(('seq', 'row'))
- grad_b_out: float32 [1088], replicated
- grad_ln2_gain: float32 [1088], P('col')
- grad_ln2_bias: float32 [1088], P('col')
- grad_w_up: float32 [1088, 4352], P(('seq', 'row'), 'col')
- grad_b_up: float32 [4352], P('col')
- grad_w_down: float32 [4352, 1088], P('col', ('seq', 'row'))
- grad_b_down: float32 [1088], P('col')
- clipped_qkv: float32 [1088, 3, 1088], P('row', None, 'col')
- head_max: float32 [17], replicated
The draws below stay inside these ranges and needn't reach their ends.
Inputs may be any that keep to these rules, and one draw needn't show every extreme that they name: Positions below a sequence's prefix length attend to each other both ways; some sequence has the largest and some the smallest allowed length.
All inputs are finite; a program needn't handle non-finite values.
Results may differ from the reference program's by a relative error of at most 0.019.
Values may be sent and summed in bfloat16 or wider, within the bound.
No kernel may reach another device: no remote copies, remote signals or barrier semaphores. Data moves between devices by JAX's collectives and lax.ppermute only.
A program may use at most 448 MiB of HBM per device.

```python
import math
import jax
import jax.numpy as jnp
from jax import lax

D = 1088
H = 17
E = 64
FF = 4352
LEN = 2048
SEQS = 4


def draw_prefix(key, part):
    low_end = LEN // 10
    high_end = LEN // 2
    keys_drawn = jax.random.split(key, 3)
    lengths = jax.random.randint(keys_drawn[0], (SEQS,), low_end, high_end + 1)
    chosen = jax.random.randint(keys_drawn[1], (), 0, SEQS)
    other_one = (chosen + 1 + jax.random.randint(keys_drawn[2], (), 0, SEQS - 1)) % SEQS
    places = jnp.arange(SEQS)
    lengths = jnp.where(places == chosen, high_end, lengths)
    lengths = jnp.where(places == other_one, low_end, lengths)
    return lengths.astype(jnp.int32)


def draw_w_qkv(key, part):
    keys_drawn = jax.random.split(key, 2)
    base = jax.random.truncated_normal(keys_drawn[0], -4.0, 4.0, (D, 3, D), jnp.float32) * D ** (-0.5)
    head_scale = jnp.exp(jax.random.uniform(keys_drawn[1], (2, H), jnp.float32, math.log(0.9), math.log(1.5)))
    column_scale = jnp.repeat(head_scale, E, axis=1)
    column_scale = jnp.concatenate([column_scale, jnp.ones((1, D), jnp.float32)], axis=0)
    return (base * column_scale[None]).astype(jnp.bfloat16)


def steps_of(key, extent, cuts, low, largest):
    def one(position, parts):
        draws = jax.random.uniform(jax.random.fold_in(jax.random.fold_in(key, 6), position), (parts,), jnp.float32, low / len(cuts), largest / len(cuts))
        return jnp.repeat(jnp.exp(draws), extent[position] // parts).reshape((-1,) + (1,) * (len(extent) - position - 1))

    gain = one(*cuts[0])
    for cut in cuts[1:]:
        gain = gain * one(*cut)
    return gain


def bell_draw(own_key, extent, scale, bound, cuts=(), kind=jnp.bfloat16):
    loudness = steps_of(own_key, extent, cuts, -0.22, 0.18) if cuts else 1.0
    entries = jax.random.normal(own_key, extent, jnp.float32) * scale * loudness
    return jnp.minimum(jnp.maximum(entries, -bound), bound).astype(kind)


def setup_inputs(seed: int = 0) -> dict:
    streams_of = jax.random.split(jax.random.key(seed), 16)
    tokens = bell_draw(streams_of[0], (SEQS, LEN, D), 1.0, 6.0, ((0, 4), (1, 2), (2, 4)))
    prefix = draw_prefix(jax.random.fold_in(streams_of[15], 71), 0)
    ln1_gain = jnp.clip(1.0 + 0.1 * jax.random.normal(streams_of[2], (D,), jnp.float32), 0.5, 1.5).astype(jnp.bfloat16)
    ln1_bias = bell_draw(streams_of[3], (D,), 0.5, 3.0, ((0, 4),))
    w_qkv = draw_w_qkv(jax.random.fold_in(streams_of[15], 71), 0)
    b_qv = bell_draw(streams_of[5], (2, D), 0.5, 3.0, ((1, 4),))
    w_out = bell_draw(streams_of[6], (D, D), (D // 32) ** -0.5, 1.0, ((0, 4),))
    b_out = bell_draw(streams_of[7], (D,), 0.5, 3.0)
    ln2_gain = jnp.clip(1.0 + 0.1 * jax.random.normal(streams_of[8], (D,), jnp.float32), 0.5, 1.5).astype(jnp.bfloat16)
    ln2_bias = bell_draw(streams_of[9], (D,), 0.5, 3.0, ((0, 4),))
    w_up = bell_draw(streams_of[10], (D, FF), D ** -0.5, 0.1875, ((0, 4), (1, 4)))
    b_up = bell_draw(streams_of[11], (FF,), 0.5, 3.0, ((0, 4),))
    w_down = bell_draw(streams_of[12], (FF, D), FF ** -0.5, 0.09375, ((0, 4), (1, 4)))
    b_down = bell_draw(streams_of[13], (D,), 0.5, 3.0, ((0, 4),))
    cotangent = bell_draw(streams_of[14], (SEQS, LEN, D), 1.0, 6.0, ((0, 4), (1, 2), (2, 4)))
    return {"tokens": tokens, "prefix": prefix, "ln1_gain": ln1_gain, "ln1_bias": ln1_bias, "w_qkv": w_qkv, "b_qv": b_qv, "w_out": w_out, "b_out": b_out, "ln2_gain": ln2_gain, "ln2_bias": ln2_bias, "w_up": w_up, "b_up": b_up, "w_down": w_down, "b_down": b_down, "cotangent": cotangent}


norm_eps = 1e-05
neg_fill = -1e+30
clip_limit = 8.0
highest = lax.Precision.HIGHEST

@jax.custom_vjp
def low(v):
    return lax.optimization_barrier(v.astype(jnp.bfloat16)).astype(jnp.float32)

@jax.custom_vjp
def low_back(v):
    return v

def low_keep(v):
    return (low(v), None)

def low_pass(kept, grad):
    return (grad,)

def back_keep(v):
    return (v, None)

def back_low(kept, grad):
    return (low(grad),)
low.defvjp(low_keep, low_pass)
low_back.defvjp(back_keep, back_low)

def layer_norm(values, gain_vec, bias_vec):
    center = values - lax.optimization_barrier(jnp.mean(values, axis=-1, keepdims=True))
    spread = lax.optimization_barrier(jnp.mean(center * center, axis=-1, keepdims=True))
    return center * lax.rsqrt(spread + norm_eps) * gain_vec + bias_vec

def visible(query_pos, key_pos, prefix_len):
    causal = key_pos[None, :] <= query_pos[:, None]
    both_prefix = (query_pos[:, None] < prefix_len) & (key_pos[None, :] < prefix_len)
    return causal | both_prefix

def attend(query_block, first_row, keys_all, values_all, prefix_len):
    block_len = query_block.shape[0]
    query_pos = first_row + jnp.arange(block_len, dtype=jnp.int32)
    key_pos = jnp.arange(keys_all.shape[0], dtype=jnp.int32)
    scores = jnp.einsum('qhe,khe->hqk', query_block, keys_all, precision=highest) * E ** (-0.5)
    scores = low_back(scores)
    seen = visible(query_pos, key_pos, prefix_len)[None]
    masked = jnp.where(seen, scores, neg_fill)
    score_top = lax.optimization_barrier(jnp.max(masked, axis=(1, 2)))
    log_total = jax.nn.logsumexp(masked, axis=-1, keepdims=True)
    softmax_w = low(jnp.exp(masked - log_total))
    outcome = jnp.einsum('hqk,khe->qhe', softmax_w, values_all, precision=highest)
    return (outcome, score_top)

def sequence_forward(params, seq_tokens, prefix_len):
    gain_one, bias_one, wqkv, bqv, wout, bout, gain_two, bias_two, wup, bup, wdown, bdown = params
    normed_one = low(layer_norm(seq_tokens, gain_one, bias_one))
    projected = jnp.einsum('td,dkf->tkf', normed_one, wqkv, precision=highest)
    bias_three = jnp.stack([bqv[0], jnp.zeros_like(bqv[0]), bqv[1]])
    qkv = low_back(low(projected + bias_three[None]))
    queries = qkv[:, 0].reshape(LEN, H, E)
    keys_all = qkv[:, 1].reshape(LEN, H, E)
    values_all = qkv[:, 2].reshape(LEN, H, E)
    block_len = math.gcd(LEN, 512)
    block_total = LEN // block_len
    query_blocks = queries.reshape(block_total, block_len, H, E)
    starts = (jnp.arange(block_total, dtype=jnp.int32) * block_len).astype(jnp.int32)
    attend_saved = jax.checkpoint(attend)

    def one_block(packed):
        return attend_saved(packed[0], packed[1], keys_all, values_all, prefix_len)
    outcomes, tops = lax.map(one_block, (query_blocks, starts))
    attn = low_back(low(outcomes.reshape(LEN, D)))
    branch = low_back(jnp.dot(attn, wout, precision=highest) + bout)
    after_attn = seq_tokens + branch
    normed_two = low(layer_norm(after_attn, gain_two, bias_two))
    pre_act = low_back(jnp.dot(normed_two, wup, precision=highest) + bup)
    act = low(jax.nn.gelu(pre_act, approximate=False))
    result = after_attn + jnp.dot(act, wdown, precision=highest) + bdown
    return (result, lax.optimization_barrier(jnp.max(tops, axis=0)))

def reference(tokens, prefix, ln1_gain, ln1_bias, w_qkv, b_qv, w_out, b_out, ln2_gain, ln2_bias, w_up, b_up, w_down, b_down, cotangent):
    params = tuple((arr.astype(jnp.float32) for arr in (ln1_gain, ln1_bias, w_qkv, b_qv, w_out, b_out, ln2_gain, ln2_bias, w_up, b_up, w_down, b_down)))
    tokens_f = tokens.astype(jnp.float32)
    forward_saved = jax.checkpoint(sequence_forward)

    def total_map(all_tokens, weights):

        def one_seq(packed):
            return forward_saved(weights, packed[0], packed[1])
        outputs, tops = lax.map(one_seq, (all_tokens, prefix))
        return (outputs, tops)
    outputs, vjp_fn, tops = jax.vjp(total_map, tokens_f, params, has_aux=True)
    grad_x, grad_params = vjp_fn(cotangent.astype(jnp.float32))
    head_max = lax.optimization_barrier(jnp.max(tops, axis=0))
    clip_factor = clip_limit / jnp.maximum(head_max, clip_limit)
    column_root = jnp.repeat(jnp.sqrt(clip_factor), E)
    scale_three = jnp.stack([column_root, column_root, jnp.ones_like(column_root)])
    clipped_qkv = params[2] * scale_three[None]
    return (outputs.astype(jnp.bfloat16), grad_x, grad_params[0], grad_params[1], grad_params[2], grad_params[3], grad_params[4], grad_params[5], grad_params[6], grad_params[7], grad_params[8], grad_params[9], grad_params[10], grad_params[11], clipped_qkv, head_max)
```

```python
import functools

import jax
import jax.numpy as jnp
from jax import lax
from jax.experimental import pallas as pl
from jax.experimental.pallas import tpu as pltpu
from jax.sharding import PartitionSpec as P

H = 17
E = 64

norm_eps = 1e-05
neg_fill = -1e30
clip_limit = 8.0

f32 = jnp.float32
bf16 = jnp.bfloat16


def dot_nn(left, right):
    return lax.dot_general(left, right, (((1,), (0,)), ((), ())), preferred_element_type=f32)


def dot_nt(left, right):
    return lax.dot_general(left, right, (((1,), (1,)), ((), ())), preferred_element_type=f32)


def dot_tn(left, right):
    return lax.dot_general(left, right, (((0,), (0,)), ((), ())), preferred_element_type=f32)


def block_limits(info, block, rows):
    prefix_len = info[0]
    query_lo = info[1] + block * rows
    query_hi = query_lo + rows - 1
    in_prefix = query_lo < prefix_len
    limit_max = jnp.where(in_prefix, jnp.maximum(prefix_len - 1, query_hi), query_hi)
    limit_min = jnp.where(in_prefix, prefix_len - 1, query_lo)
    return prefix_len, query_lo, limit_max, limit_min


def attn_fwd_body(
    slots, rows, keys, info, q_ref, kv_ref, attn_ref, exact_ref, lse_ref, top_ref, m_s, l_s, acc_s
):
    block = pl.program_id(0)
    width = slots * E
    prefix_len, query_lo, limit_max, limit_min = block_limits(info, block, rows)
    n_need = limit_max // keys + 1
    n_full = (limit_min + 1) // keys
    positions = query_lo + lax.broadcasted_iota(jnp.int32, (rows, 1), 0)
    limit = jnp.where(positions < prefix_len, prefix_len - 1, positions)
    m_s[...] = jnp.full_like(m_s, neg_fill)
    l_s[...] = jnp.zeros_like(l_s)
    acc_s[...] = jnp.zeros_like(acc_s)

    def step(index, masked):
        start = pl.multiple_of(index * keys, keys)
        if masked:
            seen = (start + lax.broadcasted_iota(jnp.int32, (rows, keys), 1)) <= limit
        for h in range(slots):
            here = slice(h * E, h * E + E)
            there = slice(width + h * E, width + h * E + E)
            scores = dot_nt(q_ref[:, here], kv_ref[pl.ds(start, keys), here])
            if masked:
                scores = jnp.where(seen, scores, neg_fill)
            old_max = m_s[h]
            new_max = jnp.maximum(old_max, jnp.max(scores, axis=1, keepdims=True))
            weights = jnp.exp(scores - new_max[:, :1])
            shrink = jnp.exp(old_max - new_max)
            l_s[h] = l_s[h] * shrink + jnp.sum(weights, axis=1, keepdims=True)
            acc_s[h] = acc_s[h] * shrink[:, :E] + dot_nn(
                weights.astype(bf16), kv_ref[pl.ds(start, keys), there]
            )
            m_s[h] = new_max

    @pl.loop(0, n_full)
    def _(index):
        step(index, False)

    @pl.loop(n_full, n_need)
    def _(index):
        step(index, True)

    @pl.when(block == 0)
    def _():
        top_ref[...] = jnp.full_like(top_ref, neg_fill)

    for h in range(slots):
        here = slice(h * E, h * E + E)
        row_max, row_sum = m_s[h], l_s[h]
        outcome = acc_s[h] / row_sum[:, :E]
        exact_ref[:, here] = outcome
        attn_ref[:, here] = outcome.astype(bf16)
        lse_ref[:, h : h + 1] = (row_max + jnp.log(row_sum))[:, :1]
        top_ref[h : h + 1, :] = jnp.maximum(
            top_ref[h : h + 1, :], jnp.max(row_max, axis=0, keepdims=True)
        )


def attn_fwd(info, queries, kv_all, slots, rows=256, keys=512):
    count, width = queries.shape
    total = kv_all.shape[0]
    row_block = pl.BlockSpec((rows, width), lambda i, _: (i, 0))
    return pl.pallas_call(
        functools.partial(attn_fwd_body, slots, rows, keys),
        grid_spec=pltpu.PrefetchScalarGridSpec(
            num_scalar_prefetch=1,
            grid=(count // rows,),
            in_specs=[row_block, pl.BlockSpec((total, 2 * width), lambda i, _: (0, 0))],
            out_specs=[
                row_block,
                row_block,
                pl.BlockSpec((rows, 8), lambda i, _: (i, 0)),
                pl.BlockSpec((8, 128), lambda i, _: (0, 0)),
            ],
            scratch_shapes=[
                pltpu.VMEM((slots, rows, 128), f32),
                pltpu.VMEM((slots, rows, 128), f32),
                pltpu.VMEM((slots, rows, E), f32),
            ],
        ),
        out_shape=[
            jax.ShapeDtypeStruct((count, width), bf16),
            jax.ShapeDtypeStruct((count, width), f32),
            jax.ShapeDtypeStruct((count, 8), f32),
            jax.ShapeDtypeStruct((8, 128), f32),
        ],
        compiler_params=pltpu.CompilerParams(vmem_limit_bytes=48 * 2**20),
        cost_estimate=pl.CostEstimate(
            flops=20 * 10**9, bytes_accessed=8 * 10**6, transcendentals=8 * 10**6
        ),
        name="attn_fwd",
    )(info, queries, kv_all)


def attn_bwd_body(
    slots, rows, keys, key_first, info, q_ref, kv_ref, do_ref, lse_ref, dot_ref, dq_ref, dkv_ref
):
    block = pl.program_id(0)
    width = slots * E
    n_blocks = kv_ref.shape[0] // keys
    prefix_len, query_lo, limit_max, limit_min = block_limits(info, block, rows)
    n_need = jnp.clip((limit_max - key_first) // keys + 1, 0, n_blocks)
    n_full = jnp.clip((limit_min - key_first + 1) // keys, 0, n_blocks)
    positions = query_lo + lax.broadcasted_iota(jnp.int32, (1, rows), 1)
    limit = jnp.where(positions < prefix_len, prefix_len - 1, positions) - key_first

    @pl.when(block == 0)
    def _():
        dkv_ref[...] = jnp.zeros_like(dkv_ref)

    dq_ref[...] = jnp.zeros_like(dq_ref)

    def step(index, masked):
        start = pl.multiple_of(index * keys, keys)
        if masked:
            seen = (start + lax.broadcasted_iota(jnp.int32, (keys, rows), 0)) <= limit
        for h in range(slots):
            here = slice(h * E, h * E + E)
            there = slice(width + h * E, width + h * E + E)
            q_head, do_head = q_ref[:, here], do_ref[:, here]
            k_head = kv_ref[pl.ds(start, keys), here]
            v_head = kv_ref[pl.ds(start, keys), there]
            probs = jnp.exp(dot_nt(k_head, q_head) - lse_ref[h : h + 1, :])
            if masked:
                probs = jnp.where(seen, probs, 0.0)
            dkv_ref[pl.ds(start, keys), there] += dot_nn(probs.astype(bf16), do_head)
            grad_probs = dot_nt(v_head, do_head)
            grad_scores = (probs * (grad_probs - dot_ref[h : h + 1, :])).astype(bf16)
            dkv_ref[pl.ds(start, keys), here] += dot_nn(grad_scores, q_head)
            dq_ref[:, here] += dot_tn(grad_scores, k_head)

    @pl.loop(0, n_full)
    def _(index):
        step(index, False)

    @pl.loop(n_full, n_need)
    def _(index):
        step(index, True)


def attn_bwd(info, queries, kv_all, grad_attn, lse_rows, dot_rows, slots, segment, rows=256, keys=256):
    count, width = queries.shape
    row_block = pl.BlockSpec((rows, width), lambda i, _: (i, 0))
    vec_block = pl.BlockSpec((8, rows), lambda i, _: (0, i))
    return pl.pallas_call(
        functools.partial(attn_bwd_body, slots, rows, keys, segment * count),
        grid_spec=pltpu.PrefetchScalarGridSpec(
            num_scalar_prefetch=1,
            grid=(count // rows,),
            in_specs=[
                row_block,
                pl.BlockSpec((count, 2 * width), lambda i, _: (segment, 0)),
                row_block,
                vec_block,
                vec_block,
            ],
            out_specs=[row_block, pl.BlockSpec((count, 2 * width), lambda i, _: (0, 0))],
        ),
        out_shape=[
            jax.ShapeDtypeStruct((count, width), f32),
            jax.ShapeDtypeStruct((count, 2 * width), f32),
        ],
        compiler_params=pltpu.CompilerParams(vmem_limit_bytes=48 * 2**20),
        cost_estimate=pl.CostEstimate(
            flops=25 * 10**9, bytes_accessed=8 * 10**6, transcendentals=8 * 10**6
        ),
        name="attn_bwd",
    )(info, queries, kv_all, grad_attn, lse_rows, dot_rows)


X_SWAP = [(0, 2), (2, 0), (1, 3), (3, 1)]
CORE_SWAP = [(0, 1), (1, 0), (2, 3), (3, 2)]


def swap_x(array):
    return lax.ppermute(array, "col", X_SWAP)


def swap_core(array):
    return lax.ppermute(array, "col", CORE_SWAP)


def ring(array, axis, shift):
    count = lax.axis_size(axis)
    return lax.ppermute(array, axis, [(i, (i + shift) % count) for i in range(count)])


def gather_col(shard, x_bit, core_bit):
    other = swap_x(shard)
    low = jnp.where(x_bit == 0, shard, other)
    high = jnp.where(x_bit == 0, other, shard)
    low_other = swap_core(low)
    high_other = swap_core(high)
    return (
        jnp.where(core_bit == 0, low, low_other),
        jnp.where(core_bit == 0, low_other, low),
        jnp.where(core_bit == 0, high, high_other),
        jnp.where(core_bit == 0, high_other, high),
    )


def scatter_col(parts, x_bit, core_bit):
    low_mine = jnp.where(core_bit == 0, parts[0], parts[1])
    low_theirs = jnp.where(core_bit == 0, parts[1], parts[0])
    high_mine = jnp.where(core_bit == 0, parts[2], parts[3])
    high_theirs = jnp.where(core_bit == 0, parts[3], parts[2])
    low = low_mine.astype(f32) + swap_core(low_theirs).astype(f32)
    high = high_mine.astype(f32) + swap_core(high_theirs).astype(f32)
    mine = jnp.where(x_bit == 0, low, high)
    theirs = jnp.where(x_bit == 0, high, low).astype(bf16)
    return mine + swap_x(theirs).astype(f32)


def gather_row(shard):
    count = lax.axis_size("row")
    index = lax.axis_index("row")
    size = shard.shape[0]
    half = size // 2
    whole = jnp.zeros((count * size,) + shard.shape[1:], shard.dtype)

    def put(whole, piece, owner, extra):
        start = (owner % count) * size + extra
        return lax.dynamic_update_slice_in_dim(whole, piece, start, 0)

    whole = put(whole, shard, index, 0)
    from_left = from_right = shard
    for step in range(1, count // 2):
        from_left = ring(from_left, "row", 1)
        from_right = ring(from_right, "row", -1)
        whole = put(whole, from_left, index - step + count, 0)
        whole = put(whole, from_right, index + step, 0)
    from_left = ring(from_left[:half], "row", 1)
    from_right = ring(from_right[half:], "row", -1)
    whole = put(whole, from_left, index + count // 2, 0)
    return put(whole, from_right, index + count // 2, half)


def scatter_seq_row(partial):
    seq_count, row_count = lax.axis_size("seq"), lax.axis_size("row")
    if seq_count != 2 or row_count != 4:
        return lax.psum_scatter(
            partial.astype(f32), ("seq", "row"), scatter_dimension=0, tiled=True
        )
    seq_index, row_index = lax.axis_index("seq"), lax.axis_index("row")
    half = partial.shape[0] // 2
    chunk = half // 4
    cut = partial.shape[1] // 256 * 128
    theirs = lax.dynamic_slice_in_dim(partial, (1 - seq_index) * half, half, 0)
    mine = lax.dynamic_slice_in_dim(partial, seq_index * half, half, 0)
    received = lax.ppermute(theirs, "seq", [(0, 1), (1, 0)])
    summed = mine.astype(f32) + received.astype(f32)

    def of(offset):
        return lax.dynamic_slice_in_dim(summed, (row_index + offset) % 4 * chunk, chunk, 0)

    far = of(2).astype(bf16)
    right_one = ring(far[:, :cut], "row", 1)
    left_one = ring(far[:, cut:], "row", -1)
    to_right, to_left = of(1), of(3)
    to_right = jnp.concatenate(
        [to_right[:, :cut] + right_one.astype(f32), to_right[:, cut:]], axis=1
    )
    to_left = jnp.concatenate([to_left[:, :cut], to_left[:, cut:] + left_one.astype(f32)], axis=1)
    right_two = ring(to_right.astype(bf16), "row", 1)
    left_two = ring(to_left.astype(bf16), "row", -1)
    return of(0) + right_two.astype(f32) + left_two.astype(f32)


def combine_axis(array, axis, join):
    total = array
    for shift in range(1, lax.axis_size(axis)):
        total = join(total, ring(array, axis, shift))
    return total


def norm_stats(values):
    mean = jnp.mean(values, axis=-1, keepdims=True)
    center = values - mean
    spread = jnp.mean(center * center, axis=-1, keepdims=True)
    return mean, lax.rsqrt(spread + norm_eps)


def gelu_exact(values):
    return jax.nn.gelu(values, approximate=False)


def on_device(
    tokens,
    prefix,
    ln1_gain,
    ln1_bias,
    w_qkv,
    b_qv,
    w_out,
    b_out,
    ln2_gain,
    ln2_bias,
    w_up,
    b_up,
    w_down,
    b_down,
    cotangent,
):
    seq_count = lax.axis_size("seq")
    row_count = lax.axis_size("row")
    col_count = lax.axis_size("col")
    seq_index = lax.axis_index("seq")
    col_index = lax.axis_index("col")
    x_bit = col_index // 2
    core_bit = col_index % 2
    span = tokens.shape[1]
    part = tokens.shape[2]
    full = part * col_count
    quarter = span // col_count
    slots = (H + col_count - 1) // col_count
    width = slots * E
    spare = width - part
    fewer = H // col_count
    head_first = jnp.where(col_index == 0, 0, 1 + fewer * col_index)
    head_count = jnp.where(col_index == 0, fewer + 1, fewer)
    column_shift = head_first * E - col_index * part
    info = jnp.stack([prefix[0], seq_index * span])

    next_to_here = [(i + 1, i) for i in range(col_count - 1)]
    here_to_next = [(i, i + 1) for i in range(col_count - 1)]
    slot_column = lax.broadcasted_iota(jnp.int32, (1, 3 * width), 1)
    slot_part, slot_index = slot_column // width, slot_column % width
    slot_source = jnp.where(slot_index < head_count * E, slot_index + column_shift, -1)
    own_row = lax.broadcasted_iota(jnp.int32, (3 * part, 1), 0)
    pick_own = ((own_row // part == slot_part) & (own_row % part == slot_source)).astype(bf16)
    next_row = lax.broadcasted_iota(jnp.int32, (3 * spare, 1), 0)
    pick_next = (
        (next_row // spare == slot_part) & (next_row % spare + part == slot_source)
    ).astype(bf16)
    qkv_edge = lax.ppermute(w_qkv[:, :, :spare], "col", next_to_here)
    w_heads_shard = (
        dot_nn(w_qkv.reshape(-1, 3 * part), pick_own)
        + dot_nn(qkv_edge.reshape(-1, 3 * spare), pick_next)
    ).astype(bf16)
    bias_own = jnp.concatenate([b_qv[0], jnp.zeros_like(b_qv[0]), b_qv[1]])[None]
    bias_edge = lax.ppermute(bias_own.reshape(3, part)[:, :spare], "col", next_to_here)
    bias_heads = dot_nn(bias_own, pick_own) + dot_nn(bias_edge.reshape(1, 3 * spare), pick_next)
    w_heads = gather_row(w_heads_shard)
    w_queries, w_keyvals = w_heads[:, :width], w_heads[:, width:]

    x_shard = tokens[0]
    x_full = jnp.concatenate(gather_col(x_shard, x_bit, core_bit), axis=1).astype(f32)
    vectors = jnp.stack([ln1_gain, ln1_bias, ln2_gain, ln2_bias])
    vectors = jnp.concatenate(gather_col(vectors, x_bit, core_bit), axis=1).astype(f32)
    gain_one, bias_one, gain_two, bias_two = (vectors[i] for i in range(4))

    def first_norm(values):
        mean, inv = norm_stats(values)
        return mean, inv, ((values - mean) * inv * gain_one + bias_one).astype(bf16)

    mean_one, inv_one, normed_one = first_norm(x_full)
    queries = (
        (dot_nn(normed_one, w_queries) + bias_heads[:, :width]).astype(bf16) * E ** (-0.5)
    ).astype(bf16)
    keyvals = (dot_nn(normed_one, w_keyvals) + bias_heads[:, width:]).astype(bf16)
    if seq_count == 2:
        x_before = lax.ppermute(x_shard, "seq", [(0, 1)])
        x_before = jnp.concatenate(gather_col(x_before, x_bit, core_bit), axis=1).astype(f32)
        normed_before = first_norm(x_before)[2]
        before = (dot_nn(normed_before, w_keyvals) + bias_heads[:, width:]).astype(bf16)
        kv_all = jnp.concatenate(
            [jnp.where(seq_index == 0, keyvals, before), jnp.where(seq_index == 0, before, keyvals)]
        )
    else:
        kv_all = lax.all_gather(keyvals, "seq", axis=0, tiled=True)

    w_out_all = gather_row(w_out)
    w_up_all = gather_row(w_up)
    w_down_t = gather_row(w_down.T)
    dy_full = jnp.concatenate(gather_col(cotangent[0], x_bit, core_bit), axis=1)

    attn_low, attn_exact, lse, tops = attn_fwd(info, queries, kv_all, slots)
    attn_all = jnp.concatenate(gather_col(attn_low, x_bit, core_bit), axis=1)
    lead = (fewer + 1) * E
    blocks = [w_out_all[:lead]]
    for device in range(1, col_count):
        first = (1 + fewer * device) * E
        blocks.append(
            jnp.pad(w_out_all[first : first + fewer * E], ((0, width - fewer * E), (0, 0)))
        )
    w_out_heads = jnp.concatenate(blocks)
    after_attn = x_full + dot_nn(attn_all, w_out_heads) + b_out.astype(f32)

    slot_head = jnp.arange(slots, dtype=jnp.int32)
    my_top = jnp.where(slot_head < head_count, tops[:slots, 0], neg_fill)
    head_ids = jnp.arange(H, dtype=jnp.int32)
    placed_top = jnp.max(
        jnp.where(
            head_ids[None] == (head_first + slot_head)[:, None], my_top[:, None], neg_fill
        ),
        axis=0,
    )[None]
    head_max = placed_top
    for axis in ("seq", "row", "col"):
        head_max = combine_axis(head_max, axis, jnp.maximum)
    head_max = head_max[0]

    mean_two, inv_two = norm_stats(after_attn)
    normed_two = ((after_attn - mean_two) * inv_two * gain_two + bias_two).astype(bf16)
    pre_act = dot_nn(normed_two, w_up_all) + b_up.astype(f32)
    act_low = gelu_exact(pre_act).astype(bf16)
    grad_act = dot_nn(dy_full, w_down_t)
    grad_pre = jax.vjp(gelu_exact, pre_act)[1](grad_act)[0].astype(bf16)
    normed_two_part = dot_nt(grad_pre, w_up_all).astype(bf16)
    back_two = scatter_col(
        [normed_two_part[i * quarter : (i + 1) * quarter] for i in range(col_count)],
        x_bit,
        core_bit,
    )
    down_part = dot_nt(act_low, w_down_t).astype(bf16)
    down_mine = scatter_col(
        [down_part[:, i * part : (i + 1) * part] for i in range(col_count)], x_bit, core_bit
    )

    def own_columns(array):
        picked = array[:, :part]
        for i in range(1, col_count):
            picked = jnp.where(col_index == i, array[:, i * part : (i + 1) * part], picked)
        return picked

    block_out = (own_columns(after_attn) + down_mine + b_down.astype(f32)).astype(bf16)[None]

    def own_rows(array):
        return lax.dynamic_slice_in_dim(array, col_index * quarter, quarter, 0)

    unit_two = (own_rows(after_attn) - own_rows(mean_two)) * own_rows(inv_two)
    unit_grad = back_two * gain_two
    grad_after = own_rows(dy_full).astype(f32) + own_rows(inv_two) * (
        unit_grad
        - jnp.mean(unit_grad, axis=1, keepdims=True)
        - unit_two * jnp.mean(unit_grad * unit_two, axis=1, keepdims=True)
    )
    grad_branch_rows = grad_after.astype(bf16)
    grad_branch = jnp.concatenate(gather_col(grad_branch_rows, x_bit, core_bit), axis=0)
    row_vectors = jnp.stack(
        [
            jnp.sum(back_two * unit_two, axis=0),
            jnp.sum(back_two, axis=0),
            jnp.sum(grad_branch_rows.astype(f32), axis=0),
        ]
    )
    row_vectors = row_vectors + swap_x(row_vectors)
    row_vectors = row_vectors + swap_core(row_vectors)

    grad_w_up = scatter_seq_row(dot_tn(normed_two, grad_pre).astype(bf16))
    grad_w_down = scatter_seq_row(dot_tn(dy_full, act_low).astype(bf16)).T

    w_out_mine = lax.dynamic_slice_in_dim(w_out_heads, col_index * width, width, 0)
    grad_attn = dot_nt(grad_branch, w_out_mine).astype(bf16)
    row_dot = jnp.sum(
        (grad_attn.astype(f32) * attn_exact).reshape(span, slots, E), axis=-1
    )
    dot_rows = jnp.pad(row_dot, ((0, 0), (0, 8 - slots))).T
    lse_rows = lse.T
    if seq_count == 2:
        dq_one, dkv_one = attn_bwd(
            info, queries, kv_all, grad_attn, lse_rows, dot_rows, slots, 0
        )
        dkv_there = lax.ppermute(dkv_one.astype(bf16), "seq", [(1, 0)])
        dq_two, dkv_two = attn_bwd(
            info, queries, kv_all, grad_attn, lse_rows, dot_rows, slots, 1
        )
        grad_queries = dq_one + dq_two
        grad_keyvals = jnp.where(seq_index == 0, dkv_one + dkv_there.astype(f32), dkv_two)
    else:
        grad_queries = 0.0
        pieces = []
        for segment in range(seq_count):
            dq_one, dkv_one = attn_bwd(
                info, queries, kv_all, grad_attn, lse_rows, dot_rows, slots, segment
            )
            grad_queries = grad_queries + dq_one
            pieces.append(dkv_one.astype(bf16))
        grad_keyvals = lax.psum_scatter(
            jnp.concatenate(pieces), "seq", scatter_dimension=0, tiled=True
        ).astype(f32)
    grad_heads = jnp.concatenate([grad_queries * E ** (-0.5), grad_keyvals], axis=1).astype(bf16)

    wide = dot_tn(attn_all, own_columns(grad_branch)).astype(bf16)
    rows_kept = [wide[:lead]]
    for device in range(1, col_count):
        rows_kept.append(wide[device * width : device * width + fewer * E])
    out_columns = scatter_seq_row(jnp.concatenate(rows_kept)).astype(bf16)
    grad_w_out = jnp.concatenate(gather_col(out_columns, x_bit, core_bit), axis=1).astype(f32)

    normed_one_part = dot_nt(grad_heads, w_heads).astype(bf16)
    back_one = scatter_col(
        [normed_one_part[:, i * part : (i + 1) * part] for i in range(col_count)],
        x_bit,
        core_bit,
    )
    grad_edge = dot_nt(grad_heads, pick_next).astype(bf16)
    edge = lax.ppermute(dot_tn(normed_one, grad_edge).astype(bf16), "col", here_to_next)
    grad_own = dot_nt(grad_heads, pick_own).astype(bf16)
    bias_grads = jnp.sum(grad_own.astype(f32), axis=0)[None]
    bias_more = lax.ppermute(
        jnp.sum(grad_edge.astype(f32), axis=0)[None], "col", here_to_next
    )

    def widen(narrow):
        return jnp.concatenate(
            [
                jnp.pad(narrow[:, i * spare : (i + 1) * spare], ((0, 0), (0, part - spare)))
                for i in range(3)
            ],
            axis=1,
        )

    qkv_partial = (dot_tn(normed_one, grad_own) + widen(edge).astype(f32)).astype(bf16)
    bias_grads = bias_grads + widen(bias_more)
    grad_w_qkv = scatter_seq_row(qkv_partial).reshape(-1, 3, part)

    unit_one = (x_shard.astype(f32) - mean_one) * inv_one
    unit_grad_one = back_one * ln1_gain.astype(f32)
    sums = jnp.stack(
        [jnp.sum(unit_grad_one, axis=1), jnp.sum(unit_grad_one * unit_one, axis=1)]
    )
    sums = sums + swap_x(sums)
    sums = (sums + swap_core(sums)) / full
    grad_tokens = (
        own_columns(grad_branch).astype(f32)
        + inv_one * (unit_grad_one - sums[0][:, None] - unit_one * sums[1][:, None])
    )[None]

    own_vectors = own_columns(row_vectors)
    small = jnp.concatenate(
        [
            jnp.sum(back_one * unit_one, axis=0),
            jnp.sum(back_one, axis=0),
            own_vectors[0],
            own_vectors[1],
            bias_grads[0, :part],
            bias_grads[0, 2 * part :],
            jnp.sum(cotangent[0].astype(f32), axis=0),
            jnp.sum(grad_pre.astype(f32), axis=0),
            row_vectors[2],
        ]
    )[None]
    for axis in ("seq", "row"):
        small = combine_axis(small, axis, jnp.add)
    small = small[0]

    def piece(start, length):
        return small[start : start + length]

    root_clip = jnp.sqrt(clip_limit / jnp.maximum(head_max, clip_limit))
    column_head = (col_index * part + jnp.arange(part, dtype=jnp.int32)) // E
    one_hot = (column_head[:, None] == head_ids[None, :]).astype(f32)
    column_root = jnp.sum(one_hot * root_clip[None, :], axis=1)
    scale_three = jnp.stack([column_root, column_root, jnp.ones_like(column_root)])
    clipped_qkv = w_qkv.astype(f32) * scale_three[None]
    return (
        block_out,
        grad_tokens,
        piece(0, part),
        piece(part, part),
        grad_w_qkv,
        jnp.stack([piece(4 * part, part), piece(5 * part, part)]),
        grad_w_out,
        piece(11 * part, full),
        piece(2 * part, part),
        piece(3 * part, part),
        grad_w_up,
        piece(7 * part, w_up.shape[1]),
        grad_w_down,
        piece(6 * part, part),
        clipped_qkv,
        head_max,
    )


def solution(mesh):
    placed = (
        P("row", "seq", "col"),
        P("row"),
        P("col"),
        P("col"),
        P("row", None, "col"),
        P(None, "col"),
        P("row", None),
        P(),
        P("col"),
        P("col"),
        P("row", "col"),
        P("col"),
        P("col", "row"),
        P("col"),
        P("row", "seq", "col"),
    )
    return jax.shard_map(
        on_device,
        mesh=mesh,
        in_specs=placed,
        out_specs=(
            P("row", "seq", "col"),
            P("row", "seq", "col"),
            P("col"),
            P("col"),
            P(("seq", "row"), None, "col"),
            P(None, "col"),
            P(("seq", "row"), None),
            P(),
            P("col"),
            P("col"),
            P(("seq", "row"), "col"),
            P("col"),
            P("col", ("seq", "row")),
            P("col"),
            P("row", None, "col"),
            P(),
        ),
        check_vma=False,
    )
```

```python
import functools

import jax
import jax.numpy as jnp
from jax import lax
from jax.experimental import pallas as pl
from jax.experimental.pallas import tpu as pltpu
from jax.sharding import PartitionSpec as P


H = 17
E = 64

norm_eps = 1e-05
neg_fill = -1e30
clip_limit = 8.0

f32 = jnp.float32
bf16 = jnp.bfloat16

VMEM = pl.BlockSpec(memory_space=pltpu.VMEM)
SMEM = pl.BlockSpec(memory_space=pltpu.SMEM)
ANY = pl.BlockSpec(memory_space=pl.ANY)


def dot_nn(left, right):
    return lax.dot_general(left, right, (((1,), (0,)), ((), ())), preferred_element_type=f32)


def dot_nt(left, right):
    return lax.dot_general(left, right, (((1,), (1,)), ((), ())), preferred_element_type=f32)


def dot_tn(left, right):
    return lax.dot_general(left, right, (((0,), (0,)), ((), ())), preferred_element_type=f32)


def params():
    return pltpu.CompilerParams(vmem_limit_bytes=50 * 2**20)


def cost(flops, moved, exps=0):
    return pl.CostEstimate(flops=int(flops), bytes_accessed=int(moved), transcendentals=int(exps))


def shape(dims, kind):
    return jax.ShapeDtypeStruct(dims, kind)


def rows_at(start, length):
    return pl.ds(pl.multiple_of(start, 16), length)


def assemble_body(plan, fill, starts, *refs):
    pieces, out_ref = refs[:-1], refs[-1]
    for piece, source, length, where in plan:
        out_ref[rows_at(starts[where], length), :] = pieces[piece][source : source + length, :]
    if fill:
        out_ref[out_ref.shape[0] - fill :, :] = jnp.zeros((fill, out_ref.shape[1]), bf16)


def whole(array):
    return pl.BlockSpec(array.shape, lambda *_: (0,) * array.ndim)


def assemble(starts, pieces, plan, rows, fill=0):
    result = shape((rows + fill, pieces[0].shape[1]), bf16)
    return pl.pallas_call(
        functools.partial(assemble_body, tuple(plan), fill),
        grid_spec=pltpu.PrefetchScalarGridSpec(
            num_scalar_prefetch=1,
            grid=(1,),
            in_specs=[whole(piece) for piece in pieces],
            out_specs=whole(result),
        ),
        out_shape=result,
        compiler_params=params(),
        cost_estimate=cost(0, rows * result.shape[1] * 4),
        name="assemble",
    )(starts, *pieces)


def first_norm_body(own, order, p0, p1, p2, p3, *refs):
    vec_ref, x_ref, n_ref, stat_ref = (refs[3], *refs[:3]) if own else refs
    part = p0.shape[0]
    full, count = x_ref.shape
    if own:
        vec_ref[full:, :] = jnp.zeros((vec_ref.shape[0] - full, vec_ref.shape[1]), f32)
    for n, piece in enumerate((p0, p1, p2, p3)):
        where = rows_at(order[n] * part, part)
        x_ref[where, :] = piece[:, :count]
        if own:
            vec_ref[where, :] = piece[:, count : count + 128].astype(f32)
    for start in range(0, count, 256):
        cols = slice(start, start + 256)
        x = x_ref[:, cols].astype(f32)
        mean = jnp.sum(x, axis=0, keepdims=True) * (1.0 / full)
        center = x - mean
        inv = lax.rsqrt(jnp.sum(center * center, axis=0, keepdims=True) * (1.0 / full) + norm_eps)
        n_ref[:, cols] = (center * inv * vec_ref[:full, 0:1] + vec_ref[:full, 1:2]).astype(bf16)
        stat_ref[0:1, cols] = mean
        stat_ref[1:2, cols] = inv


def first_norm(order, pieces, count, vectors=None):
    own = vectors is None
    full = pieces[0].shape[0] * 4
    results = [shape((full, count), bf16), shape((full, count), bf16), shape((8, count), f32)]
    operands = list(pieces)
    if own:
        results.append(shape((full + E, 128), f32))
    else:
        operands.append(vectors)
    return pl.pallas_call(
        functools.partial(first_norm_body, own),
        grid_spec=pltpu.PrefetchScalarGridSpec(
            num_scalar_prefetch=1,
            grid=(1,),
            in_specs=[whole(array) for array in operands],
            out_specs=[whole(result) for result in results],
        ),
        out_shape=results,
        compiler_params=params(),
        cost_estimate=cost(20 * full * count, full * count * 8),
        name="first_norm",
    )(order, *operands)


def head_weights_body(order, own, left, right, far_a, far_b, near, far, pick_own, pick_next, out_ref):
    size, cut = own.shape[0], far_a.shape[0]

    def put(owner, extra, rows, piece, edge):
        out_ref[rows_at(owner * size + extra, rows), :] = (
            dot_nn(piece, pick_own[...]) + dot_nn(edge, pick_next[...])
        ).astype(bf16)

    put(order[0], 0, size, own[...], near[:size, :])
    put(order[1], 0, size, left[...], near[size : 2 * size, :])
    put(order[3], 0, size, right[...], near[2 * size :, :])
    put(order[2], 0, cut, far_a[...], far[:cut, :])
    put(order[2], cut, size - cut, far_b[...], far[cut:, :])


def head_weights(order, pieces, pick_own, pick_next):
    result = shape((pieces[0].shape[0] * 4, pick_own.shape[1]), bf16)
    return pl.pallas_call(
        head_weights_body,
        grid_spec=pltpu.PrefetchScalarGridSpec(
            num_scalar_prefetch=1,
            grid=(1,),
            in_specs=[whole(array) for array in (*pieces, pick_own, pick_next)],
            out_specs=whole(result),
        ),
        out_shape=result,
        compiler_params=params(),
        cost_estimate=cost(2 * 960 * 960 * 1088, 6 * 10**6),
        name="head_weights",
    )(order, *pieces, pick_own, pick_next)


def project_body(width, info, w_ref, bias_ref, own_ref, before_ref, q_ref, kv_ref, w_s):
    step = pl.program_id(0)
    half = pl.num_programs(0) // 2
    mine = (step // half) == info[0]

    @pl.when(step == 0)
    def _():
        w_s[...] = w_ref[...].T

    def keyvals(n_ref):
        kv_ref[:width, :] = dot_nn(w_s[width : 2 * width, :], n_ref[...]).astype(bf16)
        kv_ref[width:, :] = (
            dot_nn(w_s[2 * width :, :], n_ref[...]) + bias_ref[rows_at(info[1], width), 5:6]
        ).astype(bf16)

    @pl.when(mine)
    def _():
        out = dot_nn(w_s[:width, :], own_ref[...]) + bias_ref[rows_at(info[1], width), 4:5]
        q_ref[...] = (out.astype(bf16).astype(f32) * E ** (-0.5)).astype(bf16)
        keyvals(own_ref)

    @pl.when(jnp.logical_not(mine))
    def _():
        keyvals(before_ref)


def project(info, w_heads, bias, own, before, block=512):
    full, count = own.shape
    wide = w_heads.shape[1]
    width = wide // 3
    steps = count // block
    return pl.pallas_call(
        functools.partial(project_body, width),
        grid_spec=pltpu.PrefetchScalarGridSpec(
            num_scalar_prefetch=1,
            grid=(2 * steps,),
            in_specs=[
                pl.BlockSpec((full, wide), lambda i, s: (0, 0)),
                pl.BlockSpec(bias.shape, lambda i, s: (0, 0)),
                pl.BlockSpec((full, block), lambda i, s: (0, jnp.clip(i - s[0] * steps, 0, steps - 1))),
                pl.BlockSpec(
                    (full, block), lambda i, s: (0, jnp.clip(i - (1 - s[0]) * steps, 0, steps - 1))
                ),
            ],
            out_specs=[
                pl.BlockSpec((width, block), lambda i, s: (0, jnp.clip(i - s[0] * steps, 0, steps - 1))),
                pl.BlockSpec((2 * width, block), lambda i, s: (0, i)),
            ],
            scratch_shapes=[pltpu.VMEM((wide, full), bf16)],
        ),
        out_shape=[shape((width, count), bf16), shape((2 * width, 2 * count), bf16)],
        compiler_params=params(),
        cost_estimate=cost(2 * full * count * 5 * width, 10 * 10**6),
        name="project",
    )(info, w_heads, bias, own, before)


def block_limits(info, block, rows):
    prefix_len = info[0]
    query_lo = info[1] + block * rows
    query_hi = query_lo + rows - 1
    in_prefix = query_lo < prefix_len
    limit_max = jnp.where(in_prefix, jnp.maximum(prefix_len - 1, query_hi), query_hi)
    limit_min = jnp.where(in_prefix, prefix_len - 1, query_lo)
    positions = query_lo + lax.broadcasted_iota(jnp.int32, (1, rows), 1)
    return limit_max, limit_min, jnp.where(positions < prefix_len, prefix_len - 1, positions)


def attn_fwd_body(
    slots, keys, first, info, q_ref, kv_ref, attn_ref, exact_ref, lse_ref, top_ref, k_s, m_s, l_s, acc_s
):
    width, rows = q_ref.shape
    limit_max, limit_min, limit = block_limits(info, first, rows)
    n_need = limit_max // keys + 1
    n_full = (limit_min + 1) // keys
    for h in range(slots):
        k_s[h] = kv_ref[h * E : h * E + E, :].T
    m_s[...] = jnp.full_like(m_s, neg_fill)
    l_s[...] = jnp.zeros_like(l_s)
    acc_s[...] = jnp.zeros_like(acc_s)

    def step(index, masked):
        start = pl.multiple_of(index * keys, keys)
        if masked:
            seen = (start + lax.broadcasted_iota(jnp.int32, (keys, rows), 0)) <= limit
        for h in range(slots):
            here, row = slice(h * E, h * E + E), slice(h, h + 1)
            scores = dot_nn(k_s[h, pl.ds(start, keys), :], q_ref[here, :])
            if masked:
                scores = jnp.where(seen, scores, neg_fill)
            old_max = m_s[row, :]
            new_max = jnp.maximum(old_max, jnp.max(scores, axis=0, keepdims=True))
            weights = jnp.exp(scores - new_max)
            shrink = jnp.exp(old_max - new_max)
            l_s[row, :] = l_s[row, :] * shrink + jnp.sum(weights, axis=0, keepdims=True)
            values = kv_ref[width + h * E : width + h * E + E, pl.ds(start, keys)]
            acc_s[here, :] = acc_s[here, :] * shrink + dot_nn(values, weights.astype(bf16))
            m_s[row, :] = new_max

    @pl.loop(0, n_full)
    def _(index):
        step(index, False)

    @pl.loop(n_full, n_need)
    def _(index):
        step(index, True)

    for h in range(slots):
        here, row = slice(h * E, h * E + E), slice(h, h + 1)
        outcome = acc_s[here, :] / l_s[row, :]
        exact_ref[here, :] = outcome
        attn_ref[here, :] = outcome.astype(bf16)
    row_max = m_s[...]
    lse_ref[...] = row_max + jnp.log(l_s[...])
    top = row_max[:, :128]
    for start in range(128, rows, 128):
        top = jnp.maximum(top, row_max[:, start : start + 128])
    top_ref[...] = top


def attn_fwd(info, queries, kv_all, slots, first, rows=512, keys=512):
    width = queries.shape[0]
    total = kv_all.shape[1]
    return pl.pallas_call(
        functools.partial(attn_fwd_body, slots, keys, first),
        grid_spec=pltpu.PrefetchScalarGridSpec(
            num_scalar_prefetch=1,
            grid=(1,),
            in_specs=[
                pl.BlockSpec((width, rows), lambda i, _: (0, first)),
                pl.BlockSpec((2 * width, total), lambda i, _: (0, 0)),
            ],
            out_specs=[
                pl.BlockSpec((width, rows), lambda i, _: (0, 0)),
                pl.BlockSpec((width, rows), lambda i, _: (0, 0)),
                pl.BlockSpec((8, rows), lambda i, _: (0, 0)),
                pl.BlockSpec((8, 128), lambda i, _: (0, 0)),
            ],
            scratch_shapes=[
                pltpu.VMEM((slots, total, E), bf16),
                pltpu.VMEM((8, rows), f32),
                pltpu.VMEM((8, rows), f32),
                pltpu.VMEM((width, rows), f32),
            ],
        ),
        out_shape=[
            shape((width, rows), bf16),
            shape((width, rows), f32),
            shape((8, rows), f32),
            shape((8, 128), f32),
        ],
        compiler_params=params(),
        cost_estimate=cost(8 * 10**9, 6 * 10**6, 4 * 10**6),
        name="attn_fwd",
    )(info, queries, kv_all)


def attn_bwd_body(slots, keys, key_first, more, last, info, *refs):
    if more:
        q_ref, kv_ref, do_ref, o_ref, lse_ref, dq_in, dq_ref, dkv_ref, k_s, v_s, acc_s, dkv_s = refs
    else:
        q_ref, kv_ref, do_ref, o_ref, lse_ref, dq_ref, dkv_ref, k_s, v_s, acc_s, dkv_s = refs
    block = pl.program_id(0)
    width, rows = q_ref.shape
    n_blocks = kv_ref.shape[1] // keys
    limit_max, limit_min, limit = block_limits(info, block, rows)
    n_need = jnp.clip((limit_max - key_first) // keys + 1, 0, n_blocks)
    n_full = jnp.clip((limit_min - key_first + 1) // keys, 0, n_blocks)
    limit = limit - key_first

    @pl.when(block == 0)
    def _():
        dkv_s[...] = jnp.zeros_like(dkv_s)
        for h in range(slots):
            k_s[h] = kv_ref[h * E : h * E + E, :].T
            v_s[h] = kv_ref[width + h * E : width + h * E + E, :].T

    if more:
        acc_s[...] = dq_in[...]
    else:
        acc_s[...] = jnp.zeros_like(acc_s)
    dots = [
        jnp.sum(
            do_ref[h * E : h * E + E, :].astype(f32) * o_ref[h * E : h * E + E, :],
            axis=0,
            keepdims=True,
        )
        for h in range(slots)
    ]

    def step(index, masked):
        start = pl.multiple_of(index * keys, keys)
        where = pl.ds(start, keys)
        if masked:
            seen = (start + lax.broadcasted_iota(jnp.int32, (keys, rows), 0)) <= limit
        for h in range(slots):
            here = slice(h * E, h * E + E)
            there = slice(width + h * E, width + h * E + E)
            q_head, do_head = q_ref[here, :], do_ref[here, :]
            probs = jnp.exp(dot_nn(k_s[h, where, :], q_head) - lse_ref[h : h + 1, :])
            if masked:
                probs = jnp.where(seen, probs, 0.0)
            grad_probs = dot_nn(v_s[h, where, :], do_head)
            grad_scores = (probs * (grad_probs - dots[h])).astype(bf16)
            dkv_s[there, where] += dot_nt(do_head, probs.astype(bf16))
            dkv_s[here, where] += dot_nt(q_head, grad_scores)
            acc_s[here, :] += dot_nn(kv_ref[here, where], grad_scores)

    @pl.loop(0, n_full)
    def _(index):
        step(index, False)

    @pl.loop(n_full, n_need)
    def _(index):
        step(index, True)

    if last:
        dq_ref[...] = (acc_s[...] * E ** (-0.5)).astype(bf16)
    else:
        dq_ref[...] = acc_s[...]

    @pl.when(block == pl.num_programs(0) - 1)
    def _():
        dkv_ref[...] = dkv_s[...].astype(bf16)


def attn_bwd(
    info, queries, kv_all, grad_attn, exact, lse, dq_in, slots, segment, last, rows=512, keys=512
):
    width, count = queries.shape
    more = dq_in is not None
    block = pl.BlockSpec((width, rows), lambda i, _: (0, i))
    return pl.pallas_call(
        functools.partial(attn_bwd_body, slots, keys, segment * count, more, last),
        grid_spec=pltpu.PrefetchScalarGridSpec(
            num_scalar_prefetch=1,
            grid=(count // rows,),
            in_specs=[
                block,
                pl.BlockSpec((2 * width, count), lambda i, _: (0, segment)),
                block,
                block,
                pl.BlockSpec((8, rows), lambda i, _: (0, i)),
            ]
            + [block] * more,
            out_specs=[block, pl.BlockSpec((2 * width, count), lambda i, _: (0, 0))],
            scratch_shapes=[
                pltpu.VMEM((slots, count, E), bf16),
                pltpu.VMEM((slots, count, E), bf16),
                pltpu.VMEM((width, rows), f32),
                pltpu.VMEM((2 * width, count), f32),
            ],
        ),
        out_shape=[
            shape((width, count), bf16 if last else f32),
            shape((2 * width, count), bf16),
        ],
        compiler_params=params(),
        cost_estimate=cost(16 * 10**9, 6 * 10**6, 4 * 10**6),
        name="attn_bwd",
    )(info, queries, kv_all, grad_attn, exact, lse, *([dq_in] if more else []))


def out_norm_body(starts, p0, p1, p2, p3, w_ref, x_ref, vec_ref, after_ref, n_ref, stat_ref, attn_ref, w_s):
    fewer = (attn_ref.shape[0] // E) // 4 * E
    w_s[...] = w_ref[: w_s.shape[1], :].T
    for n, piece in enumerate((p0, p1, p2, p3)):
        attn_ref[rows_at(starts[n], fewer), :] = piece[:fewer, :]

        @pl.when(starts[n] == 0)
        def _():
            attn_ref[fewer : piece.shape[0], :] = piece[fewer:, :]

    full, count = x_ref.shape
    for start in range(0, count, 256):
        cols = slice(start, start + 256)
        after = x_ref[:, cols].astype(f32) + (
            dot_nn(w_s[...], attn_ref[:, cols]) + vec_ref[:full, 6:7]
        )
        mean = jnp.sum(after, axis=0, keepdims=True) * (1.0 / full)
        center = after - mean
        inv = lax.rsqrt(jnp.sum(center * center, axis=0, keepdims=True) * (1.0 / full) + norm_eps)
        after_ref[:, cols] = after
        n_ref[:, cols] = (center * inv * vec_ref[:full, 2:3] + vec_ref[:full, 3:4]).astype(bf16)
        stat_ref[0:1, cols] = mean
        stat_ref[1:2, cols] = inv


def out_norm(starts, pieces, w_out, x_full, vectors, first):
    full = x_full.shape[0]
    rows, count = pieces[0].shape
    grid_spec = pltpu.PrefetchScalarGridSpec(
        num_scalar_prefetch=1,
        grid=(1,),
        in_specs=[whole(piece) for piece in pieces]
        + [
            pl.BlockSpec(w_out.shape, lambda i, _: (0, 0)),
            pl.BlockSpec((full, count), lambda i, _: (0, first)),
            pl.BlockSpec(vectors.shape, lambda i, _: (0, 0)),
        ],
        out_specs=[
            pl.BlockSpec((full, count), lambda i, _: (0, 0)),
            pl.BlockSpec((full, count), lambda i, _: (0, 0)),
            pl.BlockSpec((8, count), lambda i, _: (0, 0)),
            pl.BlockSpec((full, count), lambda i, _: (0, 0)),
        ],
        scratch_shapes=[pltpu.VMEM((full, full), bf16)],
    )
    return pl.pallas_call(
        out_norm_body,
        grid_spec=grid_spec,
        out_shape=[
            shape((full, count), f32),
            shape((full, count), bf16),
            shape((8, count), f32),
            shape((full, count), bf16),
        ],
        compiler_params=params(),
        cost_estimate=cost(2 * full * full * count, 10**7),
        name="out_norm",
    )(starts, *pieces, w_out, x_full, vectors)


def erf_parts(v):
    return 0.5 * (1.0 + lax.erf(v * (0.5**0.5))), jnp.exp(-0.5 * v * v)


def feed_body(n_ref, dy_ref, up_ref, down_t_ref, b_ref, act_ref, grad_ref, part_ref, bias_ref, up_s, down_s):
    step = pl.program_id(0)

    @pl.when(step == 0)
    def _():
        up_s[...] = up_ref[...].T
        down_s[...] = down_t_ref[...].T
        bias_ref[...] = jnp.zeros_like(bias_ref)

    pre = dot_nn(up_s[...], n_ref[...]) + b_ref[:, 0:1]
    grad_act = dot_nn(down_s[...], dy_ref[...])
    cdf, bell = erf_parts(pre)
    act_ref[...] = (pre * cdf).astype(bf16)
    grad = (grad_act * (cdf + pre * bell * 0.3989422804014327)).astype(bf16)
    grad_ref[...] = grad
    bias_ref[...] += dot_nn(grad, jnp.ones((grad.shape[1], 128), bf16))
    part_ref[0] = dot_nn(up_ref[...], grad).astype(bf16)


def feed(normed, dy, w_up, w_down_t, bias, block=256):
    full, count = normed.shape
    hidden = w_up.shape[1]
    cols = pl.BlockSpec((full, block), lambda i: (0, i))
    hid = pl.BlockSpec((hidden, block), lambda i: (0, i))
    return pl.pallas_call(
        feed_body,
        grid=(count // block,),
        in_specs=[
            cols,
            cols,
            pl.BlockSpec((full, hidden), lambda i: (0, 0)),
            pl.BlockSpec((full, hidden), lambda i: (0, 0)),
            pl.BlockSpec((hidden, 1), lambda i: (0, 0)),
        ],
        out_specs=[
            hid,
            hid,
            pl.BlockSpec((1, full, block), lambda i: (i, 0, 0)),
            pl.BlockSpec((hidden, 128), lambda i: (0, 0)),
        ],
        out_shape=[
            shape((hidden, count), bf16),
            shape((hidden, count), bf16),
            shape((count // block, full, block), bf16),
            shape((hidden, 128), f32),
        ],
        scratch_shapes=[pltpu.VMEM((hidden, full), bf16), pltpu.VMEM((hidden, full), bf16)],
        compiler_params=params(),
        cost_estimate=cost(6 * full * hidden * count, 2 * 10**7, 2 * hidden * count),
        name="feed",
    )(normed, dy, w_up, w_down_t, bias)


def second_back_body(index, mine_ref, got_ref, after_ref, dy_ref, stat_ref, vec_ref, out_ref, sums_ref):
    back = mine_ref[...] + got_ref[...].astype(f32)
    full = back.shape[0]
    mean, inv = stat_ref[0:1, :], stat_ref[1:2, :]
    unit = (after_ref[...] - mean) * inv
    grad = back * vec_ref[:full, 2:3]
    first = jnp.sum(grad, axis=0, keepdims=True) * (1.0 / full)
    second = jnp.sum(grad * unit, axis=0, keepdims=True) * (1.0 / full)
    total = dy_ref[...].astype(f32) + inv * (grad - first - unit * second)
    low = total.astype(bf16)
    out_ref[...] = low
    sums_ref[:, 0:1] = jnp.sum(back * unit, axis=1, keepdims=True)
    sums_ref[:, 1:2] = jnp.sum(back, axis=1, keepdims=True)
    sums_ref[:, 2:3] = jnp.sum(low.astype(f32), axis=1, keepdims=True)


def second_back(index, mine, got, after, dy, stats, vectors):
    full, count = mine.shape
    fixed = pl.BlockSpec((full, count), lambda i, c: (0, 0))
    moved = pl.BlockSpec((full, count), lambda i, c: (0, c[0]))
    return pl.pallas_call(
        second_back_body,
        grid_spec=pltpu.PrefetchScalarGridSpec(
            num_scalar_prefetch=1,
            grid=(1,),
            in_specs=[
                fixed,
                fixed,
                moved,
                moved,
                pl.BlockSpec((8, count), lambda i, c: (0, c[0])),
                pl.BlockSpec(vectors.shape, lambda i, c: (0, 0)),
            ],
            out_specs=[fixed, pl.BlockSpec((full, 8), lambda i, c: (0, 0))],
        ),
        out_shape=[shape((full, count), bf16), shape((full, 8), f32)],
        compiler_params=params(),
        cost_estimate=cost(20 * full * count, 5 * 10**6),
        name="second_back",
    )(index, mine, got, after, dy, stats, vectors)


def attn_grad_body(info, p0, p1, p2, p3, w_ref, branch_ref, out_ref):
    count = p0.shape[1]
    width = out_ref.shape[0]
    weights = w_ref[rows_at(info[0], width), :]
    real = lax.broadcasted_iota(jnp.int32, (width, 1), 0) < info[1]
    for n, piece in enumerate((p0, p1, p2, p3)):
        cols = pl.ds(pl.multiple_of(info[2 + n] * count, 128), count)
        branch_ref[:, cols] = piece[...]
        out_ref[:, cols] = jnp.where(real, dot_nn(weights, piece[...]), 0.0).astype(bf16)


def attn_grad(info, pieces, w_out, width):
    full, quarter = pieces[0].shape
    results = [shape((full, 4 * quarter), bf16), shape((width, 4 * quarter), bf16)]
    return pl.pallas_call(
        attn_grad_body,
        grid_spec=pltpu.PrefetchScalarGridSpec(
            num_scalar_prefetch=1,
            grid=(1,),
            in_specs=[whole(array) for array in (*pieces, w_out)],
            out_specs=[whole(result) for result in results],
        ),
        out_shape=results,
        compiler_params=params(),
        cost_estimate=cost(8 * full * quarter * width, 10**7),
        name="attn_grad",
    )(info, *pieces, w_out)


X_SWAP = [(0, 2), (2, 0), (1, 3), (3, 1)]
CORE_SWAP = [(0, 1), (1, 0), (2, 3), (3, 2)]


def swap_x(array):
    return lax.ppermute(array, "col", X_SWAP)


def swap_core(array):
    return lax.ppermute(array, "col", CORE_SWAP)


def swap_seq(array):
    return lax.ppermute(array, "seq", [(0, 1), (1, 0)])


def ring(array, axis, shift):
    count = lax.axis_size(axis)
    return lax.ppermute(array, axis, [(i, (i + shift) % count) for i in range(count)])


def after(array, *done):
    return lax.optimization_barrier((array,) + done)[0]


def gather_col(shard):
    other = swap_x(shard)
    beside = swap_core(jnp.stack([shard, other]))
    return shard, other, beside[0], beside[1]


def gather_col_after(shard, *done):
    other = after(swap_x(shard), *done)
    beside = swap_core(jnp.stack([shard, other]))
    return shard, other, beside[0], beside[1]


def scatter_col(parts, x_bit, core_bit):
    by_core = parts.reshape((2, 2) + parts.shape[1:])
    mine = lax.dynamic_index_in_dim(by_core, core_bit, 1, keepdims=False)
    theirs = lax.dynamic_index_in_dim(by_core, 1 - core_bit, 1, keepdims=False)
    got = swap_core(theirs)

    def of(index):
        return lax.dynamic_index_in_dim(mine, index, 0, keepdims=False).astype(
            f32
        ) + lax.dynamic_index_in_dim(got, index, 0, keepdims=False).astype(f32)

    return got, of(x_bit), swap_x(of(1 - x_bit).astype(bf16))


def seq_halves(partials):
    seq_index = lax.axis_index("seq")
    chunks = [p.reshape(2, 4, p.shape[0] // 8, p.shape[1]) for p in partials]
    mine = [lax.dynamic_index_in_dim(c, seq_index, 0, keepdims=False) for c in chunks]
    theirs = jnp.stack(
        [lax.dynamic_index_in_dim(c, 1 - seq_index, 0, keepdims=False) for c in chunks]
    )
    return jnp.stack(mine), swap_seq(theirs)


def row_chunk(halves, offset):
    index = (lax.axis_index("row") + offset) % 4

    def of(array):
        return lax.dynamic_index_in_dim(array, index, 1, keepdims=False).astype(f32)

    return of(halves[0]) + of(halves[1])


def row_sum_one(halves):
    far = row_chunk(halves, 2).astype(bf16)
    if far.shape[0] == 2:
        return ring(far[0], "row", 1), ring(far[1], "row", -1)
    cut = far.shape[2] // 256 * 128
    return ring(far[0, :, :cut], "row", 1), ring(far[0, :, cut:], "row", -1)


def row_sum_two(halves, far):
    to_right, to_left = row_chunk(halves, 1), row_chunk(halves, 3)
    one, two = (part.astype(f32) for part in far)
    if to_right.shape[0] == 2:
        to_right = jnp.stack([to_right[0] + one, to_right[1]])
        to_left = jnp.stack([to_left[0], to_left[1] + two])
    else:
        cut = one.shape[1]
        to_right = jnp.concatenate([to_right[0, :, :cut] + one, to_right[0, :, cut:]], axis=1)[None]
        to_left = jnp.concatenate([to_left[0, :, :cut], to_left[0, :, cut:] + two], axis=1)[None]
    return ring(to_right.astype(bf16), "row", 1), ring(to_left.astype(bf16), "row", -1)


def row_sum_end(halves, near):
    return row_chunk(halves, 0) + near[0].astype(f32) + near[1].astype(f32)


def scatter_plain(partial):
    return lax.psum_scatter(partial.astype(f32), ("seq", "row"), scatter_dimension=0, tiled=True)


def combine_axis(array, axis, join):
    total = array
    for shift in range(1, lax.axis_size(axis)):
        total = join(total, ring(array, axis, shift))
    return total


def on_device(
    tokens,
    prefix,
    ln1_gain,
    ln1_bias,
    w_qkv,
    b_qv,
    w_out,
    b_out,
    ln2_gain,
    ln2_bias,
    w_up,
    b_up,
    w_down,
    b_down,
    cotangent,
):
    seq_count = lax.axis_size("seq")
    row_count = lax.axis_size("row")
    col_count = lax.axis_size("col")
    fast = seq_count == 2 and row_count == 4
    seq_index = lax.axis_index("seq")
    row_index = lax.axis_index("row")
    col_index = lax.axis_index("col")
    x_bit = col_index // 2
    core_bit = col_index % 2
    span, part = tokens.shape[1], tokens.shape[2]
    full = part * col_count
    quarter = span // col_count
    fewer = H // col_count
    slots = fewer + 1
    width = slots * E
    spare = width - part

    def by_index(pieces):
        own, across, beside, other = pieces
        even = (jnp.where(core_bit == 0, own, beside), jnp.where(core_bit == 0, across, other))
        odd = (jnp.where(core_bit == 0, beside, own), jnp.where(core_bit == 0, other, across))
        return jnp.concatenate(
            [
                jnp.where(x_bit == 0, even[0], even[1]),
                jnp.where(x_bit == 0, odd[0], odd[1]),
                jnp.where(x_bit == 0, even[1], even[0]),
                jnp.where(x_bit == 0, odd[1], odd[0]),
            ],
            axis=1,
        )

    def first_head(device):
        return jnp.where(device == 0, 0, 1 + fewer * device)

    head_first = first_head(col_index)
    head_count = jnp.where(col_index == 0, fewer + 1, fewer)
    column_shift = head_first * E - col_index * part
    info = jnp.stack([prefix[0], seq_index * span]).astype(jnp.int32)
    order = jnp.stack([col_index, col_index ^ 2, col_index ^ 1, col_index ^ 3]).astype(jnp.int32)

    x_shard = tokens[0].T
    dy_shard = cotangent[0].T
    part_rows = w_qkv.shape[0]
    w_flat = w_qkv.reshape(part_rows, 3 * part)

    def own_rows(array):
        return lax.dynamic_slice_in_dim(array, col_index * part, part, 0)

    vectors = jnp.stack(
        [ln1_gain, ln1_bias, ln2_gain, ln2_bias, b_qv[0], b_qv[1], own_rows(b_out)], axis=1
    )
    x_sent = jnp.concatenate([x_shard, jnp.pad(vectors, ((0, 0), (0, 121)))], axis=1)

    slot_column = lax.broadcasted_iota(jnp.int32, (1, 3 * width), 1)
    slot_part, slot_index = slot_column // width, slot_column % width
    slot_source = jnp.where(slot_index < head_count * E, slot_index + column_shift, -1)
    own_row = lax.broadcasted_iota(jnp.int32, (3 * part, 1), 0)
    pick_own = ((own_row // part == slot_part) & (own_row % part == slot_source)).astype(bf16)
    next_row = lax.broadcasted_iota(jnp.int32, (3 * spare, 1), 0)
    pick_next = (
        (next_row // spare == slot_part) & (next_row % spare + part == slot_source)
    ).astype(bf16)
    next_to_here = [(i + 1, i) for i in range(col_count - 1)]
    here_to_next = [(i, i + 1) for i in range(col_count - 1)]

    def edge_of(array):
        return jnp.concatenate([array[:, p * part : p * part + spare] for p in range(3)], axis=1)

    if fast:
        left = ring(w_flat, "row", 1)
        right = ring(w_flat, "row", -1)
        x_pieces = gather_col(x_sent)
        x_before = lax.ppermute(x_shard, "seq", [(0, 1)])
        x_full, normed_one, stats_one, columns = first_norm(order, x_pieces, span)
        before_pieces = gather_col_after(after(x_before, x_pieces[1]), normed_one)
        near_edge = lax.ppermute(
            jnp.concatenate([edge_of(w_flat), edge_of(left), edge_of(right)]), "col", next_to_here
        )
        cut = part_rows // 32 * 16 + 16
        far_a = ring(after(left[:cut], normed_one), "row", 1)
        far_b = ring(after(right[cut:], normed_one), "row", -1)
        far_edge = lax.ppermute(
            jnp.concatenate([edge_of(far_a), edge_of(far_b)]), "col", next_to_here
        )
        w_order = ((row_index - jnp.arange(4, dtype=jnp.int32)) % 4).astype(jnp.int32)
        _, normed_before, _ = first_norm(order, before_pieces, span, columns)
        w_heads = head_weights(
            w_order,
            [w_flat, left, right, far_a, far_b, near_edge, after(far_edge, normed_before)],
            pick_own,
            pick_next,
        )
        where = jnp.stack([seq_index, head_first * E]).astype(jnp.int32)
        queries, kv_all = project(where, w_heads, columns, normed_one, normed_before)
        attn_one = attn_fwd(info, queries, kv_all, slots, 0)
        attn_pieces_one = gather_col(attn_one[0])
        attn_two = attn_fwd(info, after(queries, attn_one[3]), kv_all, slots, 1)
        attn_pieces_two = gather_col(attn_two[0])
        dy_pieces = gather_col(after(dy_shard, attn_two[3], attn_pieces_one[1]))

        some = part_rows // 64 * 16 + 16
        piece = after(
            lax.dynamic_slice_in_dim(w_out, col_index * (some - 16), some, 0), far_a, far_b
        )
        mine = jnp.concatenate([ring(piece, "row", 1), ring(piece, "row", 2), ring(piece, "row", -1)])
        mine = after(mine, attn_one[3])
        across = swap_x(mine)
        beside = swap_core(jnp.concatenate([mine, across]))
        starts = [row_index * part_rows]
        plan = [(0, 0, part_rows, 0)]
        for which, base, device in ((1, 0, 0), (2, 0, 1), (3, 0, 2), (3, 3 * some, 3)):
            for index, away in enumerate((1, 2, 3)):
                plan.append((which, base + index * some, some, len(starts)))
                starts.append((row_index - away) % 4 * part_rows + order[device] * (some - 16))
        w_out_all = assemble(
            jnp.stack(starts).astype(jnp.int32), [w_out, mine, across, beside], plan, full, E
        )

        some = part_rows // 32 * 16 + 16
        other = part_rows - some
        w_down_rows = w_down.T
        piece = jnp.concatenate(
            [
                lax.dynamic_slice_in_dim(w_up, seq_index * other, some, 0),
                lax.dynamic_slice_in_dim(w_down_rows, seq_index * other, some, 0),
            ]
        )
        piece = after(piece, far_a, far_b)
        up_left = ring(piece, "row", 1)
        up_right = ring(piece, "row", -1)
        near_mine = after(jnp.concatenate([up_left, up_right]), attn_one[3])
        near_theirs = swap_seq(near_mine)
        far_mine = jnp.concatenate(
            [ring(near_mine[:some], "row", 1), ring(near_mine[3 * some :], "row", -1)]
        )
        far_mine = after(far_mine, attn_two[3])
        far_theirs = swap_seq(far_mine)

        def weight(shard, base):
            starts = [row_index * part_rows]
            plan = [(0, 0, part_rows, 0)]
            for which, start, away, bit in (
                (1, base, 1, seq_index),
                (1, 2 * some + base, 3, seq_index),
                (2, base, 1, 1 - seq_index),
                (2, 2 * some + base, 3, 1 - seq_index),
                (3, base, 2, seq_index),
                (4, base, 2, 1 - seq_index),
            ):
                plan.append((which, start, some, len(starts)))
                starts.append((row_index - away) % 4 * part_rows + bit * other)
            return assemble(
                jnp.stack(starts).astype(jnp.int32),
                [shard, near_mine, near_theirs, far_mine, far_theirs],
                plan,
                full,
            )

        w_up_all = weight(w_up, 0)
        w_down_t = weight(w_down_rows, some)
    else:
        x_pieces = gather_col(x_sent)
        x_full, normed_one, stats_one, columns = first_norm(order, x_pieces, span)
        w_all = lax.all_gather(w_flat, "row", axis=0, tiled=True)
        edges = lax.ppermute(edge_of(w_all), "col", next_to_here)
        w_heads = (dot_nn(w_all, pick_own) + dot_nn(edges, pick_next)).astype(bf16)
        bias = lax.dynamic_slice_in_dim(columns, head_first * E, width, 0)
        projected = dot_tn(w_heads, normed_one)
        queries = (
            (projected[:width] + bias[:, 4:5]).astype(bf16) * E ** (-0.5)
        ).astype(bf16)
        keyvals = jnp.concatenate(
            [projected[width : 2 * width], projected[2 * width :] + bias[:, 5:6]]
        ).astype(bf16)
        kv_all = lax.all_gather(keyvals, "seq", axis=1, tiled=True)
        attn_one = attn_fwd(info, queries, kv_all, slots, 0)
        attn_two = attn_fwd(info, queries, kv_all, slots, 1)
        attn_pieces_one = gather_col(attn_one[0])
        attn_pieces_two = gather_col(attn_two[0])
        dy_pieces = gather_col(dy_shard)
        w_out_all = jnp.pad(lax.all_gather(w_out, "row", axis=0, tiled=True), ((0, E), (0, 0)))
        w_up_all = lax.all_gather(w_up, "row", axis=0, tiled=True)
        w_down_t = lax.all_gather(w_down.T, "row", axis=0, tiled=True)
    dy_full = assemble(
        (order * part).astype(jnp.int32), dy_pieces, [(n, 0, part, n) for n in range(4)], full
    )

    head_rows = (first_head(order) * E).astype(jnp.int32)
    normal_one = out_norm(head_rows, attn_pieces_one, w_out_all, x_full, columns, 0)
    normal_two = out_norm(head_rows, attn_pieces_two, w_out_all, x_full, columns, 1)

    def joined(index):
        return jnp.concatenate([normal_one[index], normal_two[index]], axis=1)

    after_attn, normed_two, stats_two, attn_all = (joined(i) for i in range(4))
    exact = jnp.concatenate([attn_one[1], attn_two[1]], axis=1)
    lse = jnp.concatenate([attn_one[2], attn_two[2]], axis=1)
    tops = jnp.max(jnp.maximum(attn_one[3], attn_two[3]), axis=1)

    slot_head = jnp.arange(slots, dtype=jnp.int32)
    head_ids = jnp.arange(H, dtype=jnp.int32)
    my_top = jnp.where(slot_head < head_count, tops[:slots], neg_fill)
    placed_top = jnp.max(
        jnp.where(head_ids[None] == (head_first + slot_head)[:, None], my_top[:, None], neg_fill),
        axis=0,
    )
    placed_top = jnp.pad(placed_top, (0, full - H))

    act, grad_pre, back_parts, bup_sums = feed(
        normed_two, dy_full, w_up_all, w_down_t, b_up.astype(f32)[:, None]
    )
    back_core, back_mine, back_got = scatter_col(back_parts, x_bit, core_bit)
    act_then = after(act, back_core)
    up_partial = dot_nt(normed_two, after(grad_pre, back_core)).astype(bf16)
    down_partial = dot_nt(dy_full, act_then).astype(bf16)

    branch_rows, row_sums = second_back(
        col_index[None].astype(jnp.int32),
        back_mine,
        back_got,
        after_attn,
        dy_full,
        stats_two,
        columns,
    )
    branch_pieces = gather_col(branch_rows)
    down = dot_nn(w_down_t, after(act, branch_rows)).astype(bf16).reshape(col_count, part, span)
    head_info = jnp.concatenate([jnp.stack([head_first * E, head_count * E]), order]).astype(jnp.int32)
    branch, grad_attn = attn_grad(head_info, branch_pieces, w_out_all, width)
    out_partial = dot_nt(attn_all, own_rows(branch)).astype(bf16)
    middle = jnp.concatenate([row_sums[:, :3].T, placed_top[None]])

    def join(one, two):
        return jnp.concatenate([one[:3] + two[:3], jnp.maximum(one[3:4], two[3:4]), one[4:] + two[4:]])

    middle = after(middle, grad_attn)
    middle = join(middle, swap_x(middle))
    middle = join(middle, swap_core(middle))

    if fast:
        feed_halves = seq_halves([up_partial, down_partial])
        feed_halves = (feed_halves[0], after(feed_halves[1], grad_attn))
        feed_far = row_sum_one(feed_halves)
        out_halves = seq_halves([out_partial])
        dq_one, dkv_one = attn_bwd(
            info, queries, kv_all, after(grad_attn, out_partial), exact, lse, None, slots, 0, False
        )
        dkv_there = lax.ppermute(dkv_one, "seq", [(1, 0)])
        feed_near = row_sum_two(feed_halves, (after(feed_far[0], dq_one), after(feed_far[1], dq_one)))
        dq, dkv_two = attn_bwd(
            info, after(queries, dq_one), kv_all, grad_attn, exact, lse, dq_one, slots, 1, True
        )
        dkv = jnp.where(
            seq_index == 0,
            (dkv_one.astype(f32) + after(dkv_there, dq).astype(f32)).astype(bf16),
            dkv_two,
        )
        heads_grad = jnp.concatenate([dq, dkv])
        one_parts = dot_nn(w_heads, heads_grad).astype(bf16).reshape(col_count, part, span)
        one_core, one_mine, one_got = scatter_col(one_parts, x_bit, core_bit)
        partial = dot_nt(normed_one, after(heads_grad, one_parts)).astype(bf16)
        halves = seq_halves([partial])
        feed_sums = row_sum_end(
            feed_halves, (after(feed_near[0], one_core, partial), after(feed_near[1], one_core, partial))
        )
        grad_w_up, grad_w_down = feed_sums[0], feed_sums[1].T
        _, down_mine, down_got = scatter_col(after(down, one_mine), x_bit, core_bit)
        last_halves = (
            jnp.concatenate([halves[0], out_halves[0]], axis=3),
            jnp.concatenate([after(halves[1], one_got), after(out_halves[1], one_core)], axis=3),
        )
        last_far = row_sum_one(last_halves)
        last_near = row_sum_two(last_halves, last_far)
        last = row_sum_end(last_halves, last_near)[0]
        summed, out_columns = last[:, : 3 * width], last[:, 3 * width :].astype(bf16)
    else:
        dq, pieces = None, []
        for segment in range(seq_count):
            dq, dkv_one = attn_bwd(
                info, queries, kv_all, grad_attn, exact, lse, dq, slots, segment, segment == seq_count - 1
            )
            pieces.append(dkv_one)
        dkv = lax.psum_scatter(
            jnp.concatenate(pieces, axis=1), "seq", scatter_dimension=1, tiled=True
        )
        grad_w_up = scatter_plain(up_partial)
        grad_w_down = scatter_plain(down_partial).T
        out_columns = scatter_plain(out_partial).astype(bf16)
        heads_grad = jnp.concatenate([dq, dkv])
        one_parts = dot_nn(w_heads, heads_grad).astype(bf16).reshape(col_count, part, span)
        _, one_mine, one_got = scatter_col(one_parts, x_bit, core_bit)
        summed = scatter_plain(dot_nt(normed_one, heads_grad).astype(bf16))
        _, down_mine, down_got = scatter_col(down, x_bit, core_bit)
    summed = summed.reshape(-1, 3, width)
    grad_w_out = by_index(gather_col(out_columns)).astype(f32)
    block_out = (
        own_rows(after_attn) + down_mine + down_got.astype(f32) + b_down.astype(f32)[:, None]
    ).astype(bf16)

    def to_owner(array):
        wide_array = jnp.pad(array, ((0, 0), (0, 0), (spare, 0)))
        shifted = wide_array[:, :, spare : spare + width]
        for shift in range(1, col_count):
            amount = 1 + fewer * shift
            offset = amount * E - shift * part
            shifted = jnp.where(
                col_index == shift, wide_array[:, :, spare - offset : spare - offset + width], shifted
            )
        sent = lax.ppermute(shifted[:, :, part:].reshape(-1, 3 * spare), "col", here_to_next)
        return shifted[:, :, :part] + jnp.pad(
            sent.reshape(-1, 3, spare), ((0, 0), (0, 0), (0, part - spare))
        )

    grad_w_qkv = to_owner(summed)
    head_sums = jnp.sum(heads_grad.astype(f32), axis=1)
    head_sums = jnp.stack([head_sums[:width], head_sums[2 * width :]])
    head_sums = lax.dynamic_update_slice_in_dim(
        jnp.zeros((2, full + E), f32), head_sums, head_first * E, 1
    )[:, :full]

    back_one = one_mine + one_got.astype(f32)
    unit_one = (x_shard.astype(f32) - stats_one[0:1]) * stats_one[1:2]
    unit_grad = back_one * ln1_gain.astype(f32)[:, None]
    sums = jnp.stack([jnp.sum(unit_grad, axis=0), jnp.sum(unit_grad * unit_one, axis=0)])
    sums = jnp.concatenate([jnp.pad(sums, ((0, 0), (0, full - span))) if full > span else sums, head_sums])
    sums = sums + swap_x(sums)
    sums = sums + swap_core(sums)
    bias_grads = lax.dynamic_slice_in_dim(sums[2:], col_index * part, part, 1)
    sums = sums[:2, :span] / full
    grad_tokens = own_rows(branch).astype(f32) + stats_one[1:2] * (
        unit_grad - sums[0:1] - unit_one * sums[1:2]
    )

    small = jnp.concatenate(
        [
            jnp.sum(back_one * unit_one, axis=1),
            jnp.sum(back_one, axis=1),
            jnp.sum(dy_shard.astype(f32), axis=1),
            jnp.zeros((part,), f32),
        ]
    )
    middle = jnp.concatenate(
        [
            middle,
            bup_sums[:, 0][None],
            small[None],
            jnp.pad(bias_grads.reshape(1, -1), ((0, 0), (0, full - 2 * part))),
        ]
    )
    for axis in ("seq", "row"):
        middle = combine_axis(middle, axis, join)
    row_vectors, head_max, grad_b_up = middle[:3], middle[3, :H], middle[4]
    own_vectors = lax.dynamic_slice_in_dim(row_vectors, col_index * part, part, 1)

    def piece(start, length):
        return middle[5, start : start + length]

    root_clip = jnp.sqrt(clip_limit / jnp.maximum(head_max, clip_limit))
    column_head = (col_index * part + jnp.arange(part, dtype=jnp.int32)) // E
    one_hot = (column_head[:, None] == head_ids[None, :]).astype(f32)
    column_root = jnp.sum(one_hot * root_clip[None, :], axis=1)
    scale_three = jnp.stack([column_root, column_root, jnp.ones_like(column_root)])
    clipped_qkv = w_qkv.astype(f32) * scale_three[None]
    return (
        block_out.T[None],
        grad_tokens.T[None],
        piece(0, part),
        piece(part, part),
        grad_w_qkv,
        middle[6, : 2 * part].reshape(2, part),
        grad_w_out,
        row_vectors[2],
        own_vectors[0],
        own_vectors[1],
        grad_w_up,
        grad_b_up,
        grad_w_down,
        piece(2 * part, part),
        clipped_qkv,
        head_max,
    )


def solution(mesh):
    placed = (
        P("row", "seq", "col"),
        P("row"),
        P("col"),
        P("col"),
        P("row", None, "col"),
        P(None, "col"),
        P("row", None),
        P(),
        P("col"),
        P("col"),
        P("row", "col"),
        P("col"),
        P("col", "row"),
        P("col"),
        P("row", "seq", "col"),
    )
    return jax.shard_map(
        on_device,
        mesh=mesh,
        in_specs=placed,
        out_specs=(
            P("row", "seq", "col"),
            P("row", "seq", "col"),
            P("col"),
            P("col"),
            P(("seq", "row"), None, "col"),
            P(None, "col"),
            P(("seq", "row"), None),
            P(),
            P("col"),
            P("col"),
            P(("seq", "row"), "col"),
            P("col"),
            P("col", ("seq", "row")),
            P("col"),
            P("row", None, "col"),
            P(),
        ),
        check_vma=False,
    )
```

```python
import functools

import jax
import jax.numpy as jnp
from jax import lax
from jax.experimental import pallas as pl
from jax.experimental.pallas import tpu as pltpu
from jax.sharding import PartitionSpec as P


H = 17
E = 64

norm_eps = 1e-05
neg_fill = -1e30
clip_limit = 8.0

SCALE = 0.02

f32 = jnp.float32
bf16 = jnp.bfloat16

VMEM = pl.BlockSpec(memory_space=pltpu.VMEM)
SMEM = pl.BlockSpec(memory_space=pltpu.SMEM)
ANY = pl.BlockSpec(memory_space=pl.ANY)


def dot_nn(left, right):
    return lax.dot_general(left, right, (((1,), (0,)), ((), ())), preferred_element_type=f32)


def dot_nt(left, right):
    return lax.dot_general(left, right, (((1,), (1,)), ((), ())), preferred_element_type=f32)


def dot_tn(left, right):
    return lax.dot_general(left, right, (((0,), (0,)), ((), ())), preferred_element_type=f32)


def params(mib=16):
    return pltpu.CompilerParams(vmem_limit_bytes=mib * 2**20)


def cost(flops, moved, exps=0):
    return pl.CostEstimate(
        flops=int(flops * SCALE), bytes_accessed=int(moved * SCALE), transcendentals=int(exps * SCALE)
    )


def waiting(body, inputs, count):
    def wrapped(*refs):
        return body(*refs[:inputs], *refs[inputs + count :])

    return wrapped


def shape(dims, kind):
    return jax.ShapeDtypeStruct(dims, kind)


def rows_at(start, length):
    return pl.ds(pl.multiple_of(start, 16), length)


def assemble_body(plan, fill, turned, starts, *refs):
    pieces, out_ref = (refs[:-2], refs[-2]) if turned else (refs[:-1], refs[-1])
    for piece, source, length, where in plan:
        out_ref[rows_at(starts[where], length), :] = pieces[piece][source : source + length, :]
    if turned:
        rows = out_ref.shape[0]
        refs[-1][:rows, :] = out_ref[...].T
        refs[-1][rows:, :] = jnp.zeros((fill, rows), bf16)


def whole(array):
    return VMEM


def assemble(starts, pieces, plan, rows, fill=0, turned=False):
    result = shape((rows, pieces[0].shape[1]), bf16)
    results = [result, shape((rows + fill, rows), bf16)] if turned else result
    return pl.pallas_call(
        functools.partial(assemble_body, tuple(plan), fill, turned),
        grid_spec=pltpu.PrefetchScalarGridSpec(
            num_scalar_prefetch=1,
            grid=(1,),
            in_specs=[whole(piece) for piece in pieces],
            out_specs=[whole(each) for each in results] if turned else whole(result),
        ),
        out_shape=results,
        compiler_params=params(),
        cost_estimate=cost(0, rows * result.shape[1] * 4),
        name="assemble",
    )(starts, *pieces)


def first_norm_body(own, order, p0, p1, p2, p3, *refs):
    if own:
        x_ref, n_ref, stat_ref, vec_ref, dy_ref = refs
    else:
        vec_ref, x_ref, n_ref, stat_ref = refs
    part = p0.shape[0]
    full, count = x_ref.shape
    if own:
        vec_ref[full:, :] = jnp.zeros((vec_ref.shape[0] - full, vec_ref.shape[1]), f32)
    for n, piece in enumerate((p0, p1, p2, p3)):
        where = rows_at(order[n] * part, part)
        x_ref[where, :] = piece[:, :count]
        if own:
            vec_ref[where, :] = piece[:, count : count + 128].astype(f32)
            dy_ref[where, :] = piece[:, count + 128 :]
    for start in range(0, count, 256):
        cols = slice(start, start + 256)
        x = x_ref[:, cols].astype(f32)
        mean = jnp.sum(x, axis=0, keepdims=True) * (1.0 / full)
        center = x - mean
        inv = lax.rsqrt(jnp.sum(center * center, axis=0, keepdims=True) * (1.0 / full) + norm_eps)
        n_ref[:, cols] = (center * inv * vec_ref[:full, 0:1] + vec_ref[:full, 1:2]).astype(bf16)
        stat_ref[0:1, cols] = mean
        stat_ref[1:2, cols] = inv


def first_norm(order, pieces, count, vectors=None):
    own = vectors is None
    full = pieces[0].shape[0] * 4
    results = [shape((full, count), bf16), shape((full, count), bf16), shape((8, count), f32)]
    operands = list(pieces)
    if own:
        results += [shape((full + E, 128), f32), shape((full, count), bf16)]
    else:
        operands.append(vectors)
    return pl.pallas_call(
        functools.partial(first_norm_body, own),
        grid_spec=pltpu.PrefetchScalarGridSpec(
            num_scalar_prefetch=1,
            grid=(1,),
            in_specs=[whole(array) for array in operands],
            out_specs=[whole(result) for result in results],
        ),
        out_shape=results,
        compiler_params=params(),
        cost_estimate=cost(20 * full * count, full * count * 8),
        name="first_norm",
    )(order, *operands)


def near_rows_body(order, own, left, right, pick_own, base_ref, edge_ref, out_ref):
    size = own.shape[0]
    wide = pick_own.shape[0]
    spare = edge_ref.shape[1]
    for n, piece in ((0, own), (1, left), (3, right)):
        where = rows_at(order[n] * size, size)
        base_ref[where, :] = dot_nn(piece[:, :wide], pick_own[...]).astype(bf16)
        out_ref[where, :] = piece[:, wide:]
        edge_rows(piece, edge_ref, where, wide // 3)


def edge_rows(piece, edge_ref, where, part):
    spare = 5 * E - part
    for p in range(3):
        edge_ref[where, p * spare : (p + 1) * spare] = piece[:, p * part : p * part + spare]


def far_rows_body(order, base, edge, out, far_a, far_b, pick_own, base_ref, edge_ref, turned_ref, out_s):
    size, cut = base.shape[0] // 4, far_a.shape[0]
    wide = pick_own.shape[0]
    base_ref[...] = base[...]
    edge_ref[...] = edge[...]
    out_s[...] = out[...]
    for piece, extra in ((far_a, 0), (far_b, cut)):
        where = rows_at(order[2] * size + extra, piece.shape[0])
        base_ref[where, :] = dot_nn(piece[:, :wide], pick_own[...]).astype(bf16)
        out_s[where, :] = piece[:, wide:]
        edge_rows(piece, edge_ref, where, wide // 3)
    turned_ref[...] = out_s[...].T


def near_rows(order, pieces, pick_own):
    size = pieces[0].shape[0]
    results = [
        shape((4 * size, pick_own.shape[1]), bf16),
        shape((4 * size, 256), bf16),
        shape((4 * size, size), bf16),
    ]
    return pl.pallas_call(
        near_rows_body,
        grid_spec=pltpu.PrefetchScalarGridSpec(
            num_scalar_prefetch=1, grid=(1,), in_specs=[VMEM] * 4, out_specs=[VMEM] * 3
        ),
        out_shape=results,
        compiler_params=params(),
        cost_estimate=cost(2 * 816 * 816 * 960, 6 * 10**6),
        name="near_rows",
    )(order, *pieces, pick_own)


def far_rows(order, near, far, pick_own, wait):
    size = near[0].shape[0] // 4
    results = [
        shape(near[0].shape, bf16),
        shape(near[1].shape, bf16),
        shape((size, 4 * size), bf16),
    ]
    return pl.pallas_call(
        waiting(far_rows_body, 7, 1),
        grid_spec=pltpu.PrefetchScalarGridSpec(
            num_scalar_prefetch=1,
            grid=(1,),
            in_specs=[VMEM] * 6 + [ANY],
            out_specs=[VMEM] * 3,
            scratch_shapes=[pltpu.VMEM((4 * size, size), bf16)],
        ),
        out_shape=results,
        compiler_params=params(),
        cost_estimate=cost(2 * 272 * 816 * 960, 6 * 10**6),
        name="far_rows",
    )(order, *near, *far, pick_own, wait)


def project_body(width, info, base_ref, edge_ref, pick_ref, bias_ref, own_ref, before_ref, q_ref, kv_ref, w_ref, w_s):
    step = pl.program_id(0)
    half = pl.num_programs(0) // 2
    mine = (step // half) == info[0]

    @pl.when(step == 0)
    def _():
        edges = edge_ref[:, : pick_ref.shape[0]]
        w_ref[...] = base_ref[...] + dot_nn(edges, pick_ref[...]).astype(bf16)
        w_s[...] = w_ref[...].T

    def keyvals(n_ref):
        kv_ref[:width, :] = dot_nn(w_s[width : 2 * width, :], n_ref[...]).astype(bf16)
        kv_ref[width:, :] = (
            dot_nn(w_s[2 * width :, :], n_ref[...]) + bias_ref[rows_at(info[1], width), 5:6]
        ).astype(bf16)

    @pl.when(mine)
    def _():
        out = dot_nn(w_s[:width, :], own_ref[...]) + bias_ref[rows_at(info[1], width), 4:5]
        q_ref[...] = (out.astype(bf16).astype(f32) * E ** (-0.5)).astype(bf16)
        keyvals(own_ref)

    @pl.when(jnp.logical_not(mine))
    def _():
        keyvals(before_ref)


def project(info, base, edges, pick_next, bias, own, before, block=512):
    full, count = own.shape
    wide = base.shape[1]
    width = wide // 3
    steps = count // block
    return pl.pallas_call(
        functools.partial(project_body, width),
        grid_spec=pltpu.PrefetchScalarGridSpec(
            num_scalar_prefetch=1,
            grid=(2 * steps,),
            in_specs=[
                VMEM,
                VMEM,
                VMEM,
                VMEM,
                pl.BlockSpec((full, block), lambda i, s: (0, jnp.clip(i - s[0] * steps, 0, steps - 1))),
                pl.BlockSpec(
                    (full, block), lambda i, s: (0, jnp.clip(i - (1 - s[0]) * steps, 0, steps - 1))
                ),
            ],
            out_specs=[
                pl.BlockSpec((width, block), lambda i, s: (0, jnp.clip(i - s[0] * steps, 0, steps - 1))),
                pl.BlockSpec((2 * width, block), lambda i, s: (0, i)),
                VMEM,
            ],
            scratch_shapes=[pltpu.VMEM((wide, full), bf16)],
        ),
        out_shape=[
            shape((width, count), bf16),
            shape((2 * width, 2 * count), bf16),
            shape((full, wide), bf16),
        ],
        compiler_params=params(24),
        cost_estimate=cost(2 * full * count * 5 * width, 10 * 10**6),
        name="project",
    )(info, base, edges, pick_next, bias, own, before)


def block_limits(info, block, rows):
    prefix_len = info[0]
    query_lo = info[1] + block * rows
    query_hi = query_lo + rows - 1
    in_prefix = query_lo < prefix_len
    limit_max = jnp.where(in_prefix, jnp.maximum(prefix_len - 1, query_hi), query_hi)
    limit_min = jnp.where(in_prefix, prefix_len - 1, query_lo)
    positions = query_lo + lax.broadcasted_iota(jnp.int32, (1, rows), 1)
    return limit_max, limit_min, jnp.where(positions < prefix_len, prefix_len - 1, positions)


def attn_fwd_body(
    slots, keys, first, info, q_ref, kv_ref, attn_ref, exact_ref, lse_ref, top_ref, k_s, m_s, l_s, acc_s
):
    width, rows = q_ref.shape
    limit_max, limit_min, limit = block_limits(info, first, rows)
    n_need = limit_max // keys + 1
    n_full = (limit_min + 1) // keys
    for h in range(slots):
        k_s[h] = kv_ref[h * E : h * E + E, :].T
    m_s[...] = jnp.full_like(m_s, neg_fill)
    l_s[...] = jnp.zeros_like(l_s)
    acc_s[...] = jnp.zeros_like(acc_s)

    def step(index, masked):
        start = pl.multiple_of(index * keys, keys)
        if masked:
            seen = (start + lax.broadcasted_iota(jnp.int32, (keys, rows), 0)) <= limit
        for h in range(slots):
            here, row = slice(h * E, h * E + E), slice(h, h + 1)
            scores = dot_nn(k_s[h, pl.ds(start, keys), :], q_ref[here, :])
            if masked:
                scores = jnp.where(seen, scores, neg_fill)
            old_max = m_s[row, :]
            new_max = jnp.maximum(old_max, jnp.max(scores, axis=0, keepdims=True))
            weights = jnp.exp(scores - new_max)
            shrink = jnp.exp(old_max - new_max)
            l_s[row, :] = l_s[row, :] * shrink + jnp.sum(weights, axis=0, keepdims=True)
            values = kv_ref[width + h * E : width + h * E + E, pl.ds(start, keys)]
            acc_s[here, :] = acc_s[here, :] * shrink + dot_nn(values, weights.astype(bf16))
            m_s[row, :] = new_max

    @pl.loop(0, n_full)
    def _(index):
        step(index, False)

    @pl.loop(n_full, n_need)
    def _(index):
        step(index, True)

    for h in range(slots):
        here, row = slice(h * E, h * E + E), slice(h, h + 1)
        outcome = acc_s[here, :] / l_s[row, :]
        exact_ref[here, :] = outcome
        attn_ref[here, :] = outcome.astype(bf16)
    row_max = m_s[...]
    lse_ref[...] = row_max + jnp.log(l_s[...])
    top = row_max[:, :128]
    for start in range(128, rows, 128):
        top = jnp.maximum(top, row_max[:, start : start + 128])
    top_ref[...] = top


def attn_fwd(info, queries, kv_all, slots, first, rows=512, keys=512):
    width = queries.shape[0]
    total = kv_all.shape[1]
    return pl.pallas_call(
        functools.partial(attn_fwd_body, slots, keys, first),
        grid_spec=pltpu.PrefetchScalarGridSpec(
            num_scalar_prefetch=1,
            grid=(1,),
            in_specs=[
                pl.BlockSpec((width, rows), lambda i, _: (0, first)),
                pl.BlockSpec((2 * width, total), lambda i, _: (0, 0)),
            ],
            out_specs=[
                pl.BlockSpec((width, rows), lambda i, _: (0, 0)),
                pl.BlockSpec((width, rows), lambda i, _: (0, 0)),
                pl.BlockSpec((8, rows), lambda i, _: (0, 0)),
                pl.BlockSpec((8, 128), lambda i, _: (0, 0)),
            ],
            scratch_shapes=[
                pltpu.VMEM((slots, total, E), bf16),
                pltpu.VMEM((8, rows), f32),
                pltpu.VMEM((8, rows), f32),
                pltpu.VMEM((width, rows), f32),
            ],
        ),
        out_shape=[
            shape((width, rows), bf16),
            shape((width, rows), f32),
            shape((8, rows), f32),
            shape((8, 128), f32),
        ],
        compiler_params=params(40),
        cost_estimate=cost(8 * 10**9, 6 * 10**6, 4 * 10**6),
        name="attn_fwd",
    )(info, queries, kv_all)


def attn_bwd_body(slots, keys, key_first, more, last, info, *refs):
    if more:
        q_ref, kv_ref, do_ref, o_ref, lse_ref, dq_in, dq_ref, dkv_ref, k_s, v_s, acc_s, dkv_s = refs
    else:
        q_ref, kv_ref, do_ref, o_ref, lse_ref, dq_ref, dkv_ref, k_s, v_s, acc_s, dkv_s = refs
    block = pl.program_id(0)
    width, rows = q_ref.shape
    n_blocks = kv_ref.shape[1] // keys
    limit_max, limit_min, limit = block_limits(info, block, rows)
    n_need = jnp.clip((limit_max - key_first) // keys + 1, 0, n_blocks)
    n_full = jnp.clip((limit_min - key_first + 1) // keys, 0, n_blocks)
    limit = limit - key_first

    @pl.when(block == 0)
    def _():
        dkv_s[...] = jnp.zeros_like(dkv_s)
        for h in range(slots):
            k_s[h] = kv_ref[h * E : h * E + E, :].T
            v_s[h] = kv_ref[width + h * E : width + h * E + E, :].T

    if more:
        acc_s[...] = dq_in[...]
    else:
        acc_s[...] = jnp.zeros_like(acc_s)
    dots = [
        jnp.sum(
            do_ref[h * E : h * E + E, :].astype(f32) * o_ref[h * E : h * E + E, :],
            axis=0,
            keepdims=True,
        )
        for h in range(slots)
    ]

    def step(index, masked):
        start = pl.multiple_of(index * keys, keys)
        where = pl.ds(start, keys)
        if masked:
            seen = (start + lax.broadcasted_iota(jnp.int32, (keys, rows), 0)) <= limit
        for h in range(slots):
            here = slice(h * E, h * E + E)
            there = slice(width + h * E, width + h * E + E)
            q_head, do_head = q_ref[here, :], do_ref[here, :]
            probs = jnp.exp(dot_nn(k_s[h, where, :], q_head) - lse_ref[h : h + 1, :])
            if masked:
                probs = jnp.where(seen, probs, 0.0)
            grad_probs = dot_nn(v_s[h, where, :], do_head)
            grad_scores = (probs * (grad_probs - dots[h])).astype(bf16)
            dkv_s[there, where] += dot_nt(do_head, probs.astype(bf16))
            dkv_s[here, where] += dot_nt(q_head, grad_scores)
            acc_s[here, :] += dot_nn(kv_ref[here, where], grad_scores)

    @pl.loop(0, n_full)
    def _(index):
        step(index, False)

    @pl.loop(n_full, n_need)
    def _(index):
        step(index, True)

    if last:
        dq_ref[...] = (acc_s[...] * E ** (-0.5)).astype(bf16)
    else:
        dq_ref[...] = acc_s[...]

    @pl.when(block == pl.num_programs(0) - 1)
    def _():
        dkv_ref[...] = dkv_s[...].astype(bf16)


def attn_bwd(
    info, queries, kv_all, grad_attn, exact, lse, dq_in, slots, segment, last, rows=512, keys=512
):
    width, count = queries.shape
    more = dq_in is not None
    block = pl.BlockSpec((width, rows), lambda i, _: (0, i))
    return pl.pallas_call(
        functools.partial(attn_bwd_body, slots, keys, segment * count, more, last),
        grid_spec=pltpu.PrefetchScalarGridSpec(
            num_scalar_prefetch=1,
            grid=(count // rows,),
            in_specs=[
                block,
                pl.BlockSpec((2 * width, count), lambda i, _: (0, segment)),
                block,
                block,
                pl.BlockSpec((8, rows), lambda i, _: (0, i)),
            ]
            + [block] * more,
            out_specs=[block, pl.BlockSpec((2 * width, count), lambda i, _: (0, 0))],
            scratch_shapes=[
                pltpu.VMEM((slots, count, E), bf16),
                pltpu.VMEM((slots, count, E), bf16),
                pltpu.VMEM((width, rows), f32),
                pltpu.VMEM((2 * width, count), f32),
            ],
        ),
        out_shape=[
            shape((width, count), bf16 if last else f32),
            shape((2 * width, count), bf16),
        ],
        compiler_params=params(40),
        cost_estimate=cost(16 * 10**9, 6 * 10**6, 4 * 10**6),
        name="attn_bwd",
    )(info, queries, kv_all, grad_attn, exact, lse, *([dq_in] if more else []))


def out_norm_body(starts, p0, p1, p2, p3, w_ref, x_ref, vec_ref, after_ref, n_ref, stat_ref, attn_ref):
    fewer = (attn_ref.shape[0] // E) // 4 * E
    for n, piece in enumerate((p0, p1, p2, p3)):
        attn_ref[rows_at(starts[n], fewer), :] = piece[:fewer, :]

        @pl.when(starts[n] == 0)
        def _():
            attn_ref[fewer : piece.shape[0], :] = piece[fewer:, :]

    full, count = x_ref.shape
    for start in range(0, count, 256):
        cols = slice(start, start + 256)
        after = x_ref[:, cols].astype(f32) + (
            dot_nn(w_ref[...], attn_ref[:, cols]) + vec_ref[:full, 6:7]
        )
        mean = jnp.sum(after, axis=0, keepdims=True) * (1.0 / full)
        center = after - mean
        inv = lax.rsqrt(jnp.sum(center * center, axis=0, keepdims=True) * (1.0 / full) + norm_eps)
        after_ref[:, cols] = after
        n_ref[:, cols] = (center * inv * vec_ref[:full, 2:3] + vec_ref[:full, 3:4]).astype(bf16)
        stat_ref[0:1, cols] = mean
        stat_ref[1:2, cols] = inv


def out_norm(starts, pieces, w_out_t, x_full, vectors, first):
    full = x_full.shape[0]
    rows, count = pieces[0].shape
    grid_spec = pltpu.PrefetchScalarGridSpec(
        num_scalar_prefetch=1,
        grid=(1,),
        in_specs=[whole(piece) for piece in pieces]
        + [
            pl.BlockSpec(w_out_t.shape, lambda i, _: (0, 0)),
            pl.BlockSpec((full, count), lambda i, _: (0, first)),
            pl.BlockSpec(vectors.shape, lambda i, _: (0, 0)),
        ],
        out_specs=[
            pl.BlockSpec((full, count), lambda i, _: (0, 0)),
            pl.BlockSpec((full, count), lambda i, _: (0, 0)),
            pl.BlockSpec((8, count), lambda i, _: (0, 0)),
            pl.BlockSpec((full, count), lambda i, _: (0, 0)),
        ],
    )
    return pl.pallas_call(
        out_norm_body,
        grid_spec=grid_spec,
        out_shape=[
            shape((full, count), f32),
            shape((full, count), bf16),
            shape((8, count), f32),
            shape((full, count), bf16),
        ],
        compiler_params=params(24),
        cost_estimate=cost(2 * full * full * count, 10**7),
        name="out_norm",
    )(starts, *pieces, w_out_t, x_full, vectors)


def erf_parts(v):
    return 0.5 * (1.0 + lax.erf(v * (0.5**0.5))), jnp.exp(-0.5 * v * v)


def feed_body(
    info, n_ref, dy_ref, up_ref, down_t_ref, b_ref, act_ref, grad_ref, theirs_ref, mine_ref, bias_ref, up_s, down_s
):
    step = pl.program_id(0)

    @pl.when(step == 0)
    def _():
        up_s[...] = up_ref[...].T
        down_s[...] = down_t_ref[...].T
        bias_ref[...] = jnp.zeros_like(bias_ref)

    pre = dot_nn(up_s[...], n_ref[...]) + b_ref[:, 0:1]
    grad_act = dot_nn(down_s[...], dy_ref[...])
    cdf, bell = erf_parts(pre)
    act_ref[...] = (pre * cdf).astype(bf16)
    grad = (grad_act * (cdf + pre * bell * 0.3989422804014327)).astype(bf16)
    grad_ref[...] = grad
    bias_ref[...] += dot_nn(grad, jnp.ones((grad.shape[1], 128), bf16))
    part = dot_nn(up_ref[...], grad).astype(bf16)

    @pl.when(step < 2)
    def _():
        theirs_ref[0] = part

    @pl.when(step >= 2)
    def _():
        mine_ref[0] = part


def turn(step, info):
    return jnp.where(step < 2, 2 * step + 1 - info[0], 2 * (step - 2) + info[0])


def feed(core, normed, dy, w_up, w_down_t, bias):
    full, count = normed.shape
    hidden = w_up.shape[1]
    block = count // 4
    cols = pl.BlockSpec((full, block), lambda i, c: (0, turn(i, c)))
    hid = pl.BlockSpec((hidden, block), lambda i, c: (0, turn(i, c)))
    return pl.pallas_call(
        feed_body,
        grid_spec=pltpu.PrefetchScalarGridSpec(
            num_scalar_prefetch=1,
            grid=(4,),
            in_specs=[
                cols,
                cols,
                pl.BlockSpec((full, hidden), lambda i, c: (0, 0)),
                pl.BlockSpec((full, hidden), lambda i, c: (0, 0)),
                pl.BlockSpec((hidden, 1), lambda i, c: (0, 0)),
            ],
            out_specs=[
                hid,
                hid,
                pl.BlockSpec((1, full, block), lambda i, c: (jnp.minimum(i, 1), 0, 0)),
                pl.BlockSpec((1, full, block), lambda i, c: (jnp.maximum(i - 2, 0), 0, 0)),
                pl.BlockSpec((hidden, 128), lambda i, c: (0, 0)),
            ],
            scratch_shapes=[pltpu.VMEM((hidden, full), bf16), pltpu.VMEM((hidden, full), bf16)],
        ),
        out_shape=[
            shape((hidden, count), bf16),
            shape((hidden, count), bf16),
            shape((2, full, block), bf16),
            shape((2, full, block), bf16),
            shape((hidden, 128), f32),
        ],
        compiler_params=params(40),
        cost_estimate=cost(6 * full * hidden * count, 2 * 10**7, 2 * hidden * count),
        name="feed",
    )(core, normed, dy, w_up, w_down_t, bias)


def second_back_body(index, mine_ref, got_ref, across_ref, after_ref, dy_ref, stat_ref, vec_ref, out_ref, sums_ref):
    back = mine_ref[0].astype(f32) + got_ref[0].astype(f32) + across_ref[...].astype(f32)
    full = back.shape[0]
    mean, inv = stat_ref[0:1, :], stat_ref[1:2, :]
    unit = (after_ref[...] - mean) * inv
    grad = back * vec_ref[:full, 2:3]
    first = jnp.sum(grad, axis=0, keepdims=True) * (1.0 / full)
    second = jnp.sum(grad * unit, axis=0, keepdims=True) * (1.0 / full)
    total = dy_ref[...].astype(f32) + inv * (grad - first - unit * second)
    low = total.astype(bf16)
    out_ref[...] = low
    sums_ref[:, 0:1] = jnp.sum(back * unit, axis=1, keepdims=True)
    sums_ref[:, 1:2] = jnp.sum(back, axis=1, keepdims=True)
    sums_ref[:, 2:3] = jnp.sum(low.astype(f32), axis=1, keepdims=True)


def second_back(index, mine, got, across, after, dy, stats, vectors):
    full, count = across.shape
    fixed = pl.BlockSpec((full, count), lambda i, c: (0, 0))
    moved = pl.BlockSpec((full, count), lambda i, c: (0, c[0]))
    part = pl.BlockSpec((1, full, count), lambda i, c: (c[1], 0, 0))
    return pl.pallas_call(
        second_back_body,
        grid_spec=pltpu.PrefetchScalarGridSpec(
            num_scalar_prefetch=1,
            grid=(1,),
            in_specs=[
                part,
                part,
                fixed,
                moved,
                moved,
                pl.BlockSpec((8, count), lambda i, c: (0, c[0])),
                pl.BlockSpec(vectors.shape, lambda i, c: (0, 0)),
            ],
            out_specs=[fixed, pl.BlockSpec((full, 8), lambda i, c: (0, 0))],
        ),
        out_shape=[shape((full, count), bf16), shape((full, 8), f32)],
        compiler_params=params(16),
        cost_estimate=cost(20 * full * count, 5 * 10**6),
        name="second_back",
    )(index, mine, got, across, after, dy, stats, vectors)


def attn_grad_body(info, p0, p1, p2, p3, w_ref, branch_ref, out_ref):
    count = p0.shape[1]
    width = out_ref.shape[0]
    weights = w_ref[rows_at(info[0], width), :]
    real = lax.broadcasted_iota(jnp.int32, (width, 1), 0) < info[1]
    for n, piece in enumerate((p0, p1, p2, p3)):
        cols = pl.ds(pl.multiple_of(info[2 + n] * count, 128), count)
        branch_ref[:, cols] = piece[...]
        out_ref[:, cols] = jnp.where(real, dot_nn(weights, piece[...]), 0.0).astype(bf16)


def attn_grad(info, pieces, w_out, width):
    full, quarter = pieces[0].shape
    results = [shape((full, 4 * quarter), bf16), shape((width, 4 * quarter), bf16)]
    return pl.pallas_call(
        attn_grad_body,
        grid_spec=pltpu.PrefetchScalarGridSpec(
            num_scalar_prefetch=1,
            grid=(1,),
            in_specs=[whole(array) for array in (*pieces, w_out)],
            out_specs=[whole(result) for result in results],
        ),
        out_shape=results,
        compiler_params=params(),
        cost_estimate=cost(8 * full * quarter * width, 10**7),
        name="attn_grad",
    )(info, *pieces, w_out)


def one_back_body(info, w_ref, dq_ref, one_ref, there_ref, two_ref, theirs_ref, mine_ref, grad_ref):
    step = pl.program_id(0)
    width = dq_ref.shape[0]

    @pl.when(step == 0)
    def _():
        grad_ref[:width, :] = dq_ref[...]

    @pl.when((step == 0) & (info[1] == 0))
    def _():
        grad_ref[width:, :] = (one_ref[...].astype(f32) + there_ref[...].astype(f32)).astype(bf16)

    @pl.when((step == 0) & (info[1] != 0))
    def _():
        grad_ref[width:, :] = two_ref[...]

    part = dot_nn(w_ref[0], grad_ref[...]).astype(bf16)

    @pl.when(step < 2)
    def _():
        theirs_ref[0] = part

    @pl.when(step >= 2)
    def _():
        mine_ref[0] = part


def one_back(info, w_heads, dq, dkv_one, dkv_there, dkv_two, wait):
    full, wide = w_heads.shape
    count = dq.shape[1]
    part = full // 4
    parts = shape((2, part, count), bf16)
    return pl.pallas_call(
        waiting(one_back_body, 6, 1),
        grid_spec=pltpu.PrefetchScalarGridSpec(
            num_scalar_prefetch=1,
            grid=(4,),
            in_specs=[pl.BlockSpec((1, part, wide), lambda i, c: (turn(i, c), 0, 0))]
            + [whole(array) for array in (dq, dkv_one, dkv_there, dkv_two)]
            + [ANY],
            out_specs=[
                pl.BlockSpec((1, part, count), lambda i, c: (jnp.minimum(i, 1), 0, 0)),
                pl.BlockSpec((1, part, count), lambda i, c: (jnp.maximum(i - 2, 0), 0, 0)),
            ],
            scratch_shapes=[pltpu.VMEM((wide, count), bf16)],
        ),
        out_shape=[parts, parts],
        compiler_params=params(16),
        cost_estimate=cost(2 * full * wide * count, 10**7),
        name="one_back",
    )(info, w_heads.reshape(4, part, wide), dq, dkv_one, dkv_there, dkv_two, wait)


def weight_grad_body(info, own_ref, before_ref, dq_ref, one_ref, two_ref, theirs_ref, mine_ref, acc_ref):
    width = dq_ref.shape[0]
    acc_ref[:, :width] = dot_nt(own_ref[...], dq_ref[...])

    @pl.when(info[0] == 0)
    def _():
        acc_ref[:, width:] = dot_nt(own_ref[...], one_ref[...])

    @pl.when(info[0] != 0)
    def _():
        acc_ref[:, width:] = dot_nt(before_ref[...], one_ref[...]) + dot_nt(own_ref[...], two_ref[...])

    chunk = theirs_ref.shape[1]
    for k in range(4):
        theirs = ((1 - info[0]) * 4 + k) * chunk
        mine = (info[0] * 4 + k) * chunk
        theirs_ref[k] = acc_ref[pl.ds(pl.multiple_of(theirs, 8), chunk), :].astype(bf16)
        mine_ref[k] = acc_ref[pl.ds(pl.multiple_of(mine, 8), chunk), :].astype(bf16)


def weight_grad(info, own, before, dq, dkv_one, dkv_two):
    rows, count = own.shape
    columns = 3 * dq.shape[0]
    result = shape((4, rows // 8, columns), bf16)
    operands = [own, before, dq, dkv_one, dkv_two]
    return pl.pallas_call(
        weight_grad_body,
        grid_spec=pltpu.PrefetchScalarGridSpec(
            num_scalar_prefetch=1,
            grid=(1,),
            in_specs=[whole(array) for array in operands],
            out_specs=[whole(result), whole(result)],
            scratch_shapes=[pltpu.VMEM((rows, columns), f32)],
        ),
        out_shape=[result, result],
        compiler_params=params(24),
        cost_estimate=cost(3 * rows * columns * count, 8 * 10**6),
        name="weight_grad",
    )(info, *operands)


def product_body(left_ref, right_ref, out_ref):
    out_ref[...] = dot_nt(left_ref[...], right_ref[...]).astype(bf16)


def product(left, right):
    rows, count = left.shape
    columns = right.shape[0]
    return pl.pallas_call(
        product_body,
        grid=(2,),
        in_specs=[
            pl.BlockSpec((rows // 2, count), lambda i: (i, 0)),
            pl.BlockSpec((columns, count), lambda i: (0, 0)),
        ],
        out_specs=pl.BlockSpec((rows // 2, columns), lambda i: (i, 0)),
        out_shape=shape((rows, columns), bf16),
        compiler_params=params(24),
        cost_estimate=cost(2 * rows * columns * count, 6 * 10**6),
        name="product",
    )(left, right)


X_SWAP = [(0, 2), (2, 0), (1, 3), (3, 1)]
CORE_SWAP = [(0, 1), (1, 0), (2, 3), (3, 2)]


def swap_x(array):
    return lax.ppermute(array, "col", X_SWAP)


def swap_core(array):
    return lax.ppermute(array, "col", CORE_SWAP)


def swap_seq(array):
    return lax.ppermute(array, "seq", [(0, 1), (1, 0)])


def ring(array, axis, shift):
    count = lax.axis_size(axis)
    return lax.ppermute(array, axis, [(i, (i + shift) % count) for i in range(count)])


def after(array, *done):
    return lax.optimization_barrier((array,) + done)[0]


def after_all(arrays, *done):
    return lax.optimization_barrier(tuple(arrays) + done)[: len(arrays)]


def gather_col(shard):
    other = swap_x(shard)
    beside = swap_core(jnp.stack([shard, other]))
    return shard, other, beside[0], beside[1]


def gather_rest(shard, other):
    beside = swap_core(jnp.stack([shard, other]))
    return shard, other, beside[0], beside[1]


def scatter_col(parts, x_bit, core_bit):
    by_core = parts.reshape((2, 2) + parts.shape[1:])
    mine = lax.dynamic_index_in_dim(by_core, core_bit, 1, keepdims=False)
    theirs = lax.dynamic_index_in_dim(by_core, 1 - core_bit, 1, keepdims=False)
    return across_sum(mine, swap_core(theirs), x_bit)


def across_sum(mine, got, x_bit):
    def of(index):
        return lax.dynamic_index_in_dim(mine, index, 0, keepdims=False).astype(
            f32
        ) + lax.dynamic_index_in_dim(got, index, 0, keepdims=False).astype(f32)

    return of(x_bit), swap_x(of(1 - x_bit).astype(bf16))


def seq_halves(partials):
    theirs = jnp.stack([p[0] for p in partials]) if len(partials) > 1 else partials[0][0][None]
    mine = jnp.stack([p[1] for p in partials]) if len(partials) > 1 else partials[0][1][None]
    return mine, swap_seq(theirs)


def row_chunk(halves, offset):
    index = (lax.axis_index("row") + offset) % 4

    def of(array):
        return lax.dynamic_index_in_dim(array, index, 1, keepdims=False).astype(f32)

    return of(halves[0]) + of(halves[1])


def row_sum_one(halves):
    far = row_chunk(halves, 2).astype(bf16)
    if far.shape[0] == 2:
        return ring(far[0], "row", 1), ring(far[1], "row", -1)
    cut = far.shape[2] // 256 * 128
    return ring(far[0, :, :cut], "row", 1), ring(far[0, :, cut:], "row", -1)


def row_sum_two(halves, far):
    to_right, to_left = row_chunk(halves, 1), row_chunk(halves, 3)
    one, two = (part.astype(f32) for part in far)
    if to_right.shape[0] == 2:
        to_right = jnp.stack([to_right[0] + one, to_right[1]])
        to_left = jnp.stack([to_left[0], to_left[1] + two])
    else:
        cut = one.shape[1]
        to_right = jnp.concatenate([to_right[0, :, :cut] + one, to_right[0, :, cut:]], axis=1)[None]
        to_left = jnp.concatenate([to_left[0, :, :cut], to_left[0, :, cut:] + two], axis=1)[None]
    return ring(to_right.astype(bf16), "row", 1), ring(to_left.astype(bf16), "row", -1)


def row_sum_end(halves, near):
    return row_chunk(halves, 0) + near[0].astype(f32) + near[1].astype(f32)


def scatter_row(partial):
    chunks = partial.reshape(2, 4, partial.shape[0] // 8, partial.shape[1])
    return lax.psum_scatter(chunks, "row", scatter_dimension=1, tiled=False)


def scatter_plain(partial):
    return lax.psum_scatter(partial, ("seq", "row"), scatter_dimension=0, tiled=True).astype(f32)


def combine_axis(array, axis, join):
    total = array
    for shift in range(1, lax.axis_size(axis)):
        total = join(total, ring(array, axis, shift))
    return total


def on_device(
    tokens,
    prefix,
    ln1_gain,
    ln1_bias,
    w_qkv,
    b_qv,
    w_out,
    b_out,
    ln2_gain,
    ln2_bias,
    w_up,
    b_up,
    w_down,
    b_down,
    cotangent,
):
    seq_count = lax.axis_size("seq")
    row_count = lax.axis_size("row")
    col_count = lax.axis_size("col")
    fast = seq_count == 2 and row_count == 4
    seq_index = lax.axis_index("seq")
    row_index = lax.axis_index("row")
    col_index = lax.axis_index("col")
    x_bit = col_index // 2
    core_bit = col_index % 2
    span, part = tokens.shape[1], tokens.shape[2]
    full = part * col_count
    quarter = span // col_count
    fewer = H // col_count
    slots = fewer + 1
    width = slots * E
    spare = width - part

    def by_index(pieces):
        own, across, beside, other = pieces
        even = (jnp.where(core_bit == 0, own, beside), jnp.where(core_bit == 0, across, other))
        odd = (jnp.where(core_bit == 0, beside, own), jnp.where(core_bit == 0, other, across))
        return jnp.concatenate(
            [
                jnp.where(x_bit == 0, even[0], even[1]),
                jnp.where(x_bit == 0, odd[0], odd[1]),
                jnp.where(x_bit == 0, even[1], even[0]),
                jnp.where(x_bit == 0, odd[1], odd[0]),
            ],
            axis=1,
        )

    def first_head(device):
        return jnp.where(device == 0, 0, 1 + fewer * device)

    head_first = first_head(col_index)
    head_count = jnp.where(col_index == 0, fewer + 1, fewer)
    column_shift = head_first * E - col_index * part
    info = jnp.stack([prefix[0], seq_index * span]).astype(jnp.int32)
    order = jnp.stack([col_index, col_index ^ 2, col_index ^ 1, col_index ^ 3]).astype(jnp.int32)

    x_shard = tokens[0].T
    dy_shard = cotangent[0].T
    part_rows = w_qkv.shape[0]
    w_flat = w_qkv.reshape(part_rows, 3 * part)

    def own_rows(array):
        return lax.dynamic_slice_in_dim(array, col_index * part, part, 0)

    vectors = jnp.stack(
        [ln1_gain, ln1_bias, ln2_gain, ln2_bias, b_qv[0], b_qv[1], own_rows(b_out)], axis=1
    )
    x_sent = jnp.concatenate([x_shard, jnp.pad(vectors, ((0, 0), (0, 121))), dy_shard], axis=1)

    slot_column = lax.broadcasted_iota(jnp.int32, (1, 3 * width), 1)
    slot_part, slot_index = slot_column // width, slot_column % width
    slot_source = jnp.where(slot_index < head_count * E, slot_index + column_shift, -1)
    own_row = lax.broadcasted_iota(jnp.int32, (3 * part, 1), 0)
    pick_own = ((own_row // part == slot_part) & (own_row % part == slot_source)).astype(bf16)
    next_row = lax.broadcasted_iota(jnp.int32, (3 * spare, 1), 0)
    pick_next = (
        (next_row // spare == slot_part) & (next_row % spare + part == slot_source)
    ).astype(bf16)
    next_to_here = [(i + 1, i) for i in range(col_count - 1)]
    here_to_next = [(i, i + 1) for i in range(col_count - 1)]

    def edge_of(array):
        return jnp.concatenate([array[:, p * part : p * part + spare] for p in range(3)], axis=1)

    where = jnp.stack([seq_index, head_first * E]).astype(jnp.int32)
    core = core_bit[None].astype(jnp.int32)
    if fast:
        w_sent = jnp.concatenate(
            [w_flat, lax.dynamic_slice_in_dim(w_out, col_index * part, part, 1)], axis=1
        )
        left = ring(w_sent, "row", 1)
        right = ring(w_sent, "row", -1)
        x_before = lax.ppermute(x_shard, "seq", [(0, 1)])
        w_order = ((row_index - jnp.arange(4, dtype=jnp.int32)) % 4).astype(jnp.int32)
        near = near_rows(w_order, [w_sent, after(left, x_before), right], pick_own)
        x_pieces = gather_rest(x_sent, after(swap_x(x_sent), near[2]))
        x_full, normed_one, stats_one, columns, dy_full = first_norm(order, x_pieces, span)
        x_across = swap_x(after(x_before, x_pieces[1]))
        cut = part_rows // 32 * 16 + 16
        far_a = ring(left[:cut], "row", 1)
        far_b = ring(right[cut:], "row", -1)
        w_base, edges, out_mine = far_rows(w_order, near, [far_a, far_b], pick_own, normed_one)
        edges = lax.ppermute(edges, "col", next_to_here)
        some, give = 176, 96
        w_down_rows = w_down.T
        up_piece = jnp.concatenate(
            [lax.dynamic_slice_in_dim(w, seq_index * give, some, 0) for w in (w_up, w_down_rows)]
        )
        up_piece = after(up_piece, out_mine)
        up_left = ring(up_piece, "row", 1)
        up_right = ring(up_piece, "row", -1)

        before_pieces = gather_rest(x_before, after(x_across, out_mine))
        _, normed_before, _ = first_norm(order, before_pieces, span, columns)
        out_across = swap_x(out_mine)
        queries, kv_all, w_heads = project(
            where, w_base, after(edges, normed_before), pick_next, columns, normed_one, normed_before
        )
        attn_one = attn_fwd(info, queries, kv_all, slots, 0)
        attn_across_one = swap_x(attn_one[0])
        out_pieces = gather_rest(out_mine, after(out_across, attn_one[3]))
        def given(pieces):
            return jnp.concatenate(
                [lax.dynamic_slice_in_dim(p, seq_index * (some - give), give, 0) for p in pieces]
            )

        attn_two = attn_fwd(info, after(queries, attn_one[3]), kv_all, slots, 1)
        attn_across_two = swap_x(attn_two[0])
        up_left, up_right = after_all((up_left, up_right), attn_two[3], attn_across_one)
        near_mine = (up_left[:some], up_left[some:], up_right[:some], up_right[some:])
        near_theirs = swap_seq(given(near_mine))
        far_mine = (ring(near_mine[0], "row", 1), ring(near_mine[3], "row", -1))
        attn_pieces_one = gather_rest(attn_one[0], after(attn_across_one, attn_two[3]))
        w_out_t, w_out_all = assemble(
            (order * part).astype(jnp.int32),
            after_all(out_pieces, attn_two[3]),
            [(n, 0, part, n) for n in range(4)],
            full,
            E,
            True,
        )
        far_theirs = swap_seq(given(far_mine))
        def weight(shard, which):
            starts = [row_index * part_rows]
            plan = [(0, 0, part_rows, 0)]
            pieces = [shard, near_mine[which], near_mine[2 + which], far_mine[which], near_theirs, far_theirs]
            mine_at, theirs_at = seq_index * give, (1 - seq_index) * some
            for piece, start, length, away, at in (
                (1, 0, some, 1, mine_at),
                (2, 0, some, 3, mine_at),
                (3, 0, some, 2, mine_at),
                (4, which * give, give, 1, theirs_at),
                (4, (2 + which) * give, give, 3, theirs_at),
                (5, which * give, give, 2, theirs_at),
            ):
                plan.append((piece, start, length, len(starts)))
                starts.append((row_index - away) % 4 * part_rows + at)
            return assemble(jnp.stack(starts).astype(jnp.int32), pieces, plan, full)

    else:
        x_pieces = gather_col(x_sent)
        x_full, normed_one, stats_one, columns, dy_full = first_norm(order, x_pieces, span)
        w_all = lax.all_gather(w_flat, "row", axis=0, tiled=True)
        edges = lax.ppermute(edge_of(w_all), "col", next_to_here)
        w_heads = (dot_nn(w_all, pick_own) + dot_nn(edges, pick_next)).astype(bf16)
        bias = lax.dynamic_slice_in_dim(columns, head_first * E, width, 0)
        projected = dot_tn(w_heads, normed_one)
        queries = (
            (projected[:width] + bias[:, 4:5]).astype(bf16) * E ** (-0.5)
        ).astype(bf16)
        keyvals = jnp.concatenate(
            [projected[width : 2 * width], projected[2 * width :] + bias[:, 5:6]]
        ).astype(bf16)
        kv_all = lax.all_gather(keyvals, "seq", axis=1, tiled=True)
        attn_one = attn_fwd(info, queries, kv_all, slots, 0)
        attn_two = attn_fwd(info, queries, kv_all, slots, 1)
        attn_pieces_one = gather_col(attn_one[0])
        attn_pieces_two = gather_col(attn_two[0])
        w_out_all = jnp.pad(lax.all_gather(w_out, "row", axis=0, tiled=True), ((0, E), (0, 0)))
        w_out_t = w_out_all[:full].T
        w_up_all = lax.all_gather(w_up, "row", axis=0, tiled=True)
        w_down_t = lax.all_gather(w_down.T, "row", axis=0, tiled=True)

    head_rows = (first_head(order) * E).astype(jnp.int32)
    normal_one = out_norm(head_rows, attn_pieces_one, w_out_t, x_full, columns, 0)
    if fast:
        attn_pieces_two = gather_rest(attn_two[0], after(attn_across_two, normal_one[2]))
    normal_two = out_norm(head_rows, attn_pieces_two, w_out_t, x_full, columns, 1)
    if fast:
        far_theirs = after(far_theirs, normal_two[2])
        w_up_all = weight(w_up, 0)
        w_down_t = weight(w_down_rows, 1)

    def joined(index):
        return jnp.concatenate([normal_one[index], normal_two[index]], axis=1)

    after_attn, normed_two, stats_two, attn_all = (joined(i) for i in range(4))
    exact = jnp.concatenate([attn_one[1], attn_two[1]], axis=1)
    lse = jnp.concatenate([attn_one[2], attn_two[2]], axis=1)
    tops = jnp.max(jnp.maximum(attn_one[3], attn_two[3]), axis=1)

    slot_head = jnp.arange(slots, dtype=jnp.int32)
    head_ids = jnp.arange(H, dtype=jnp.int32)
    my_top = jnp.where(slot_head < head_count, tops[:slots], neg_fill)
    placed_top = jnp.max(
        jnp.where(head_ids[None] == (head_first + slot_head)[:, None], my_top[:, None], neg_fill),
        axis=0,
    )
    placed_top = jnp.pad(placed_top, (0, full - H))

    act, grad_pre, back_theirs, back_mine, bup_sums = feed(
        core, normed_two, dy_full, w_up_all, w_down_t, b_up.astype(f32)[:, None]
    )
    back_core = swap_core(back_theirs)
    back_sent = (
        lax.dynamic_index_in_dim(back_mine, 1 - x_bit, 0, keepdims=False).astype(f32)
        + lax.dynamic_index_in_dim(back_core, 1 - x_bit, 0, keepdims=False).astype(f32)
    ).astype(bf16)
    back_got = swap_x(back_sent)
    up_partial = product(normed_two, after(grad_pre, back_sent))
    down_partial = product(dy_full, after(act, back_sent))

    branch_rows, row_sums = second_back(
        jnp.stack([col_index, x_bit]).astype(jnp.int32),
        back_mine,
        back_core,
        after(back_got, up_partial, down_partial),
        after_attn,
        dy_full,
        stats_two,
        columns,
    )
    branch_across = swap_x(branch_rows)
    down = dot_nn(w_down_t, after(act, branch_rows)).astype(bf16).reshape(col_count, part, span)
    head_info = jnp.concatenate([jnp.stack([head_first * E, head_count * E]), order]).astype(jnp.int32)
    branch_pieces = gather_rest(branch_rows, after(branch_across, down))
    branch, grad_attn = attn_grad(head_info, branch_pieces, w_out_all, width)
    middle = jnp.concatenate([row_sums[:, :3].T, placed_top[None]])

    def join(one, two):
        return jnp.concatenate([one[:3] + two[:3], jnp.maximum(one[3:4], two[3:4]), one[4:] + two[4:]])

    middle = after(middle, grad_attn)
    middle = join(middle, swap_x(middle))
    middle = join(middle, swap_core(middle))

    branch_own = own_rows(branch)
    out_partial = dot_nt(attn_all, branch_own).astype(bf16)
    if fast:

        def halves_of(partial):
            chunks = partial.reshape(2, 4, partial.shape[0] // 8, partial.shape[1])
            return [
                lax.dynamic_index_in_dim(chunks, i, 0, keepdims=False) for i in (1 - seq_index, seq_index)
            ]

        feed_halves = seq_halves([halves_of(up_partial), halves_of(down_partial)])
        out_chunks = halves_of(out_partial)
        down_mine, down_got = scatter_col(down, x_bit, core_bit)
        dq_one, dkv_one = attn_bwd(
            info, after(queries, out_partial), kv_all, grad_attn, exact, lse, None, slots, 0, False
        )
        dkv_there = lax.ppermute(dkv_one, "seq", [(1, 0)])
        feed_halves = (feed_halves[0], after(feed_halves[1], dq_one))
        feed_far = row_sum_one(feed_halves)
        dq, dkv_two = attn_bwd(
            info,
            after(queries, dq_one, down_got, middle, feed_halves[1]),
            kv_all,
            grad_attn,
            exact,
            lse,
            dq_one,
            slots,
            1,
            True,
        )
        chunks = weight_grad(where, normed_one, normed_before, dq, dkv_one, dkv_two)
        halves = seq_halves([[jnp.concatenate(pair, axis=2) for pair in zip(chunks, out_chunks)]])
        one_theirs, one_mine = one_back(
            jnp.stack([core_bit, seq_index]).astype(jnp.int32),
            w_heads,
            dq,
            dkv_one,
            dkv_there,
            dkv_two,
            chunks[0],
        )
        feed_near = row_sum_two(feed_halves, after_all(feed_far, one_theirs))
        one_core = swap_core(one_theirs)
        one_mine, one_got = across_sum(one_mine, one_core, x_bit)
        halves = (halves[0], after(halves[1], one_got, *feed_near))
        last_far = row_sum_one(halves)
        feed_sums = row_sum_end(feed_halves, feed_near)
        grad_w_up, grad_w_down = feed_sums[0], feed_sums[1].T
        last_near = row_sum_two(halves, last_far)
        last = row_sum_end(halves, last_near)[0]
        summed, out_columns = last[:, : 3 * width], last[:, 3 * width :].astype(bf16)
        middle = after(middle, *last_far)
        head_sums = jnp.sum(dq.astype(f32), axis=1), (
            jnp.sum(dkv_one[width:].astype(f32), axis=1) + jnp.sum(dkv_two[width:].astype(f32), axis=1)
        )
    else:
        grad_w_up = scatter_plain(up_partial)
        grad_w_down = scatter_plain(down_partial).T
        out_columns = scatter_plain(out_partial).astype(bf16)
        dq, pieces = None, []
        for segment in range(seq_count):
            dq, dkv_one = attn_bwd(
                info, queries, kv_all, grad_attn, exact, lse, dq, slots, segment, segment == seq_count - 1
            )
            pieces.append(dkv_one)
        dkv = lax.psum_scatter(
            jnp.concatenate(pieces, axis=1), "seq", scatter_dimension=1, tiled=True
        )
        heads_grad = jnp.concatenate([dq, dkv])
        one_parts = dot_nn(w_heads, heads_grad).astype(bf16).reshape(col_count, part, span)
        one_mine, one_got = scatter_col(one_parts, x_bit, core_bit)
        summed = scatter_plain(dot_nt(normed_one, heads_grad).astype(bf16))
        head_sums = jnp.sum(dq.astype(f32), axis=1), jnp.sum(dkv[width:].astype(f32), axis=1)
        down_mine, down_got = scatter_col(down, x_bit, core_bit)
    summed = summed.reshape(-1, 3, width)
    grad_w_out = by_index(gather_col(out_columns)).astype(f32)
    block_out = (
        own_rows(after_attn) + down_mine + down_got.astype(f32) + b_down.astype(f32)[:, None]
    ).astype(bf16)

    def to_owner(array):
        wide_array = jnp.pad(array, ((0, 0), (0, 0), (spare, 0)))
        shifted = wide_array[:, :, spare : spare + width]
        for shift in range(1, col_count):
            amount = 1 + fewer * shift
            offset = amount * E - shift * part
            shifted = jnp.where(
                col_index == shift, wide_array[:, :, spare - offset : spare - offset + width], shifted
            )
        sent = lax.ppermute(shifted[:, :, part:].reshape(-1, 3 * spare), "col", here_to_next)
        return shifted[:, :, :part] + jnp.pad(
            sent.reshape(-1, 3, spare), ((0, 0), (0, 0), (0, part - spare))
        )

    grad_w_qkv = to_owner(summed)
    head_sums = jnp.stack(head_sums)
    head_sums = lax.dynamic_update_slice_in_dim(
        jnp.zeros((2, full + E), f32), head_sums, head_first * E, 1
    )[:, :full]

    back_one = one_mine + one_got.astype(f32)
    unit_one = (x_shard.astype(f32) - stats_one[0:1]) * stats_one[1:2]
    unit_grad = back_one * ln1_gain.astype(f32)[:, None]
    sums = jnp.stack([jnp.sum(unit_grad, axis=0), jnp.sum(unit_grad * unit_one, axis=0)])
    sums = jnp.concatenate([jnp.pad(sums, ((0, 0), (0, full - span))) if full > span else sums, head_sums])
    sums = sums + swap_x(sums)
    sums = sums + swap_core(sums)
    bias_grads = lax.dynamic_slice_in_dim(sums[2:], col_index * part, part, 1)
    sums = sums[:2, :span] / full
    grad_tokens = own_rows(branch).astype(f32) + stats_one[1:2] * (
        unit_grad - sums[0:1] - unit_one * sums[1:2]
    )

    small = jnp.concatenate(
        [
            jnp.sum(back_one * unit_one, axis=1),
            jnp.sum(back_one, axis=1),
            jnp.sum(dy_shard.astype(f32), axis=1),
            jnp.zeros((part,), f32),
        ]
    )
    middle = jnp.concatenate(
        [
            middle,
            bup_sums[:, 0][None],
            small[None],
            jnp.pad(bias_grads.reshape(1, -1), ((0, 0), (0, full - 2 * part))),
        ]
    )
    for axis in ("seq", "row"):
        middle = combine_axis(middle, axis, join)
    row_vectors, head_max, grad_b_up = middle[:3], middle[3, :H], middle[4]
    own_vectors = lax.dynamic_slice_in_dim(row_vectors, col_index * part, part, 1)

    def piece(start, length):
        return middle[5, start : start + length]

    root_clip = jnp.sqrt(clip_limit / jnp.maximum(head_max, clip_limit))
    column_head = (col_index * part + jnp.arange(part, dtype=jnp.int32)) // E
    one_hot = (column_head[:, None] == head_ids[None, :]).astype(f32)
    column_root = jnp.sum(one_hot * root_clip[None, :], axis=1)
    scale_three = jnp.stack([column_root, column_root, jnp.ones_like(column_root)])
    clipped_qkv = w_qkv.astype(f32) * scale_three[None]
    return (
        block_out.T[None],
        grad_tokens.T[None],
        piece(0, part),
        piece(part, part),
        grad_w_qkv,
        middle[6, : 2 * part].reshape(2, part),
        grad_w_out,
        row_vectors[2],
        own_vectors[0],
        own_vectors[1],
        grad_w_up,
        grad_b_up,
        grad_w_down,
        piece(2 * part, part),
        clipped_qkv,
        head_max,
    )


def solution(mesh):
    placed = (
        P("row", "seq", "col"),
        P("row"),
        P("col"),
        P("col"),
        P("row", None, "col"),
        P(None, "col"),
        P("row", None),
        P(),
        P("col"),
        P("col"),
        P("row", "col"),
        P("col"),
        P("col", "row"),
        P("col"),
        P("row", "seq", "col"),
    )
    return jax.shard_map(
        on_device,
        mesh=mesh,
        in_specs=placed,
        out_specs=(
            P("row", "seq", "col"),
            P("row", "seq", "col"),
            P("col"),
            P("col"),
            P(("seq", "row"), None, "col"),
            P(None, "col"),
            P(("seq", "row"), None),
            P(),
            P("col"),
            P("col"),
            P(("seq", "row"), "col"),
            P("col"),
            P("col", ("seq", "row")),
            P("col"),
            P("row", None, "col"),
            P(),
        ),
        check_vma=False,
    )
```

```python
import functools

import jax
import jax.numpy as jnp
from jax import lax
from jax.experimental import pallas as pl
from jax.experimental.pallas import tpu as pltpu
from jax.sharding import PartitionSpec as P


H = 17
E = 64

norm_eps = 1e-05
neg_fill = -1e30
clip_limit = 8.0

SCALE = 0.02

f32 = jnp.float32
bf16 = jnp.bfloat16

VMEM = pl.BlockSpec(memory_space=pltpu.VMEM)
SMEM = pl.BlockSpec(memory_space=pltpu.SMEM)
ANY = pl.BlockSpec(memory_space=pl.ANY)


def dot_nn(left, right):
    return lax.dot_general(left, right, (((1,), (0,)), ((), ())), preferred_element_type=f32)


def dot_nt(left, right):
    return lax.dot_general(left, right, (((1,), (1,)), ((), ())), preferred_element_type=f32)


def dot_tn(left, right):
    return lax.dot_general(left, right, (((0,), (0,)), ((), ())), preferred_element_type=f32)


def params(mib=16):
    return pltpu.CompilerParams(vmem_limit_bytes=mib * 2**20)


def cost(flops, moved, exps=0):
    return pl.CostEstimate(
        flops=int(flops * SCALE), bytes_accessed=int(moved * SCALE), transcendentals=int(exps * SCALE)
    )


def waiting(body, inputs, count):
    def wrapped(*refs):
        return body(*refs[:inputs], *refs[inputs + count :])

    return wrapped


def shape(dims, kind):
    return jax.ShapeDtypeStruct(dims, kind)


def rows_at(start, length):
    return pl.ds(pl.multiple_of(start, 16), length)


def assemble_body(plan, fill, turned, starts, *refs):
    pieces, out_ref = (refs[:-2], refs[-2]) if turned else (refs[:-1], refs[-1])
    for piece, source, length, where in plan:
        out_ref[rows_at(starts[where], length), :] = pieces[piece][source : source + length, :]
    if turned:
        rows = out_ref.shape[0]
        refs[-1][:rows, :] = out_ref[...].T
        refs[-1][rows:, :] = jnp.zeros((fill, rows), bf16)


def whole(array):
    return VMEM


def assemble(starts, pieces, plan, rows, fill=0, turned=False):
    result = shape((rows, pieces[0].shape[1]), bf16)
    results = [result, shape((rows + fill, rows), bf16)] if turned else result
    return pl.pallas_call(
        functools.partial(assemble_body, tuple(plan), fill, turned),
        grid_spec=pltpu.PrefetchScalarGridSpec(
            num_scalar_prefetch=1,
            grid=(1,),
            in_specs=[whole(piece) for piece in pieces],
            out_specs=[whole(each) for each in results] if turned else whole(result),
        ),
        out_shape=results,
        compiler_params=params(),
        cost_estimate=cost(0, rows * result.shape[1] * 4),
        name="assemble",
    )(starts, *pieces)


def first_norm_body(own, order, p0, p1, p2, p3, *refs):
    if own:
        x_ref, n_ref, stat_ref, vec_ref, dy_ref = refs
    else:
        vec_ref, x_ref, n_ref, stat_ref = refs
    part = p0.shape[0]
    full, count = x_ref.shape
    if own:
        vec_ref[full:, :] = jnp.zeros((vec_ref.shape[0] - full, vec_ref.shape[1]), f32)
    for n, piece in enumerate((p0, p1, p2, p3)):
        where = rows_at(order[n] * part, part)
        x_ref[where, :] = piece[:, :count]
        if own:
            vec_ref[where, :] = piece[:, count : count + 128].astype(f32)
            dy_ref[where, :] = piece[:, count + 128 :]
    for start in range(0, count, 256):
        cols = slice(start, start + 256)
        x = x_ref[:, cols].astype(f32)
        mean = jnp.sum(x, axis=0, keepdims=True) * (1.0 / full)
        center = x - mean
        inv = lax.rsqrt(jnp.sum(center * center, axis=0, keepdims=True) * (1.0 / full) + norm_eps)
        n_ref[:, cols] = (center * inv * vec_ref[:full, 0:1] + vec_ref[:full, 1:2]).astype(bf16)
        stat_ref[0:1, cols] = mean
        stat_ref[1:2, cols] = inv


def first_norm(order, pieces, count, vectors=None):
    own = vectors is None
    full = pieces[0].shape[0] * 4
    results = [shape((full, count), bf16), shape((full, count), bf16), shape((8, count), f32)]
    operands = list(pieces)
    if own:
        results += [shape((full + E, 128), f32), shape((full, count), bf16)]
    else:
        operands.append(vectors)
    return pl.pallas_call(
        functools.partial(first_norm_body, own),
        grid_spec=pltpu.PrefetchScalarGridSpec(
            num_scalar_prefetch=1,
            grid=(1,),
            in_specs=[whole(array) for array in operands],
            out_specs=[whole(result) for result in results],
        ),
        out_shape=results,
        compiler_params=params(),
        cost_estimate=cost(20 * full * count, full * count * 8),
        name="first_norm",
    )(order, *operands)


def near_rows_body(order, own, left, right, pick_own, base_ref, edge_ref, out_ref):
    size = own.shape[0]
    wide = pick_own.shape[0]
    spare = edge_ref.shape[1]
    for n, piece in ((0, own), (1, left), (3, right)):
        where = rows_at(order[n] * size, size)
        base_ref[where, :] = dot_nn(piece[:, :wide], pick_own[...]).astype(bf16)
        out_ref[where, :] = piece[:, wide:]
        edge_rows(piece, edge_ref, where, wide // 3)


def edge_rows(piece, edge_ref, where, part):
    spare = 5 * E - part
    for p in range(3):
        edge_ref[where, p * spare : (p + 1) * spare] = piece[:, p * part : p * part + spare]


def far_rows_body(order, base, edge, out, far_a, far_b, pick_own, base_ref, edge_ref, turned_ref, out_s):
    size, cut = base.shape[0] // 4, far_a.shape[0]
    wide = pick_own.shape[0]
    base_ref[...] = base[...]
    edge_ref[...] = edge[...]
    out_s[...] = out[...]
    for piece, extra in ((far_a, 0), (far_b, cut)):
        where = rows_at(order[2] * size + extra, piece.shape[0])
        base_ref[where, :] = dot_nn(piece[:, :wide], pick_own[...]).astype(bf16)
        out_s[where, :] = piece[:, wide:]
        edge_rows(piece, edge_ref, where, wide // 3)
    turned_ref[...] = out_s[...].T


def given_body(info, one_ref, two_ref, out_ref, *more):
    give = out_ref.shape[0] // (2 * (one_ref.shape[0] // 176))
    at = 0
    for piece in (one_ref, two_ref):
        for first in range(0, piece.shape[0], 176):
            out_ref[at : at + give, :] = piece[rows_at(first + info[0], give), :]
            at += give
    if more:
        more[0][...] = one_ref[:176, :]
        more[1][...] = two_ref[176:, :]


def given_rows(info, one, two, give):
    parts = one.shape[0] // 176
    columns = one.shape[1]
    results = [shape((2 * parts * give, columns), bf16)]
    if parts == 2:
        results += [shape((176, columns), bf16)] * 2
    return pl.pallas_call(
        given_body,
        grid_spec=pltpu.PrefetchScalarGridSpec(
            num_scalar_prefetch=1, grid=(1,), in_specs=[VMEM] * 2, out_specs=[VMEM] * len(results)
        ),
        out_shape=results,
        compiler_params=params(),
        cost_estimate=cost(0, 3 * 10**6),
        name="given_rows",
    )(info, one, two)


def near_rows(order, pieces, pick_own):
    size = pieces[0].shape[0]
    results = [
        shape((4 * size, pick_own.shape[1]), bf16),
        shape((4 * size, 256), bf16),
        shape((4 * size, size), bf16),
    ]
    return pl.pallas_call(
        near_rows_body,
        grid_spec=pltpu.PrefetchScalarGridSpec(
            num_scalar_prefetch=1, grid=(1,), in_specs=[VMEM] * 4, out_specs=[VMEM] * 3
        ),
        out_shape=results,
        compiler_params=params(),
        cost_estimate=cost(2 * 816 * 816 * 960, 6 * 10**6),
        name="near_rows",
    )(order, *pieces, pick_own)


def far_rows(order, near, far, pick_own, wait):
    size = near[0].shape[0] // 4
    results = [
        shape(near[0].shape, bf16),
        shape(near[1].shape, bf16),
        shape((size, 4 * size), bf16),
    ]
    return pl.pallas_call(
        waiting(far_rows_body, 7, 1),
        grid_spec=pltpu.PrefetchScalarGridSpec(
            num_scalar_prefetch=1,
            grid=(1,),
            in_specs=[VMEM] * 6 + [ANY],
            out_specs=[VMEM] * 3,
            scratch_shapes=[pltpu.VMEM((4 * size, size), bf16)],
        ),
        out_shape=results,
        compiler_params=params(),
        cost_estimate=cost(2 * 272 * 816 * 960, 6 * 10**6),
        name="far_rows",
    )(order, *near, *far, pick_own, wait)


def project_body(width, info, base_ref, edge_ref, pick_ref, bias_ref, own_ref, before_ref, q_ref, kv_ref, w_ref, w_s):
    step = pl.program_id(0)
    half = pl.num_programs(0) // 2
    mine = (step // half) == info[0]

    @pl.when(step == 0)
    def _():
        edges = edge_ref[:, : pick_ref.shape[0]]
        w_ref[...] = base_ref[...] + dot_nn(edges, pick_ref[...]).astype(bf16)
        w_s[...] = w_ref[...].T

    def keyvals(n_ref):
        kv_ref[:width, :] = dot_nn(w_s[width : 2 * width, :], n_ref[...]).astype(bf16)
        kv_ref[width:, :] = (
            dot_nn(w_s[2 * width :, :], n_ref[...]) + bias_ref[rows_at(info[1], width), 5:6]
        ).astype(bf16)

    @pl.when(mine)
    def _():
        out = dot_nn(w_s[:width, :], own_ref[...]) + bias_ref[rows_at(info[1], width), 4:5]
        q_ref[...] = (out.astype(bf16).astype(f32) * E ** (-0.5)).astype(bf16)
        keyvals(own_ref)

    @pl.when(jnp.logical_not(mine))
    def _():
        keyvals(before_ref)


def project(info, base, edges, pick_next, bias, own, before, block=512):
    full, count = own.shape
    wide = base.shape[1]
    width = wide // 3
    steps = count // block
    return pl.pallas_call(
        functools.partial(project_body, width),
        grid_spec=pltpu.PrefetchScalarGridSpec(
            num_scalar_prefetch=1,
            grid=(2 * steps,),
            in_specs=[
                VMEM,
                VMEM,
                VMEM,
                VMEM,
                pl.BlockSpec((full, block), lambda i, s: (0, jnp.clip(i - s[0] * steps, 0, steps - 1))),
                pl.BlockSpec(
                    (full, block), lambda i, s: (0, jnp.clip(i - (1 - s[0]) * steps, 0, steps - 1))
                ),
            ],
            out_specs=[
                pl.BlockSpec((width, block), lambda i, s: (0, jnp.clip(i - s[0] * steps, 0, steps - 1))),
                pl.BlockSpec((2 * width, block), lambda i, s: (0, i)),
                VMEM,
            ],
            scratch_shapes=[pltpu.VMEM((wide, full), bf16)],
        ),
        out_shape=[
            shape((width, count), bf16),
            shape((2 * width, 2 * count), bf16),
            shape((full, wide), bf16),
        ],
        compiler_params=params(24),
        cost_estimate=cost(2 * full * count * 5 * width, 10 * 10**6),
        name="project",
    )(info, base, edges, pick_next, bias, own, before)


def block_limits(info, block, rows):
    prefix_len = info[0]
    query_lo = info[1] + block * rows
    query_hi = query_lo + rows - 1
    in_prefix = query_lo < prefix_len
    limit_max = jnp.where(in_prefix, jnp.maximum(prefix_len - 1, query_hi), query_hi)
    limit_min = jnp.where(in_prefix, prefix_len - 1, query_lo)
    positions = query_lo + lax.broadcasted_iota(jnp.int32, (1, rows), 1)
    return limit_max, limit_min, jnp.where(positions < prefix_len, prefix_len - 1, positions)


def attn_fwd_body(
    slots, keys, first, info, q_ref, kv_ref, attn_ref, exact_ref, lse_ref, top_ref, k_s, m_s, l_s, acc_s
):
    width, rows = q_ref.shape
    limit_max, limit_min, limit = block_limits(info, first, rows)
    n_need = limit_max // keys + 1
    n_full = (limit_min + 1) // keys
    for h in range(slots):
        k_s[h] = kv_ref[h * E : h * E + E, :].T
    m_s[...] = jnp.full_like(m_s, neg_fill)
    l_s[...] = jnp.zeros_like(l_s)
    acc_s[...] = jnp.zeros_like(acc_s)

    def step(index, masked):
        start = pl.multiple_of(index * keys, keys)
        if masked:
            seen = (start + lax.broadcasted_iota(jnp.int32, (keys, rows), 0)) <= limit
        for h in range(slots):
            here, row = slice(h * E, h * E + E), slice(h, h + 1)
            scores = dot_nn(k_s[h, pl.ds(start, keys), :], q_ref[here, :])
            if masked:
                scores = jnp.where(seen, scores, neg_fill)
            old_max = m_s[row, :]
            new_max = jnp.maximum(old_max, jnp.max(scores, axis=0, keepdims=True))
            weights = jnp.exp(scores - new_max)
            shrink = jnp.exp(old_max - new_max)
            l_s[row, :] = l_s[row, :] * shrink + jnp.sum(weights, axis=0, keepdims=True)
            values = kv_ref[width + h * E : width + h * E + E, pl.ds(start, keys)]
            acc_s[here, :] = acc_s[here, :] * shrink + dot_nn(values, weights.astype(bf16))
            m_s[row, :] = new_max

    @pl.loop(0, n_full)
    def _(index):
        step(index, False)

    @pl.loop(n_full, n_need)
    def _(index):
        step(index, True)

    for h in range(slots):
        here, row = slice(h * E, h * E + E), slice(h, h + 1)
        outcome = acc_s[here, :] / l_s[row, :]
        exact_ref[here, :] = outcome
        attn_ref[here, :] = outcome.astype(bf16)
    row_max = m_s[...]
    lse_ref[...] = row_max + jnp.log(l_s[...])
    top = row_max[:, :128]
    for start in range(128, rows, 128):
        top = jnp.maximum(top, row_max[:, start : start + 128])
    top_ref[...] = top


def attn_fwd(info, queries, kv_all, slots, first, rows=512, keys=512):
    width = queries.shape[0]
    total = kv_all.shape[1]
    return pl.pallas_call(
        functools.partial(attn_fwd_body, slots, keys, first),
        grid_spec=pltpu.PrefetchScalarGridSpec(
            num_scalar_prefetch=1,
            grid=(1,),
            in_specs=[
                pl.BlockSpec((width, rows), lambda i, _: (0, first)),
                pl.BlockSpec((2 * width, total), lambda i, _: (0, 0)),
            ],
            out_specs=[
                pl.BlockSpec((width, rows), lambda i, _: (0, 0)),
                pl.BlockSpec((width, rows), lambda i, _: (0, 0)),
                pl.BlockSpec((8, rows), lambda i, _: (0, 0)),
                pl.BlockSpec((8, 128), lambda i, _: (0, 0)),
            ],
            scratch_shapes=[
                pltpu.VMEM((slots, total, E), bf16),
                pltpu.VMEM((8, rows), f32),
                pltpu.VMEM((8, rows), f32),
                pltpu.VMEM((width, rows), f32),
            ],
        ),
        out_shape=[
            shape((width, rows), bf16),
            shape((width, rows), f32),
            shape((8, rows), f32),
            shape((8, 128), f32),
        ],
        compiler_params=params(40),
        cost_estimate=cost(8 * 10**9, 6 * 10**6, 4 * 10**6),
        name="attn_fwd",
    )(info, queries, kv_all)


def attn_bwd_body(slots, keys, key_first, more, last, info, *refs):
    if more:
        q_ref, kv_ref, do_ref, o_ref, lse_ref, dq_in, dq_ref, dkv_ref, k_s, v_s, acc_s, dkv_s = refs
    else:
        q_ref, kv_ref, do_ref, o_ref, lse_ref, dq_ref, dkv_ref, k_s, v_s, acc_s, dkv_s = refs
    block = pl.program_id(0)
    width, rows = q_ref.shape
    n_blocks = kv_ref.shape[1] // keys
    limit_max, limit_min, limit = block_limits(info, block, rows)
    n_need = jnp.clip((limit_max - key_first) // keys + 1, 0, n_blocks)
    n_full = jnp.clip((limit_min - key_first + 1) // keys, 0, n_blocks)
    limit = limit - key_first

    @pl.when(block == 0)
    def _():
        dkv_s[...] = jnp.zeros_like(dkv_s)
        for h in range(slots):
            k_s[h] = kv_ref[h * E : h * E + E, :].T
            v_s[h] = kv_ref[width + h * E : width + h * E + E, :].T

    if more:
        acc_s[...] = dq_in[...]
    else:
        acc_s[...] = jnp.zeros_like(acc_s)
    dots = [
        jnp.sum(
            do_ref[h * E : h * E + E, :].astype(f32) * o_ref[h * E : h * E + E, :],
            axis=0,
            keepdims=True,
        )
        for h in range(slots)
    ]

    def step(index, masked):
        start = pl.multiple_of(index * keys, keys)
        where = pl.ds(start, keys)
        if masked:
            seen = (start + lax.broadcasted_iota(jnp.int32, (keys, rows), 0)) <= limit
        for h in range(slots):
            here = slice(h * E, h * E + E)
            there = slice(width + h * E, width + h * E + E)
            q_head, do_head = q_ref[here, :], do_ref[here, :]
            probs = jnp.exp(dot_nn(k_s[h, where, :], q_head) - lse_ref[h : h + 1, :])
            if masked:
                probs = jnp.where(seen, probs, 0.0)
            grad_probs = dot_nn(v_s[h, where, :], do_head)
            grad_scores = (probs * (grad_probs - dots[h])).astype(bf16)
            dkv_s[there, where] += dot_nt(do_head, probs.astype(bf16))
            dkv_s[here, where] += dot_nt(q_head, grad_scores)
            acc_s[here, :] += dot_nn(kv_ref[here, where], grad_scores)

    @pl.loop(0, n_full)
    def _(index):
        step(index, False)

    @pl.loop(n_full, n_need)
    def _(index):
        step(index, True)

    if last:
        dq_ref[...] = (acc_s[...] * E ** (-0.5)).astype(bf16)
    else:
        dq_ref[...] = acc_s[...]

    @pl.when(block == pl.num_programs(0) - 1)
    def _():
        dkv_ref[...] = dkv_s[...].astype(bf16)


def attn_bwd(
    info, queries, kv_all, grad_attn, exact, lse, dq_in, slots, segment, last, rows=512, keys=512
):
    width, count = queries.shape
    more = dq_in is not None
    block = pl.BlockSpec((width, rows), lambda i, _: (0, i))
    return pl.pallas_call(
        functools.partial(attn_bwd_body, slots, keys, segment * count, more, last),
        grid_spec=pltpu.PrefetchScalarGridSpec(
            num_scalar_prefetch=1,
            grid=(count // rows,),
            in_specs=[
                block,
                pl.BlockSpec((2 * width, count), lambda i, _: (0, segment)),
                block,
                block,
                pl.BlockSpec((8, rows), lambda i, _: (0, i)),
            ]
            + [block] * more,
            out_specs=[block, pl.BlockSpec((2 * width, count), lambda i, _: (0, 0))],
            scratch_shapes=[
                pltpu.VMEM((slots, count, E), bf16),
                pltpu.VMEM((slots, count, E), bf16),
                pltpu.VMEM((width, rows), f32),
                pltpu.VMEM((2 * width, count), f32),
            ],
        ),
        out_shape=[
            shape((width, count), bf16 if last else f32),
            shape((2 * width, count), bf16),
        ],
        compiler_params=params(40),
        cost_estimate=cost(16 * 10**9, 6 * 10**6, 4 * 10**6),
        name="attn_bwd",
    )(info, queries, kv_all, grad_attn, exact, lse, *([dq_in] if more else []))


def out_norm_body(starts, p0, p1, p2, p3, w_ref, x_ref, vec_ref, after_ref, n_ref, stat_ref, attn_ref):
    fewer = (attn_ref.shape[0] // E) // 4 * E
    for n, piece in enumerate((p0, p1, p2, p3)):
        attn_ref[rows_at(starts[n], fewer), :] = piece[:fewer, :]

        @pl.when(starts[n] == 0)
        def _():
            attn_ref[fewer : piece.shape[0], :] = piece[fewer:, :]

    full, count = x_ref.shape
    for start in range(0, count, 256):
        cols = slice(start, start + 256)
        after = x_ref[:, cols].astype(f32) + (
            dot_nn(w_ref[...], attn_ref[:, cols]) + vec_ref[:full, 6:7]
        )
        mean = jnp.sum(after, axis=0, keepdims=True) * (1.0 / full)
        center = after - mean
        inv = lax.rsqrt(jnp.sum(center * center, axis=0, keepdims=True) * (1.0 / full) + norm_eps)
        after_ref[:, cols] = after
        n_ref[:, cols] = (center * inv * vec_ref[:full, 2:3] + vec_ref[:full, 3:4]).astype(bf16)
        stat_ref[0:1, cols] = mean
        stat_ref[1:2, cols] = inv


def out_norm(starts, pieces, w_out_t, x_full, vectors, first):
    full = x_full.shape[0]
    rows, count = pieces[0].shape
    grid_spec = pltpu.PrefetchScalarGridSpec(
        num_scalar_prefetch=1,
        grid=(1,),
        in_specs=[whole(piece) for piece in pieces]
        + [
            pl.BlockSpec(w_out_t.shape, lambda i, _: (0, 0)),
            pl.BlockSpec((full, count), lambda i, _: (0, first)),
            pl.BlockSpec(vectors.shape, lambda i, _: (0, 0)),
        ],
        out_specs=[
            pl.BlockSpec((full, count), lambda i, _: (0, 0)),
            pl.BlockSpec((full, count), lambda i, _: (0, 0)),
            pl.BlockSpec((8, count), lambda i, _: (0, 0)),
            pl.BlockSpec((full, count), lambda i, _: (0, 0)),
        ],
    )
    return pl.pallas_call(
        out_norm_body,
        grid_spec=grid_spec,
        out_shape=[
            shape((full, count), f32),
            shape((full, count), bf16),
            shape((8, count), f32),
            shape((full, count), bf16),
        ],
        compiler_params=params(24),
        cost_estimate=cost(2 * full * full * count, 10**7),
        name="out_norm",
    )(starts, *pieces, w_out_t, x_full, vectors)


def erf_parts(v):
    return 0.5 * (1.0 + lax.erf(v * (0.5**0.5))), jnp.exp(-0.5 * v * v)


def feed_body(
    info, n_ref, dy_ref, up_ref, down_t_ref, b_ref, act_ref, grad_ref, theirs_ref, mine_ref, bias_ref, up_s, down_s
):
    step = pl.program_id(0)

    @pl.when(step == 0)
    def _():
        up_s[...] = up_ref[...].T
        down_s[...] = down_t_ref[...].T
        bias_ref[...] = jnp.zeros_like(bias_ref)

    hidden = up_s.shape[0]
    edges = list(range(0, hidden - 127, 256))
    ones = jnp.ones((n_ref.shape[1], 128), bf16)
    part = 0.0
    for first, end in zip(edges, edges[1:] + [hidden]):
        rows = slice(first, end)
        pre = dot_nn(up_s[rows, :], n_ref[...]) + b_ref[rows, 0:1]
        grad_act = dot_nn(down_s[rows, :], dy_ref[...])
        cdf, bell = erf_parts(pre)
        act_ref[rows, :] = (pre * cdf).astype(bf16)
        grad = (grad_act * (cdf + pre * bell * 0.3989422804014327)).astype(bf16)
        grad_ref[rows, :] = grad
        bias_ref[rows, :] += dot_nn(grad, ones)
        part += dot_nn(up_ref[:, rows], grad)
    part = part.astype(bf16)

    @pl.when(step < 2)
    def _():
        theirs_ref[0] = part

    @pl.when(step >= 2)
    def _():
        mine_ref[0] = part


def turn(step, info):
    return jnp.where(step < 2, 2 * step + 1 - info[0], 2 * (step - 2) + info[0])


def feed(core, normed, dy, w_up, w_down_t, bias):
    full, count = normed.shape
    hidden = w_up.shape[1]
    block = count // 4
    cols = pl.BlockSpec((full, block), lambda i, c: (0, turn(i, c)))
    hid = pl.BlockSpec((hidden, block), lambda i, c: (0, turn(i, c)))
    return pl.pallas_call(
        feed_body,
        grid_spec=pltpu.PrefetchScalarGridSpec(
            num_scalar_prefetch=1,
            grid=(4,),
            in_specs=[
                cols,
                cols,
                pl.BlockSpec((full, hidden), lambda i, c: (0, 0)),
                pl.BlockSpec((full, hidden), lambda i, c: (0, 0)),
                pl.BlockSpec((hidden, 1), lambda i, c: (0, 0)),
            ],
            out_specs=[
                hid,
                hid,
                pl.BlockSpec((1, full, block), lambda i, c: (jnp.minimum(i, 1), 0, 0)),
                pl.BlockSpec((1, full, block), lambda i, c: (jnp.maximum(i - 2, 0), 0, 0)),
                pl.BlockSpec((hidden, 128), lambda i, c: (0, 0)),
            ],
            scratch_shapes=[pltpu.VMEM((hidden, full), bf16), pltpu.VMEM((hidden, full), bf16)],
        ),
        out_shape=[
            shape((hidden, count), bf16),
            shape((hidden, count), bf16),
            shape((2, full, block), bf16),
            shape((2, full, block), bf16),
            shape((hidden, 128), f32),
        ],
        compiler_params=params(40),
        cost_estimate=cost(6 * full * hidden * count, 2 * 10**7, 2 * hidden * count),
        name="feed",
    )(core, normed, dy, w_up, w_down_t, bias)


def second_back_body(index, mine_ref, got_ref, across_ref, after_ref, dy_ref, stat_ref, vec_ref, out_ref, sums_ref):
    back = mine_ref[0].astype(f32) + got_ref[0].astype(f32) + across_ref[...].astype(f32)
    full = back.shape[0]
    mean, inv = stat_ref[0:1, :], stat_ref[1:2, :]
    unit = (after_ref[...] - mean) * inv
    grad = back * vec_ref[:full, 2:3]
    first = jnp.sum(grad, axis=0, keepdims=True) * (1.0 / full)
    second = jnp.sum(grad * unit, axis=0, keepdims=True) * (1.0 / full)
    total = dy_ref[...].astype(f32) + inv * (grad - first - unit * second)
    low = total.astype(bf16)
    out_ref[...] = low
    sums_ref[:, 0:1] = jnp.sum(back * unit, axis=1, keepdims=True)
    sums_ref[:, 1:2] = jnp.sum(back, axis=1, keepdims=True)
    sums_ref[:, 2:3] = jnp.sum(low.astype(f32), axis=1, keepdims=True)


def second_back(index, mine, got, across, after, dy, stats, vectors):
    full, count = across.shape
    fixed = pl.BlockSpec((full, count), lambda i, c: (0, 0))
    moved = pl.BlockSpec((full, count), lambda i, c: (0, c[0]))
    part = pl.BlockSpec((1, full, count), lambda i, c: (c[1], 0, 0))
    return pl.pallas_call(
        second_back_body,
        grid_spec=pltpu.PrefetchScalarGridSpec(
            num_scalar_prefetch=1,
            grid=(1,),
            in_specs=[
                part,
                part,
                fixed,
                moved,
                moved,
                pl.BlockSpec((8, count), lambda i, c: (0, c[0])),
                pl.BlockSpec(vectors.shape, lambda i, c: (0, 0)),
            ],
            out_specs=[fixed, pl.BlockSpec((full, 8), lambda i, c: (0, 0))],
        ),
        out_shape=[shape((full, count), bf16), shape((full, 8), f32)],
        compiler_params=params(16),
        cost_estimate=cost(20 * full * count, 5 * 10**6),
        name="second_back",
    )(index, mine, got, across, after, dy, stats, vectors)


def attn_grad_body(info, p0, p1, p2, p3, w_ref, branch_ref, out_ref):
    count = p0.shape[1]
    width = out_ref.shape[0]
    weights = w_ref[rows_at(info[0], width), :]
    real = lax.broadcasted_iota(jnp.int32, (width, 1), 0) < info[1]
    for n, piece in enumerate((p0, p1, p2, p3)):
        cols = pl.ds(pl.multiple_of(info[2 + n] * count, 128), count)
        branch_ref[:, cols] = piece[...]
        out_ref[:, cols] = jnp.where(real, dot_nn(weights, piece[...]), 0.0).astype(bf16)


def attn_grad(info, pieces, w_out, width):
    full, quarter = pieces[0].shape
    results = [shape((full, 4 * quarter), bf16), shape((width, 4 * quarter), bf16)]
    return pl.pallas_call(
        attn_grad_body,
        grid_spec=pltpu.PrefetchScalarGridSpec(
            num_scalar_prefetch=1,
            grid=(1,),
            in_specs=[whole(array) for array in (*pieces, w_out)],
            out_specs=[whole(result) for result in results],
        ),
        out_shape=results,
        compiler_params=params(),
        cost_estimate=cost(8 * full * quarter * width, 10**7),
        name="attn_grad",
    )(info, *pieces, w_out)


def one_back_body(info, w_ref, dq_ref, one_ref, there_ref, two_ref, theirs_ref, mine_ref, grad_ref):
    step = pl.program_id(0)
    width = dq_ref.shape[0]

    @pl.when(step == 0)
    def _():
        grad_ref[:width, :] = dq_ref[...]

    @pl.when((step == 0) & (info[1] == 0))
    def _():
        grad_ref[width:, :] = (one_ref[...].astype(f32) + there_ref[...].astype(f32)).astype(bf16)

    @pl.when((step == 0) & (info[1] != 0))
    def _():
        grad_ref[width:, :] = two_ref[...]

    part = dot_nn(w_ref[0], grad_ref[...]).astype(bf16)

    @pl.when(step < 2)
    def _():
        theirs_ref[0] = part

    @pl.when(step >= 2)
    def _():
        mine_ref[0] = part


def one_back(info, w_heads, dq, dkv_one, dkv_there, dkv_two, wait):
    full, wide = w_heads.shape
    count = dq.shape[1]
    part = full // 4
    parts = shape((2, part, count), bf16)
    return pl.pallas_call(
        waiting(one_back_body, 6, 1),
        grid_spec=pltpu.PrefetchScalarGridSpec(
            num_scalar_prefetch=1,
            grid=(4,),
            in_specs=[pl.BlockSpec((1, part, wide), lambda i, c: (turn(i, c), 0, 0))]
            + [whole(array) for array in (dq, dkv_one, dkv_there, dkv_two)]
            + [ANY],
            out_specs=[
                pl.BlockSpec((1, part, count), lambda i, c: (jnp.minimum(i, 1), 0, 0)),
                pl.BlockSpec((1, part, count), lambda i, c: (jnp.maximum(i - 2, 0), 0, 0)),
            ],
            scratch_shapes=[pltpu.VMEM((wide, count), bf16)],
        ),
        out_shape=[parts, parts],
        compiler_params=params(16),
        cost_estimate=cost(2 * full * wide * count, 10**7),
        name="one_back",
    )(info, w_heads.reshape(4, part, wide), dq, dkv_one, dkv_there, dkv_two, wait)


def weight_grad_body(info, own_ref, before_ref, dq_ref, one_ref, two_ref, theirs_ref, mine_ref, acc_ref):
    width = dq_ref.shape[0]
    acc_ref[:, :width] = dot_nt(own_ref[...], dq_ref[...])

    @pl.when(info[0] == 0)
    def _():
        acc_ref[:, width:] = dot_nt(own_ref[...], one_ref[...])

    @pl.when(info[0] != 0)
    def _():
        acc_ref[:, width:] = dot_nt(before_ref[...], one_ref[...]) + dot_nt(own_ref[...], two_ref[...])

    chunk = theirs_ref.shape[1]
    for k in range(4):
        theirs = ((1 - info[0]) * 4 + k) * chunk
        mine = (info[0] * 4 + k) * chunk
        theirs_ref[k] = acc_ref[pl.ds(pl.multiple_of(theirs, 8), chunk), :].astype(bf16)
        mine_ref[k] = acc_ref[pl.ds(pl.multiple_of(mine, 8), chunk), :].astype(bf16)


def weight_grad(info, own, before, dq, dkv_one, dkv_two):
    rows, count = own.shape
    columns = 3 * dq.shape[0]
    result = shape((4, rows // 8, columns), bf16)
    operands = [own, before, dq, dkv_one, dkv_two]
    return pl.pallas_call(
        weight_grad_body,
        grid_spec=pltpu.PrefetchScalarGridSpec(
            num_scalar_prefetch=1,
            grid=(1,),
            in_specs=[whole(array) for array in operands],
            out_specs=[whole(result), whole(result)],
            scratch_shapes=[pltpu.VMEM((rows, columns), f32)],
        ),
        out_shape=[result, result],
        compiler_params=params(24),
        cost_estimate=cost(3 * rows * columns * count, 8 * 10**6),
        name="weight_grad",
    )(info, *operands)


def product_body(left_ref, right_ref, out_ref):
    out_ref[...] = dot_nt(left_ref[...], right_ref[...]).astype(bf16)


def product(left, right):
    rows, count = left.shape
    columns = right.shape[0]
    return pl.pallas_call(
        product_body,
        grid=(2,),
        in_specs=[
            pl.BlockSpec((rows // 2, count), lambda i: (i, 0)),
            pl.BlockSpec((columns, count), lambda i: (0, 0)),
        ],
        out_specs=pl.BlockSpec((rows // 2, columns), lambda i: (i, 0)),
        out_shape=shape((rows, columns), bf16),
        compiler_params=params(24),
        cost_estimate=cost(2 * rows * columns * count, 6 * 10**6),
        name="product",
    )(left, right)


X_SWAP = [(0, 2), (2, 0), (1, 3), (3, 1)]
CORE_SWAP = [(0, 1), (1, 0), (2, 3), (3, 2)]


def swap_x(array):
    return lax.ppermute(array, "col", X_SWAP)


def swap_core(array):
    return lax.ppermute(array, "col", CORE_SWAP)


def swap_seq(array):
    return lax.ppermute(array, "seq", [(0, 1), (1, 0)])


def ring(array, axis, shift):
    count = lax.axis_size(axis)
    return lax.ppermute(array, axis, [(i, (i + shift) % count) for i in range(count)])


def after(array, *done):
    return lax.optimization_barrier((array,) + done)[0]


def after_all(arrays, *done):
    return lax.optimization_barrier(tuple(arrays) + done)[: len(arrays)]


def gather_col(shard):
    other = swap_x(shard)
    beside = swap_core(jnp.stack([shard, other]))
    return shard, other, beside[0], beside[1]


def gather_rest(shard, other):
    beside = swap_core(jnp.stack([shard, other]))
    return shard, other, beside[0], beside[1]


def scatter_col(parts, x_bit, core_bit):
    by_core = parts.reshape((2, 2) + parts.shape[1:])
    mine = lax.dynamic_index_in_dim(by_core, core_bit, 1, keepdims=False)
    theirs = lax.dynamic_index_in_dim(by_core, 1 - core_bit, 1, keepdims=False)
    return across_sum(mine, swap_core(theirs), x_bit)


def across_sum(mine, got, x_bit):
    def of(index):
        return lax.dynamic_index_in_dim(mine, index, 0, keepdims=False).astype(
            f32
        ) + lax.dynamic_index_in_dim(got, index, 0, keepdims=False).astype(f32)

    return of(x_bit), swap_x(of(1 - x_bit).astype(bf16))


def seq_halves(partials):
    theirs = jnp.stack([p[0] for p in partials]) if len(partials) > 1 else partials[0][0][None]
    mine = jnp.stack([p[1] for p in partials]) if len(partials) > 1 else partials[0][1][None]
    return mine, swap_seq(theirs)


def row_chunk(halves, offset):
    index = (lax.axis_index("row") + offset) % 4

    def of(array):
        return lax.dynamic_index_in_dim(array, index, 1, keepdims=False).astype(f32)

    return of(halves[0]) + of(halves[1])


def row_sum_one(halves):
    far = row_chunk(halves, 2).astype(bf16)
    if far.shape[0] == 2:
        return ring(far[0], "row", 1), ring(far[1], "row", -1)
    cut = far.shape[2] // 256 * 128
    return ring(far[0, :, :cut], "row", 1), ring(far[0, :, cut:], "row", -1)


def row_sum_two(halves, far):
    to_right, to_left = row_chunk(halves, 1), row_chunk(halves, 3)
    one, two = (part.astype(f32) for part in far)
    if to_right.shape[0] == 2:
        to_right = jnp.stack([to_right[0] + one, to_right[1]])
        to_left = jnp.stack([to_left[0], to_left[1] + two])
    else:
        cut = one.shape[1]
        to_right = jnp.concatenate([to_right[0, :, :cut] + one, to_right[0, :, cut:]], axis=1)[None]
        to_left = jnp.concatenate([to_left[0, :, :cut], to_left[0, :, cut:] + two], axis=1)[None]
    return ring(to_right.astype(bf16), "row", 1), ring(to_left.astype(bf16), "row", -1)


def row_sum_end(halves, near):
    return row_chunk(halves, 0) + near[0].astype(f32) + near[1].astype(f32)


def scatter_row(partial):
    chunks = partial.reshape(2, 4, partial.shape[0] // 8, partial.shape[1])
    return lax.psum_scatter(chunks, "row", scatter_dimension=1, tiled=False)


def scatter_plain(partial):
    return lax.psum_scatter(partial, ("seq", "row"), scatter_dimension=0, tiled=True).astype(f32)


def combine_axis(array, axis, join):
    total = array
    for shift in range(1, lax.axis_size(axis)):
        total = join(total, ring(array, axis, shift))
    return total


def on_device(
    tokens,
    prefix,
    ln1_gain,
    ln1_bias,
    w_qkv,
    b_qv,
    w_out,
    b_out,
    ln2_gain,
    ln2_bias,
    w_up,
    b_up,
    w_down,
    b_down,
    cotangent,
):
    seq_count = lax.axis_size("seq")
    row_count = lax.axis_size("row")
    col_count = lax.axis_size("col")
    fast = seq_count == 2 and row_count == 4
    seq_index = lax.axis_index("seq")
    row_index = lax.axis_index("row")
    col_index = lax.axis_index("col")
    x_bit = col_index // 2
    core_bit = col_index % 2
    span, part = tokens.shape[1], tokens.shape[2]
    full = part * col_count
    quarter = span // col_count
    fewer = H // col_count
    slots = fewer + 1
    width = slots * E
    spare = width - part

    def by_index(pieces):
        own, across, beside, other = pieces
        even = (jnp.where(core_bit == 0, own, beside), jnp.where(core_bit == 0, across, other))
        odd = (jnp.where(core_bit == 0, beside, own), jnp.where(core_bit == 0, other, across))
        return jnp.concatenate(
            [
                jnp.where(x_bit == 0, even[0], even[1]),
                jnp.where(x_bit == 0, odd[0], odd[1]),
                jnp.where(x_bit == 0, even[1], even[0]),
                jnp.where(x_bit == 0, odd[1], odd[0]),
            ],
            axis=1,
        )

    def first_head(device):
        return jnp.where(device == 0, 0, 1 + fewer * device)

    head_first = first_head(col_index)
    head_count = jnp.where(col_index == 0, fewer + 1, fewer)
    column_shift = head_first * E - col_index * part
    info = jnp.stack([prefix[0], seq_index * span]).astype(jnp.int32)
    order = jnp.stack([col_index, col_index ^ 2, col_index ^ 1, col_index ^ 3]).astype(jnp.int32)

    x_shard = tokens[0].T
    dy_shard = cotangent[0].T
    part_rows = w_qkv.shape[0]
    w_flat = w_qkv.reshape(part_rows, 3 * part)

    def own_rows(array):
        return lax.dynamic_slice_in_dim(array, col_index * part, part, 0)

    vectors = jnp.stack(
        [ln1_gain, ln1_bias, ln2_gain, ln2_bias, b_qv[0], b_qv[1], own_rows(b_out)], axis=1
    )
    x_sent = jnp.concatenate([x_shard, jnp.pad(vectors, ((0, 0), (0, 121))), dy_shard], axis=1)

    slot_column = lax.broadcasted_iota(jnp.int32, (1, 3 * width), 1)
    slot_part, slot_index = slot_column // width, slot_column % width
    slot_source = jnp.where(slot_index < head_count * E, slot_index + column_shift, -1)
    own_row = lax.broadcasted_iota(jnp.int32, (3 * part, 1), 0)
    pick_own = ((own_row // part == slot_part) & (own_row % part == slot_source)).astype(bf16)
    next_row = lax.broadcasted_iota(jnp.int32, (3 * spare, 1), 0)
    pick_next = (
        (next_row // spare == slot_part) & (next_row % spare + part == slot_source)
    ).astype(bf16)
    next_to_here = [(i + 1, i) for i in range(col_count - 1)]
    here_to_next = [(i, i + 1) for i in range(col_count - 1)]

    def edge_of(array):
        return jnp.concatenate([array[:, p * part : p * part + spare] for p in range(3)], axis=1)

    where = jnp.stack([seq_index, head_first * E]).astype(jnp.int32)
    core = core_bit[None].astype(jnp.int32)
    if fast:
        w_sent = jnp.concatenate(
            [w_flat, lax.dynamic_slice_in_dim(w_out, col_index * part, part, 1)], axis=1
        )
        left = ring(w_sent, "row", 1)
        right = ring(w_sent, "row", -1)
        x_before = lax.ppermute(x_shard, "seq", [(0, 1)])
        w_order = ((row_index - jnp.arange(4, dtype=jnp.int32)) % 4).astype(jnp.int32)
        near = near_rows(w_order, [w_sent, after(left, x_before), right], pick_own)
        x_pieces = gather_rest(x_sent, after(swap_x(x_sent), near[2]))
        x_full, normed_one, stats_one, columns, dy_full = first_norm(order, x_pieces, span)
        x_across = swap_x(after(x_before, x_pieces[1]))
        cut = part_rows // 32 * 16 + 16
        far_a = ring(left[:cut], "row", 1)
        far_b = ring(right[cut:], "row", -1)
        w_base, edges, out_mine = far_rows(w_order, near, [far_a, far_b], pick_own, normed_one)
        edges = lax.ppermute(edges, "col", next_to_here)
        some, give = 176, 96
        w_down_rows = w_down.T
        up_piece = jnp.concatenate(
            [lax.dynamic_slice_in_dim(w, seq_index * give, some, 0) for w in (w_up, w_down_rows)]
        )
        up_piece = after(up_piece, out_mine)
        up_left = ring(up_piece, "row", 1)
        up_right = ring(up_piece, "row", -1)

        before_pieces = gather_rest(x_before, after(x_across, out_mine))
        _, normed_before, _ = first_norm(order, before_pieces, span, columns)
        out_across = swap_x(after(out_mine, edges))
        queries, kv_all, w_heads = project(
            where, w_base, after(edges, normed_before), pick_next, columns, normed_one, normed_before
        )
        attn_one = attn_fwd(info, queries, kv_all, slots, 0)
        attn_across_one = swap_x(attn_one[0])
        out_pieces = gather_rest(out_mine, after(out_across, attn_one[3]))
        up_left, up_right = after_all((up_left, up_right), attn_one[3])
        lacked = (seq_index * (some - give))[None].astype(jnp.int32)
        near_given, up_on, down_on = given_rows(lacked, up_left, up_right, give)
        near_theirs = swap_seq(near_given)
        far_mine = (ring(up_on, "row", 1), ring(down_on, "row", -1))
        attn_two = attn_fwd(info, after(queries, attn_one[3], near_given), kv_all, slots, 1)
        attn_across_two = swap_x(attn_two[0])
        far_mine = after_all(far_mine, attn_two[3], attn_across_one)
        attn_pieces_one = gather_rest(attn_one[0], after(attn_across_one, attn_two[3]))
        w_out_t, w_out_all = assemble(
            (order * part).astype(jnp.int32),
            after_all(out_pieces, attn_two[3]),
            [(n, 0, part, n) for n in range(4)],
            full,
            E,
            True,
        )
        far_theirs = swap_seq(given_rows(lacked, *far_mine, give)[0])
        def weight(shard, which):
            starts = [row_index * part_rows]
            plan = [(0, 0, part_rows, 0)]
            pieces = [shard, up_left, up_right, far_mine[which], near_theirs, far_theirs]
            mine_at, theirs_at = seq_index * give, (1 - seq_index) * some
            for piece, start, length, away, at in (
                (1, which * some, some, 1, mine_at),
                (2, which * some, some, 3, mine_at),
                (3, 0, some, 2, mine_at),
                (4, which * give, give, 1, theirs_at),
                (4, (2 + which) * give, give, 3, theirs_at),
                (5, which * give, give, 2, theirs_at),
            ):
                plan.append((piece, start, length, len(starts)))
                starts.append((row_index - away) % 4 * part_rows + at)
            return assemble(jnp.stack(starts).astype(jnp.int32), pieces, plan, full)

    else:
        x_pieces = gather_col(x_sent)
        x_full, normed_one, stats_one, columns, dy_full = first_norm(order, x_pieces, span)
        w_all = lax.all_gather(w_flat, "row", axis=0, tiled=True)
        edges = lax.ppermute(edge_of(w_all), "col", next_to_here)
        w_heads = (dot_nn(w_all, pick_own) + dot_nn(edges, pick_next)).astype(bf16)
        bias = lax.dynamic_slice_in_dim(columns, head_first * E, width, 0)
        projected = dot_tn(w_heads, normed_one)
        queries = (
            (projected[:width] + bias[:, 4:5]).astype(bf16) * E ** (-0.5)
        ).astype(bf16)
        keyvals = jnp.concatenate(
            [projected[width : 2 * width], projected[2 * width :] + bias[:, 5:6]]
        ).astype(bf16)
        kv_all = lax.all_gather(keyvals, "seq", axis=1, tiled=True)
        attn_one = attn_fwd(info, queries, kv_all, slots, 0)
        attn_two = attn_fwd(info, queries, kv_all, slots, 1)
        attn_pieces_one = gather_col(attn_one[0])
        attn_pieces_two = gather_col(attn_two[0])
        w_out_all = jnp.pad(lax.all_gather(w_out, "row", axis=0, tiled=True), ((0, E), (0, 0)))
        w_out_t = w_out_all[:full].T
        w_up_all = lax.all_gather(w_up, "row", axis=0, tiled=True)
        w_down_t = lax.all_gather(w_down.T, "row", axis=0, tiled=True)

    head_rows = (first_head(order) * E).astype(jnp.int32)
    normal_one = out_norm(head_rows, attn_pieces_one, w_out_t, x_full, columns, 0)
    if fast:
        attn_pieces_two = gather_rest(attn_two[0], after(attn_across_two, normal_one[2]))
    normal_two = out_norm(head_rows, attn_pieces_two, w_out_t, x_full, columns, 1)
    if fast:
        far_theirs = after(far_theirs, normal_two[2])
        w_up_all = weight(w_up, 0)
        w_down_t = weight(w_down_rows, 1)

    def joined(index):
        return jnp.concatenate([normal_one[index], normal_two[index]], axis=1)

    after_attn, normed_two, stats_two, attn_all = (joined(i) for i in range(4))
    exact = jnp.concatenate([attn_one[1], attn_two[1]], axis=1)
    lse = jnp.concatenate([attn_one[2], attn_two[2]], axis=1)
    tops = jnp.max(jnp.maximum(attn_one[3], attn_two[3]), axis=1)

    slot_head = jnp.arange(slots, dtype=jnp.int32)
    head_ids = jnp.arange(H, dtype=jnp.int32)
    my_top = jnp.where(slot_head < head_count, tops[:slots], neg_fill)
    placed_top = jnp.max(
        jnp.where(head_ids[None] == (head_first + slot_head)[:, None], my_top[:, None], neg_fill),
        axis=0,
    )
    placed_top = jnp.pad(placed_top, (0, full - H))

    act, grad_pre, back_theirs, back_mine, bup_sums = feed(
        core, normed_two, dy_full, w_up_all, w_down_t, b_up.astype(f32)[:, None]
    )
    back_core = swap_core(back_theirs)
    back_sent = (
        lax.dynamic_index_in_dim(back_mine, 1 - x_bit, 0, keepdims=False).astype(f32)
        + lax.dynamic_index_in_dim(back_core, 1 - x_bit, 0, keepdims=False).astype(f32)
    ).astype(bf16)
    back_got = swap_x(back_sent)
    up_partial = product(normed_two, after(grad_pre, back_sent))
    down_partial = product(dy_full, after(act, back_sent))

    branch_rows, row_sums = second_back(
        jnp.stack([col_index, x_bit]).astype(jnp.int32),
        back_mine,
        back_core,
        after(back_got, up_partial, down_partial),
        after_attn,
        dy_full,
        stats_two,
        columns,
    )
    branch_across = swap_x(branch_rows)
    if fast:
        down_chunks = down_partial.reshape(2, 4, full // 8, full)

        def down_chunk(offset):
            return lax.dynamic_index_in_dim(down_chunks, (row_index + offset) % 4, 1, keepdims=False)

        down_far = down_chunk(2)
        down_far = ring(down_far[0], "row", 1), ring(down_far[1], "row", -1)
    else:
        down_far = ()
    down = dot_nn(w_down_t, after(act, branch_rows)).astype(bf16).reshape(col_count, part, span)
    head_info = jnp.concatenate([jnp.stack([head_first * E, head_count * E]), order]).astype(jnp.int32)
    branch_pieces = gather_rest(branch_rows, after(branch_across, down, *down_far))
    branch, grad_attn = attn_grad(head_info, branch_pieces, w_out_all, width)
    middle = jnp.concatenate([row_sums[:, :3].T, placed_top[None]])

    def join(one, two):
        return jnp.concatenate([one[:3] + two[:3], jnp.maximum(one[3:4], two[3:4]), one[4:] + two[4:]])

    middle = after(middle, grad_attn)
    middle = join(middle, swap_x(middle))
    middle = join(middle, swap_core(middle))

    branch_own = own_rows(branch)
    out_partial = dot_nt(attn_all, branch_own).astype(bf16)
    if fast:

        def halves_of(partial):
            chunks = partial.reshape(2, 4, partial.shape[0] // 8, partial.shape[1])
            return [
                lax.dynamic_index_in_dim(chunks, i, 0, keepdims=False) for i in (1 - seq_index, seq_index)
            ]

        feed_halves = seq_halves([halves_of(up_partial)])
        down_far = after_all(down_far, *branch_pieces[2:])
        to_right, to_left = down_chunk(1).astype(f32), down_chunk(3).astype(f32)
        to_right = jnp.stack([to_right[0] + down_far[0].astype(f32), to_right[1]]).astype(bf16)
        to_left = jnp.stack([to_left[0], to_left[1] + down_far[1].astype(f32)]).astype(bf16)
        down_near = ring(to_right, "row", 1), ring(to_left, "row", -1)
        out_chunks = halves_of(out_partial)
        down_mine, down_got = scatter_col(down, x_bit, core_bit)
        dq_one, dkv_one = attn_bwd(
            info, after(queries, out_partial), kv_all, grad_attn, exact, lse, None, slots, 0, False
        )
        dkv_there = lax.ppermute(dkv_one, "seq", [(1, 0)])
        dq, dkv_two = attn_bwd(
            info,
            after(queries, dq_one, down_got, middle),
            kv_all,
            grad_attn,
            exact,
            lse,
            dq_one,
            slots,
            1,
            True,
        )
        feed_halves = (feed_halves[0], after(feed_halves[1], dq))
        feed_far = row_sum_one(feed_halves)
        chunks = weight_grad(where, normed_one, normed_before, dq, dkv_one, dkv_two)
        halves = seq_halves([[jnp.concatenate(pair, axis=2) for pair in zip(chunks, out_chunks)]])
        one_theirs, one_mine = one_back(
            jnp.stack([core_bit, seq_index]).astype(jnp.int32),
            w_heads,
            dq,
            dkv_one,
            dkv_there,
            dkv_two,
            chunks[0],
        )
        feed_near = row_sum_two(feed_halves, after_all(feed_far, one_theirs))
        down_sums = down_chunk(0).astype(f32) + sum(p.astype(f32) for p in after_all(down_near, dq))
        down_sent = lax.dynamic_index_in_dim(down_sums, 1 - seq_index, 0, keepdims=False).astype(bf16)
        down_sent = swap_seq(after(down_sent, halves[1]))
        down_sums = lax.dynamic_index_in_dim(down_sums, seq_index, 0, keepdims=False)
        one_core = after(swap_core(one_theirs), halves[1])
        one_mine, one_got = across_sum(one_mine, one_core, x_bit)
        last_far = row_sum_one(halves)
        feed_sums = row_sum_end(feed_halves, feed_near)
        last_far = after_all(last_far, down_sent, *feed_near)
        grad_w_up = feed_sums[0]
        grad_w_down = (down_sums + down_sent.astype(f32)).T
        last_near = row_sum_two(halves, last_far)
        last = row_sum_end(halves, after_all(last_near, one_got))[0]
        summed, out_columns = last[:, : 3 * width], last[:, 3 * width :].astype(bf16)
        middle = after(middle, *last_far)
        head_sums = jnp.sum(dq.astype(f32), axis=1), (
            jnp.sum(dkv_one[width:].astype(f32), axis=1) + jnp.sum(dkv_two[width:].astype(f32), axis=1)
        )
    else:
        grad_w_up = scatter_plain(up_partial)
        grad_w_down = scatter_plain(down_partial).T
        out_columns = scatter_plain(out_partial).astype(bf16)
        dq, pieces = None, []
        for segment in range(seq_count):
            dq, dkv_one = attn_bwd(
                info, queries, kv_all, grad_attn, exact, lse, dq, slots, segment, segment == seq_count - 1
            )
            pieces.append(dkv_one)
        dkv = lax.psum_scatter(
            jnp.concatenate(pieces, axis=1), "seq", scatter_dimension=1, tiled=True
        )
        heads_grad = jnp.concatenate([dq, dkv])
        one_parts = dot_nn(w_heads, heads_grad).astype(bf16).reshape(col_count, part, span)
        one_mine, one_got = scatter_col(one_parts, x_bit, core_bit)
        summed = scatter_plain(dot_nt(normed_one, heads_grad).astype(bf16))
        head_sums = jnp.sum(dq.astype(f32), axis=1), jnp.sum(dkv[width:].astype(f32), axis=1)
        down_mine, down_got = scatter_col(down, x_bit, core_bit)
    summed = summed.reshape(-1, 3, width)
    grad_w_out = by_index(gather_col(out_columns)).astype(f32)
    block_out = (
        own_rows(after_attn) + down_mine + down_got.astype(f32) + b_down.astype(f32)[:, None]
    ).astype(bf16)

    def to_owner(array):
        wide_array = jnp.pad(array, ((0, 0), (0, 0), (spare, 0)))
        shifted = wide_array[:, :, spare : spare + width]
        for shift in range(1, col_count):
            amount = 1 + fewer * shift
            offset = amount * E - shift * part
            shifted = jnp.where(
                col_index == shift, wide_array[:, :, spare - offset : spare - offset + width], shifted
            )
        sent = lax.ppermute(shifted[:, :, part:].reshape(-1, 3 * spare), "col", here_to_next)
        return shifted[:, :, :part] + jnp.pad(
            sent.reshape(-1, 3, spare), ((0, 0), (0, 0), (0, part - spare))
        )

    grad_w_qkv = to_owner(summed)
    head_sums = jnp.stack(head_sums)
    head_sums = lax.dynamic_update_slice_in_dim(
        jnp.zeros((2, full + E), f32), head_sums, head_first * E, 1
    )[:, :full]

    back_one = one_mine + one_got.astype(f32)
    unit_one = (x_shard.astype(f32) - stats_one[0:1]) * stats_one[1:2]
    unit_grad = back_one * ln1_gain.astype(f32)[:, None]
    sums = jnp.stack([jnp.sum(unit_grad, axis=0), jnp.sum(unit_grad * unit_one, axis=0)])
    sums = jnp.concatenate([jnp.pad(sums, ((0, 0), (0, full - span))) if full > span else sums, head_sums])
    sums = sums + swap_x(sums)
    sums = sums + swap_core(sums)
    bias_grads = lax.dynamic_slice_in_dim(sums[2:], col_index * part, part, 1)
    sums = sums[:2, :span] / full
    grad_tokens = own_rows(branch).astype(f32) + stats_one[1:2] * (
        unit_grad - sums[0:1] - unit_one * sums[1:2]
    )

    small = jnp.concatenate(
        [
            jnp.sum(back_one * unit_one, axis=1),
            jnp.sum(back_one, axis=1),
            jnp.sum(dy_shard.astype(f32), axis=1),
            jnp.zeros((part,), f32),
        ]
    )
    middle = jnp.concatenate(
        [
            middle,
            bup_sums[:, 0][None],
            small[None],
            jnp.pad(bias_grads.reshape(1, -1), ((0, 0), (0, full - 2 * part))),
        ]
    )
    for axis in ("seq", "row"):
        middle = combine_axis(middle, axis, join)
    row_vectors, head_max, grad_b_up = middle[:3], middle[3, :H], middle[4]
    own_vectors = lax.dynamic_slice_in_dim(row_vectors, col_index * part, part, 1)

    def piece(start, length):
        return middle[5, start : start + length]

    root_clip = jnp.sqrt(clip_limit / jnp.maximum(head_max, clip_limit))
    column_head = (col_index * part + jnp.arange(part, dtype=jnp.int32)) // E
    one_hot = (column_head[:, None] == head_ids[None, :]).astype(f32)
    column_root = jnp.sum(one_hot * root_clip[None, :], axis=1)
    scale_three = jnp.stack([column_root, column_root, jnp.ones_like(column_root)])
    clipped_qkv = w_qkv.astype(f32) * scale_three[None]
    return (
        block_out.T[None],
        grad_tokens.T[None],
        piece(0, part),
        piece(part, part),
        grad_w_qkv,
        middle[6, : 2 * part].reshape(2, part),
        grad_w_out,
        row_vectors[2],
        own_vectors[0],
        own_vectors[1],
        grad_w_up,
        grad_b_up,
        grad_w_down,
        piece(2 * part, part),
        clipped_qkv,
        head_max,
    )


def solution(mesh):
    placed = (
        P("row", "seq", "col"),
        P("row"),
        P("col"),
        P("col"),
        P("row", None, "col"),
        P(None, "col"),
        P("row", None),
        P(),
        P("col"),
        P("col"),
        P("row", "col"),
        P("col"),
        P("col", "row"),
        P("col"),
        P("row", "seq", "col"),
    )
    return jax.shard_map(
        on_device,
        mesh=mesh,
        in_specs=placed,
        out_specs=(
            P("row", "seq", "col"),
            P("row", "seq", "col"),
            P("col"),
            P("col"),
            P(("seq", "row"), None, "col"),
            P(None, "col"),
            P(("seq", "row"), None),
            P(),
            P("col"),
            P("col"),
            P(("seq", "row"), "col"),
            P("col"),
            P("col", ("seq", "row")),
            P("col"),
            P("row", None, "col"),
            P(),
        ),
        check_vma=False,
    )
```

```python
import functools

import jax
import jax.numpy as jnp
from jax import lax
from jax.experimental import pallas as pl
from jax.experimental.pallas import tpu as pltpu
from jax.sharding import PartitionSpec as P


H = 17
E = 64

norm_eps = 1e-05
neg_fill = -1e30
clip_limit = 8.0

SCALE = 0.02

f32 = jnp.float32
bf16 = jnp.bfloat16

VMEM = pl.BlockSpec(memory_space=pltpu.VMEM)
SMEM = pl.BlockSpec(memory_space=pltpu.SMEM)
ANY = pl.BlockSpec(memory_space=pl.ANY)


def dot_nn(left, right):
    return lax.dot_general(left, right, (((1,), (0,)), ((), ())), preferred_element_type=f32)


def dot_nt(left, right):
    return lax.dot_general(left, right, (((1,), (1,)), ((), ())), preferred_element_type=f32)


def dot_tn(left, right):
    return lax.dot_general(left, right, (((0,), (0,)), ((), ())), preferred_element_type=f32)


def params(mib=16):
    return pltpu.CompilerParams(vmem_limit_bytes=mib * 2**20)


def cost(flops, moved, exps=0):
    return pl.CostEstimate(
        flops=int(flops * SCALE), bytes_accessed=int(moved * SCALE), transcendentals=int(exps * SCALE)
    )


def waiting(body, inputs, count):
    def wrapped(*refs):
        return body(*refs[:inputs], *refs[inputs + count :])

    return wrapped


def shape(dims, kind):
    return jax.ShapeDtypeStruct(dims, kind)


def rows_at(start, length):
    return pl.ds(pl.multiple_of(start, 16), length)


def assemble_body(plan, fill, turned, starts, *refs):
    pieces, out_ref = (refs[:-2], refs[-2]) if turned else (refs[:-1], refs[-1])
    for piece, source, length, where in plan:
        out_ref[rows_at(starts[where], length), :] = pieces[piece][source : source + length, :]
    if turned:
        rows = out_ref.shape[0]
        refs[-1][:rows, :] = out_ref[...].T
        refs[-1][rows:, :] = jnp.zeros((fill, rows), bf16)


def whole(array):
    return VMEM


def assemble(starts, pieces, plan, rows, fill=0, turned=False):
    result = shape((rows, pieces[0].shape[1]), bf16)
    results = [result, shape((rows + fill, rows), bf16)] if turned else result
    return pl.pallas_call(
        functools.partial(assemble_body, tuple(plan), fill, turned),
        grid_spec=pltpu.PrefetchScalarGridSpec(
            num_scalar_prefetch=1,
            grid=(1,),
            in_specs=[whole(piece) for piece in pieces],
            out_specs=[whole(each) for each in results] if turned else whole(result),
        ),
        out_shape=results,
        compiler_params=params(),
        cost_estimate=cost(0, rows * result.shape[1] * 4),
        name="assemble",
    )(starts, *pieces)


def first_norm_body(own, order, p0, p1, p2, p3, *refs):
    if own:
        x_ref, n_ref, stat_ref, vec_ref, dy_ref = refs
    else:
        vec_ref, x_ref, n_ref, stat_ref = refs
    part = p0.shape[0]
    full, count = x_ref.shape
    if own:
        vec_ref[full:, :] = jnp.zeros((vec_ref.shape[0] - full, vec_ref.shape[1]), f32)
    for n, piece in enumerate((p0, p1, p2, p3)):
        where = rows_at(order[n] * part, part)
        x_ref[where, :] = piece[:, :count]
        if own:
            vec_ref[where, :] = piece[:, count : count + 128].astype(f32)
            dy_ref[where, :] = piece[:, count + 128 :]
    for start in range(0, count, 256):
        cols = slice(start, start + 256)
        x = x_ref[:, cols].astype(f32)
        mean = jnp.sum(x, axis=0, keepdims=True) * (1.0 / full)
        center = x - mean
        inv = lax.rsqrt(jnp.sum(center * center, axis=0, keepdims=True) * (1.0 / full) + norm_eps)
        n_ref[:, cols] = (center * inv * vec_ref[:full, 0:1] + vec_ref[:full, 1:2]).astype(bf16)
        stat_ref[0:1, cols] = mean
        stat_ref[1:2, cols] = inv


def first_norm(order, pieces, count, vectors=None):
    own = vectors is None
    full = pieces[0].shape[0] * 4
    results = [shape((full, count), bf16), shape((full, count), bf16), shape((8, count), f32)]
    operands = list(pieces)
    if own:
        results += [shape((full + E, 128), f32), shape((full, count), bf16)]
    else:
        operands.append(vectors)
    return pl.pallas_call(
        functools.partial(first_norm_body, own),
        grid_spec=pltpu.PrefetchScalarGridSpec(
            num_scalar_prefetch=1,
            grid=(1,),
            in_specs=[whole(array) for array in operands],
            out_specs=[whole(result) for result in results],
        ),
        out_shape=results,
        compiler_params=params(),
        cost_estimate=cost(20 * full * count, full * count * 8),
        name="first_norm",
    )(order, *operands)


def near_rows_body(order, own, left, right, pick_own, base_ref, edge_ref, out_ref):
    size = own.shape[0]
    wide = pick_own.shape[0]
    spare = edge_ref.shape[1]
    for n, piece in ((0, own), (1, left), (3, right)):
        where = rows_at(order[n] * size, size)
        base_ref[where, :] = dot_nn(piece[:, :wide], pick_own[...]).astype(bf16)
        out_ref[where, :] = piece[:, wide:]
        edge_rows(piece, edge_ref, where, wide // 3)


def edge_rows(piece, edge_ref, where, part):
    spare = 5 * E - part
    for p in range(3):
        edge_ref[where, p * spare : (p + 1) * spare] = piece[:, p * part : p * part + spare]


def far_rows_body(order, base, edge, out, far_a, far_b, pick_own, base_ref, edge_ref, turned_ref, out_s):
    size, cut = base.shape[0] // 4, far_a.shape[0]
    wide = pick_own.shape[0]
    base_ref[...] = base[...]
    edge_ref[...] = edge[...]
    out_s[...] = out[...]
    for piece, extra in ((far_a, 0), (far_b, cut)):
        where = rows_at(order[2] * size + extra, piece.shape[0])
        base_ref[where, :] = dot_nn(piece[:, :wide], pick_own[...]).astype(bf16)
        out_s[where, :] = piece[:, wide:]
        edge_rows(piece, edge_ref, where, wide // 3)
    turned_ref[...] = out_s[...].T


def given_body(info, one_ref, two_ref, out_ref, *more):
    give = out_ref.shape[0] // (2 * (one_ref.shape[0] // 176))
    at = 0
    for piece in (one_ref, two_ref):
        for first in range(0, piece.shape[0], 176):
            out_ref[at : at + give, :] = piece[rows_at(first + info[0], give), :]
            at += give
    if more:
        more[0][...] = one_ref[:176, :]
        more[1][...] = two_ref[176:, :]


def given_rows(info, one, two, give):
    parts = one.shape[0] // 176
    columns = one.shape[1]
    results = [shape((2 * parts * give, columns), bf16)]
    if parts == 2:
        results += [shape((176, columns), bf16)] * 2
    return pl.pallas_call(
        given_body,
        grid_spec=pltpu.PrefetchScalarGridSpec(
            num_scalar_prefetch=1, grid=(1,), in_specs=[VMEM] * 2, out_specs=[VMEM] * len(results)
        ),
        out_shape=results,
        compiler_params=params(),
        cost_estimate=cost(0, 3 * 10**6),
        name="given_rows",
    )(info, one, two)


def near_rows(order, pieces, pick_own):
    size = pieces[0].shape[0]
    results = [
        shape((4 * size, pick_own.shape[1]), bf16),
        shape((4 * size, 256), bf16),
        shape((4 * size, size), bf16),
    ]
    return pl.pallas_call(
        near_rows_body,
        grid_spec=pltpu.PrefetchScalarGridSpec(
            num_scalar_prefetch=1, grid=(1,), in_specs=[VMEM] * 4, out_specs=[VMEM] * 3
        ),
        out_shape=results,
        compiler_params=params(),
        cost_estimate=cost(2 * 816 * 816 * 960, 6 * 10**6),
        name="near_rows",
    )(order, *pieces, pick_own)


def far_rows(order, near, far, pick_own, wait):
    size = near[0].shape[0] // 4
    results = [
        shape(near[0].shape, bf16),
        shape(near[1].shape, bf16),
        shape((size, 4 * size), bf16),
    ]
    return pl.pallas_call(
        waiting(far_rows_body, 7, 1),
        grid_spec=pltpu.PrefetchScalarGridSpec(
            num_scalar_prefetch=1,
            grid=(1,),
            in_specs=[VMEM] * 6 + [ANY],
            out_specs=[VMEM] * 3,
            scratch_shapes=[pltpu.VMEM((4 * size, size), bf16)],
        ),
        out_shape=results,
        compiler_params=params(),
        cost_estimate=cost(2 * 272 * 816 * 960, 6 * 10**6),
        name="far_rows",
    )(order, *near, *far, pick_own, wait)


def project_body(width, info, base_ref, edge_ref, pick_ref, bias_ref, own_ref, before_ref, q_ref, kv_ref, w_ref, w_s):
    step = pl.program_id(0)
    half = pl.num_programs(0) // 2
    mine = (step // half) == info[0]

    @pl.when(step == 0)
    def _():
        edges = edge_ref[:, : pick_ref.shape[0]]
        w_ref[...] = base_ref[...] + dot_nn(edges, pick_ref[...]).astype(bf16)
        w_s[...] = w_ref[...].T

    def keyvals(n_ref):
        kv_ref[:width, :] = dot_nn(w_s[width : 2 * width, :], n_ref[...]).astype(bf16)
        kv_ref[width:, :] = (
            dot_nn(w_s[2 * width :, :], n_ref[...]) + bias_ref[rows_at(info[1], width), 5:6]
        ).astype(bf16)

    @pl.when(mine)
    def _():
        out = dot_nn(w_s[:width, :], own_ref[...]) + bias_ref[rows_at(info[1], width), 4:5]
        q_ref[...] = (out.astype(bf16).astype(f32) * E ** (-0.5)).astype(bf16)
        keyvals(own_ref)

    @pl.when(jnp.logical_not(mine))
    def _():
        keyvals(before_ref)


def project(info, base, edges, pick_next, bias, own, before, block=512):
    full, count = own.shape
    wide = base.shape[1]
    width = wide // 3
    steps = count // block
    return pl.pallas_call(
        functools.partial(project_body, width),
        grid_spec=pltpu.PrefetchScalarGridSpec(
            num_scalar_prefetch=1,
            grid=(2 * steps,),
            in_specs=[
                VMEM,
                VMEM,
                VMEM,
                VMEM,
                pl.BlockSpec((full, block), lambda i, s: (0, jnp.clip(i - s[0] * steps, 0, steps - 1))),
                pl.BlockSpec(
                    (full, block), lambda i, s: (0, jnp.clip(i - (1 - s[0]) * steps, 0, steps - 1))
                ),
            ],
            out_specs=[
                pl.BlockSpec((width, block), lambda i, s: (0, jnp.clip(i - s[0] * steps, 0, steps - 1))),
                pl.BlockSpec((2 * width, block), lambda i, s: (0, i)),
                VMEM,
            ],
            scratch_shapes=[pltpu.VMEM((wide, full), bf16)],
        ),
        out_shape=[
            shape((width, count), bf16),
            shape((2 * width, 2 * count), bf16),
            shape((full, wide), bf16),
        ],
        compiler_params=params(24),
        cost_estimate=cost(2 * full * count * 5 * width, 10 * 10**6),
        name="project",
    )(info, base, edges, pick_next, bias, own, before)


def block_limits(info, block, rows):
    prefix_len = info[0]
    query_lo = info[1] + block * rows
    query_hi = query_lo + rows - 1
    in_prefix = query_lo < prefix_len
    limit_max = jnp.where(in_prefix, jnp.maximum(prefix_len - 1, query_hi), query_hi)
    limit_min = jnp.where(in_prefix, prefix_len - 1, query_lo)
    positions = query_lo + lax.broadcasted_iota(jnp.int32, (1, rows), 1)
    return limit_max, limit_min, jnp.where(positions < prefix_len, prefix_len - 1, positions)


def attn_fwd_body(
    slots, keys, first, info, q_ref, kv_ref, attn_ref, exact_ref, lse_ref, top_ref, k_s, m_s, l_s, acc_s
):
    width, rows = q_ref.shape
    limit_max, limit_min, limit = block_limits(info, first, rows)
    n_need = limit_max // keys + 1
    n_full = (limit_min + 1) // keys
    for h in range(slots):
        k_s[h] = kv_ref[h * E : h * E + E, :].T
    m_s[...] = jnp.full_like(m_s, neg_fill)
    l_s[...] = jnp.zeros_like(l_s)
    acc_s[...] = jnp.zeros_like(acc_s)

    def step(index, masked):
        start = pl.multiple_of(index * keys, keys)
        if masked:
            seen = (start + lax.broadcasted_iota(jnp.int32, (keys, rows), 0)) <= limit
        for h in range(slots):
            here, row = slice(h * E, h * E + E), slice(h, h + 1)
            scores = dot_nn(k_s[h, pl.ds(start, keys), :], q_ref[here, :])
            if masked:
                scores = jnp.where(seen, scores, neg_fill)
            old_max = m_s[row, :]
            new_max = jnp.maximum(old_max, jnp.max(scores, axis=0, keepdims=True))
            weights = jnp.exp(scores - new_max)
            shrink = jnp.exp(old_max - new_max)
            l_s[row, :] = l_s[row, :] * shrink + jnp.sum(weights, axis=0, keepdims=True)
            values = kv_ref[width + h * E : width + h * E + E, pl.ds(start, keys)]
            acc_s[here, :] = acc_s[here, :] * shrink + dot_nn(values, weights.astype(bf16))
            m_s[row, :] = new_max

    @pl.loop(0, n_full)
    def _(index):
        step(index, False)

    @pl.loop(n_full, n_need)
    def _(index):
        step(index, True)

    for h in range(slots):
        here, row = slice(h * E, h * E + E), slice(h, h + 1)
        outcome = acc_s[here, :] / l_s[row, :]
        exact_ref[here, :] = outcome
        attn_ref[here, :] = outcome.astype(bf16)
    row_max = m_s[...]
    lse_ref[...] = row_max + jnp.log(l_s[...])
    top = row_max[:, :128]
    for start in range(128, rows, 128):
        top = jnp.maximum(top, row_max[:, start : start + 128])
    top_ref[...] = top


def attn_fwd(info, queries, kv_all, slots, first, rows=512, keys=512):
    width = queries.shape[0]
    total = kv_all.shape[1]
    return pl.pallas_call(
        functools.partial(attn_fwd_body, slots, keys, first),
        grid_spec=pltpu.PrefetchScalarGridSpec(
            num_scalar_prefetch=1,
            grid=(1,),
            in_specs=[
                pl.BlockSpec((width, rows), lambda i, _: (0, first)),
                pl.BlockSpec((2 * width, total), lambda i, _: (0, 0)),
            ],
            out_specs=[
                pl.BlockSpec((width, rows), lambda i, _: (0, 0)),
                pl.BlockSpec((width, rows), lambda i, _: (0, 0)),
                pl.BlockSpec((8, rows), lambda i, _: (0, 0)),
                pl.BlockSpec((8, 128), lambda i, _: (0, 0)),
            ],
            scratch_shapes=[
                pltpu.VMEM((slots, total, E), bf16),
                pltpu.VMEM((8, rows), f32),
                pltpu.VMEM((8, rows), f32),
                pltpu.VMEM((width, rows), f32),
            ],
        ),
        out_shape=[
            shape((width, rows), bf16),
            shape((width, rows), f32),
            shape((8, rows), f32),
            shape((8, 128), f32),
        ],
        compiler_params=params(40),
        cost_estimate=cost(8 * 10**9, 6 * 10**6, 4 * 10**6),
        name="attn_fwd",
    )(info, queries, kv_all)


def attn_bwd_body(slots, keys, key_first, more, last, info, *refs):
    if more:
        q_ref, kv_ref, do_ref, o_ref, lse_ref, dq_in, dq_ref, dkv_ref, k_s, v_s, acc_s, dkv_s = refs
    else:
        q_ref, kv_ref, do_ref, o_ref, lse_ref, dq_ref, dkv_ref, k_s, v_s, acc_s, dkv_s = refs
    block = pl.program_id(0)
    width, rows = q_ref.shape
    n_blocks = kv_ref.shape[1] // keys
    limit_max, limit_min, limit = block_limits(info, block, rows)
    n_need = jnp.clip((limit_max - key_first) // keys + 1, 0, n_blocks)
    n_full = jnp.clip((limit_min - key_first + 1) // keys, 0, n_blocks)
    limit = limit - key_first

    @pl.when(block == 0)
    def _():
        dkv_s[...] = jnp.zeros_like(dkv_s)
        for h in range(slots):
            k_s[h] = kv_ref[h * E : h * E + E, :].T
            v_s[h] = kv_ref[width + h * E : width + h * E + E, :].T

    if more:
        acc_s[...] = dq_in[...]
    else:
        acc_s[...] = jnp.zeros_like(acc_s)
    dots = [
        jnp.sum(
            do_ref[h * E : h * E + E, :].astype(f32) * o_ref[h * E : h * E + E, :],
            axis=0,
            keepdims=True,
        )
        for h in range(slots)
    ]

    def step(index, masked):
        start = pl.multiple_of(index * keys, keys)
        where = pl.ds(start, keys)
        if masked:
            seen = (start + lax.broadcasted_iota(jnp.int32, (keys, rows), 0)) <= limit
        for h in range(slots):
            here = slice(h * E, h * E + E)
            there = slice(width + h * E, width + h * E + E)
            q_head, do_head = q_ref[here, :], do_ref[here, :]
            probs = jnp.exp(dot_nn(k_s[h, where, :], q_head) - lse_ref[h : h + 1, :])
            if masked:
                probs = jnp.where(seen, probs, 0.0)
            grad_probs = dot_nn(v_s[h, where, :], do_head)
            grad_scores = (probs * (grad_probs - dots[h])).astype(bf16)
            dkv_s[there, where] += dot_nt(do_head, probs.astype(bf16))
            dkv_s[here, where] += dot_nt(q_head, grad_scores)
            acc_s[here, :] += dot_nn(kv_ref[here, where], grad_scores)

    @pl.loop(0, n_full)
    def _(index):
        step(index, False)

    @pl.loop(n_full, n_need)
    def _(index):
        step(index, True)

    if last:
        dq_ref[...] = (acc_s[...] * E ** (-0.5)).astype(bf16)
    else:
        dq_ref[...] = acc_s[...]

    @pl.when(block == pl.num_programs(0) - 1)
    def _():
        dkv_ref[...] = dkv_s[...].astype(bf16)


def attn_bwd(
    info, queries, kv_all, grad_attn, exact, lse, dq_in, slots, segment, last, rows=512, keys=512
):
    width, count = queries.shape
    more = dq_in is not None
    block = pl.BlockSpec((width, rows), lambda i, _: (0, i))
    return pl.pallas_call(
        functools.partial(attn_bwd_body, slots, keys, segment * count, more, last),
        grid_spec=pltpu.PrefetchScalarGridSpec(
            num_scalar_prefetch=1,
            grid=(count // rows,),
            in_specs=[
                block,
                pl.BlockSpec((2 * width, count), lambda i, _: (0, segment)),
                block,
                block,
                pl.BlockSpec((8, rows), lambda i, _: (0, i)),
            ]
            + [block] * more,
            out_specs=[block, pl.BlockSpec((2 * width, count), lambda i, _: (0, 0))],
            scratch_shapes=[
                pltpu.VMEM((slots, count, E), bf16),
                pltpu.VMEM((slots, count, E), bf16),
                pltpu.VMEM((width, rows), f32),
                pltpu.VMEM((2 * width, count), f32),
            ],
        ),
        out_shape=[
            shape((width, count), bf16 if last else f32),
            shape((2 * width, count), bf16),
        ],
        compiler_params=params(40),
        cost_estimate=cost(16 * 10**9, 6 * 10**6, 4 * 10**6),
        name="attn_bwd",
    )(info, queries, kv_all, grad_attn, exact, lse, *([dq_in] if more else []))


def out_norm_body(starts, p0, p1, p2, p3, w_ref, x_ref, vec_ref, after_ref, n_ref, stat_ref, attn_ref):
    fewer = (attn_ref.shape[0] // E) // 4 * E
    for n, piece in enumerate((p0, p1, p2, p3)):
        attn_ref[rows_at(starts[n], fewer), :] = piece[:fewer, :]

        @pl.when(starts[n] == 0)
        def _():
            attn_ref[fewer : piece.shape[0], :] = piece[fewer:, :]

    full, count = x_ref.shape
    for start in range(0, count, 256):
        cols = slice(start, start + 256)
        after = x_ref[:, cols].astype(f32) + (
            dot_nn(w_ref[...], attn_ref[:, cols]) + vec_ref[:full, 6:7]
        )
        mean = jnp.sum(after, axis=0, keepdims=True) * (1.0 / full)
        center = after - mean
        inv = lax.rsqrt(jnp.sum(center * center, axis=0, keepdims=True) * (1.0 / full) + norm_eps)
        after_ref[:, cols] = after
        n_ref[:, cols] = (center * inv * vec_ref[:full, 2:3] + vec_ref[:full, 3:4]).astype(bf16)
        stat_ref[0:1, cols] = mean
        stat_ref[1:2, cols] = inv


def out_norm(starts, pieces, w_out_t, x_full, vectors, first):
    full = x_full.shape[0]
    rows, count = pieces[0].shape
    grid_spec = pltpu.PrefetchScalarGridSpec(
        num_scalar_prefetch=1,
        grid=(1,),
        in_specs=[whole(piece) for piece in pieces]
        + [
            pl.BlockSpec(w_out_t.shape, lambda i, _: (0, 0)),
            pl.BlockSpec((full, count), lambda i, _: (0, first)),
            pl.BlockSpec(vectors.shape, lambda i, _: (0, 0)),
        ],
        out_specs=[
            pl.BlockSpec((full, count), lambda i, _: (0, 0)),
            pl.BlockSpec((full, count), lambda i, _: (0, 0)),
            pl.BlockSpec((8, count), lambda i, _: (0, 0)),
            pl.BlockSpec((full, count), lambda i, _: (0, 0)),
        ],
    )
    return pl.pallas_call(
        out_norm_body,
        grid_spec=grid_spec,
        out_shape=[
            shape((full, count), f32),
            shape((full, count), bf16),
            shape((8, count), f32),
            shape((full, count), bf16),
        ],
        compiler_params=params(24),
        cost_estimate=cost(2 * full * full * count, 10**7),
        name="out_norm",
    )(starts, *pieces, w_out_t, x_full, vectors)


def erf_parts(v):
    return 0.5 * (1.0 + lax.erf(v * (0.5**0.5))), jnp.exp(-0.5 * v * v)


def feed_body(
    info, n_ref, dy_ref, up_ref, down_t_ref, b_ref, act_ref, grad_ref, theirs_ref, mine_ref, bias_ref, up_s, down_s
):
    step = pl.program_id(0)

    @pl.when(step == 0)
    def _():
        up_s[...] = up_ref[...].T
        down_s[...] = down_t_ref[...].T
        bias_ref[...] = jnp.zeros_like(bias_ref)

    pre = dot_nn(up_s[...], n_ref[...]) + b_ref[:, 0:1]
    grad_act = dot_nn(down_s[...], dy_ref[...])
    cdf, bell = erf_parts(pre)
    act_ref[...] = (pre * cdf).astype(bf16)
    grad = (grad_act * (cdf + pre * bell * 0.3989422804014327)).astype(bf16)
    grad_ref[...] = grad
    bias_ref[...] += dot_nn(grad, jnp.ones((grad.shape[1], 128), bf16))
    part = dot_nn(up_ref[...], grad).astype(bf16)

    @pl.when(step < 2)
    def _():
        theirs_ref[0] = part

    @pl.when(step >= 2)
    def _():
        mine_ref[0] = part


def turn(step, info):
    return jnp.where(step < 2, 2 * step + 1 - info[0], 2 * (step - 2) + info[0])


def feed(core, normed, dy, w_up, w_down_t, bias):
    full, count = normed.shape
    hidden = w_up.shape[1]
    block = count // 4
    cols = pl.BlockSpec((full, block), lambda i, c: (0, turn(i, c)))
    hid = pl.BlockSpec((hidden, block), lambda i, c: (0, turn(i, c)))
    return pl.pallas_call(
        feed_body,
        grid_spec=pltpu.PrefetchScalarGridSpec(
            num_scalar_prefetch=1,
            grid=(4,),
            in_specs=[
                cols,
                cols,
                pl.BlockSpec((full, hidden), lambda i, c: (0, 0)),
                pl.BlockSpec((full, hidden), lambda i, c: (0, 0)),
                pl.BlockSpec((hidden, 1), lambda i, c: (0, 0)),
            ],
            out_specs=[
                hid,
                hid,
                pl.BlockSpec((1, full, block), lambda i, c: (jnp.minimum(i, 1), 0, 0)),
                pl.BlockSpec((1, full, block), lambda i, c: (jnp.maximum(i - 2, 0), 0, 0)),
                pl.BlockSpec((hidden, 128), lambda i, c: (0, 0)),
            ],
            scratch_shapes=[pltpu.VMEM((hidden, full), bf16), pltpu.VMEM((hidden, full), bf16)],
        ),
        out_shape=[
            shape((hidden, count), bf16),
            shape((hidden, count), bf16),
            shape((2, full, block), bf16),
            shape((2, full, block), bf16),
            shape((hidden, 128), f32),
        ],
        compiler_params=params(40),
        cost_estimate=cost(6 * full * hidden * count, 2 * 10**7, 2 * hidden * count),
        name="feed",
    )(core, normed, dy, w_up, w_down_t, bias)


def second_back_body(index, mine_ref, got_ref, across_ref, after_ref, dy_ref, stat_ref, vec_ref, out_ref, sums_ref):
    back = mine_ref[0].astype(f32) + got_ref[0].astype(f32) + across_ref[...].astype(f32)
    full = back.shape[0]
    mean, inv = stat_ref[0:1, :], stat_ref[1:2, :]
    unit = (after_ref[...] - mean) * inv
    grad = back * vec_ref[:full, 2:3]
    first = jnp.sum(grad, axis=0, keepdims=True) * (1.0 / full)
    second = jnp.sum(grad * unit, axis=0, keepdims=True) * (1.0 / full)
    total = dy_ref[...].astype(f32) + inv * (grad - first - unit * second)
    low = total.astype(bf16)
    out_ref[...] = low
    sums_ref[:, 0:1] = jnp.sum(back * unit, axis=1, keepdims=True)
    sums_ref[:, 1:2] = jnp.sum(back, axis=1, keepdims=True)
    sums_ref[:, 2:3] = jnp.sum(low.astype(f32), axis=1, keepdims=True)


def second_back(index, mine, got, across, after, dy, stats, vectors):
    full, count = across.shape
    fixed = pl.BlockSpec((full, count), lambda i, c: (0, 0))
    moved = pl.BlockSpec((full, count), lambda i, c: (0, c[0]))
    part = pl.BlockSpec((1, full, count), lambda i, c: (c[1], 0, 0))
    return pl.pallas_call(
        second_back_body,
        grid_spec=pltpu.PrefetchScalarGridSpec(
            num_scalar_prefetch=1,
            grid=(1,),
            in_specs=[
                part,
                part,
                fixed,
                moved,
                moved,
                pl.BlockSpec((8, count), lambda i, c: (0, c[0])),
                pl.BlockSpec(vectors.shape, lambda i, c: (0, 0)),
            ],
            out_specs=[fixed, pl.BlockSpec((full, 8), lambda i, c: (0, 0))],
        ),
        out_shape=[shape((full, count), bf16), shape((full, 8), f32)],
        compiler_params=params(16),
        cost_estimate=cost(20 * full * count, 5 * 10**6),
        name="second_back",
    )(index, mine, got, across, after, dy, stats, vectors)


def attn_grad_body(info, p0, p1, p2, p3, w_ref, branch_ref, out_ref):
    count = p0.shape[1]
    width = out_ref.shape[0]
    weights = w_ref[rows_at(info[0], width), :]
    real = lax.broadcasted_iota(jnp.int32, (width, 1), 0) < info[1]
    for n, piece in enumerate((p0, p1, p2, p3)):
        cols = pl.ds(pl.multiple_of(info[2 + n] * count, 128), count)
        branch_ref[:, cols] = piece[...]
        out_ref[:, cols] = jnp.where(real, dot_nn(weights, piece[...]), 0.0).astype(bf16)


def attn_grad(info, pieces, w_out, width):
    full, quarter = pieces[0].shape
    results = [shape((full, 4 * quarter), bf16), shape((width, 4 * quarter), bf16)]
    return pl.pallas_call(
        attn_grad_body,
        grid_spec=pltpu.PrefetchScalarGridSpec(
            num_scalar_prefetch=1,
            grid=(1,),
            in_specs=[whole(array) for array in (*pieces, w_out)],
            out_specs=[whole(result) for result in results],
        ),
        out_shape=results,
        compiler_params=params(),
        cost_estimate=cost(8 * full * quarter * width, 10**7),
        name="attn_grad",
    )(info, *pieces, w_out)


def one_back_body(info, w_ref, dq_ref, one_ref, there_ref, two_ref, theirs_ref, mine_ref, grad_ref):
    step = pl.program_id(0)
    width = dq_ref.shape[0]

    @pl.when(step == 0)
    def _():
        grad_ref[:width, :] = dq_ref[...]

    @pl.when((step == 0) & (info[1] == 0))
    def _():
        grad_ref[width:, :] = (one_ref[...].astype(f32) + there_ref[...].astype(f32)).astype(bf16)

    @pl.when((step == 0) & (info[1] != 0))
    def _():
        grad_ref[width:, :] = two_ref[...]

    part = dot_nn(w_ref[0], grad_ref[...]).astype(bf16)

    @pl.when(step < 2)
    def _():
        theirs_ref[0] = part

    @pl.when(step >= 2)
    def _():
        mine_ref[0] = part


def one_back(info, w_heads, dq, dkv_one, dkv_there, dkv_two, wait):
    full, wide = w_heads.shape
    count = dq.shape[1]
    part = full // 4
    parts = shape((2, part, count), bf16)
    return pl.pallas_call(
        waiting(one_back_body, 6, 1),
        grid_spec=pltpu.PrefetchScalarGridSpec(
            num_scalar_prefetch=1,
            grid=(4,),
            in_specs=[pl.BlockSpec((1, part, wide), lambda i, c: (turn(i, c), 0, 0))]
            + [whole(array) for array in (dq, dkv_one, dkv_there, dkv_two)]
            + [ANY],
            out_specs=[
                pl.BlockSpec((1, part, count), lambda i, c: (jnp.minimum(i, 1), 0, 0)),
                pl.BlockSpec((1, part, count), lambda i, c: (jnp.maximum(i - 2, 0), 0, 0)),
            ],
            scratch_shapes=[pltpu.VMEM((wide, count), bf16)],
        ),
        out_shape=[parts, parts],
        compiler_params=params(16),
        cost_estimate=cost(2 * full * wide * count, 10**7),
        name="one_back",
    )(info, w_heads.reshape(4, part, wide), dq, dkv_one, dkv_there, dkv_two, wait)


def weight_grad_body(info, own_ref, before_ref, dq_ref, one_ref, two_ref, theirs_ref, mine_ref, acc_ref):
    width = dq_ref.shape[0]
    acc_ref[:, :width] = dot_nt(own_ref[...], dq_ref[...])

    @pl.when(info[0] == 0)
    def _():
        acc_ref[:, width:] = dot_nt(own_ref[...], one_ref[...])

    @pl.when(info[0] != 0)
    def _():
        acc_ref[:, width:] = dot_nt(before_ref[...], one_ref[...]) + dot_nt(own_ref[...], two_ref[...])

    chunk = theirs_ref.shape[1]
    for k in range(4):
        theirs = ((1 - info[0]) * 4 + k) * chunk
        mine = (info[0] * 4 + k) * chunk
        theirs_ref[k] = acc_ref[pl.ds(pl.multiple_of(theirs, 8), chunk), :].astype(bf16)
        mine_ref[k] = acc_ref[pl.ds(pl.multiple_of(mine, 8), chunk), :].astype(bf16)


def weight_grad(info, own, before, dq, dkv_one, dkv_two):
    rows, count = own.shape
    columns = 3 * dq.shape[0]
    result = shape((4, rows // 8, columns), bf16)
    operands = [own, before, dq, dkv_one, dkv_two]
    return pl.pallas_call(
        weight_grad_body,
        grid_spec=pltpu.PrefetchScalarGridSpec(
            num_scalar_prefetch=1,
            grid=(1,),
            in_specs=[whole(array) for array in operands],
            out_specs=[whole(result), whole(result)],
            scratch_shapes=[pltpu.VMEM((rows, columns), f32)],
        ),
        out_shape=[result, result],
        compiler_params=params(24),
        cost_estimate=cost(3 * rows * columns * count, 8 * 10**6),
        name="weight_grad",
    )(info, *operands)


def product_body(left_ref, right_ref, out_ref):
    out_ref[...] = dot_nt(left_ref[...], right_ref[...]).astype(bf16)


def product(left, right):
    rows, count = left.shape
    columns = right.shape[0]
    return pl.pallas_call(
        product_body,
        grid=(2,),
        in_specs=[
            pl.BlockSpec((rows // 2, count), lambda i: (i, 0)),
            pl.BlockSpec((columns, count), lambda i: (0, 0)),
        ],
        out_specs=pl.BlockSpec((rows // 2, columns), lambda i: (i, 0)),
        out_shape=shape((rows, columns), bf16),
        compiler_params=params(24),
        cost_estimate=cost(2 * rows * columns * count, 6 * 10**6),
        name="product",
    )(left, right)


X_SWAP = [(0, 2), (2, 0), (1, 3), (3, 1)]
CORE_SWAP = [(0, 1), (1, 0), (2, 3), (3, 2)]


def swap_x(array):
    return lax.ppermute(array, "col", X_SWAP)


def swap_core(array):
    return lax.ppermute(array, "col", CORE_SWAP)


def swap_seq(array):
    return lax.ppermute(array, "seq", [(0, 1), (1, 0)])


def ring(array, axis, shift):
    count = lax.axis_size(axis)
    return lax.ppermute(array, axis, [(i, (i + shift) % count) for i in range(count)])


def after(array, *done):
    return lax.optimization_barrier((array,) + done)[0]


def after_all(arrays, *done):
    return lax.optimization_barrier(tuple(arrays) + done)[: len(arrays)]


def gather_col(shard):
    other = swap_x(shard)
    beside = swap_core(jnp.stack([shard, other]))
    return shard, other, beside[0], beside[1]


def gather_rest(shard, other):
    beside = swap_core(jnp.stack([shard, other]))
    return shard, other, beside[0], beside[1]


def scatter_col(parts, x_bit, core_bit):
    by_core = parts.reshape((2, 2) + parts.shape[1:])
    mine = lax.dynamic_index_in_dim(by_core, core_bit, 1, keepdims=False)
    theirs = lax.dynamic_index_in_dim(by_core, 1 - core_bit, 1, keepdims=False)
    return across_sum(mine, swap_core(theirs), x_bit)


def across_sum(mine, got, x_bit):
    def of(index):
        return lax.dynamic_index_in_dim(mine, index, 0, keepdims=False).astype(
            f32
        ) + lax.dynamic_index_in_dim(got, index, 0, keepdims=False).astype(f32)

    return of(x_bit), swap_x(of(1 - x_bit).astype(bf16))


def seq_halves(partials):
    theirs = jnp.stack([p[0] for p in partials]) if len(partials) > 1 else partials[0][0][None]
    mine = jnp.stack([p[1] for p in partials]) if len(partials) > 1 else partials[0][1][None]
    return mine, swap_seq(theirs)


def row_chunk(halves, offset):
    index = (lax.axis_index("row") + offset) % 4

    def of(array):
        return lax.dynamic_index_in_dim(array, index, 1, keepdims=False).astype(f32)

    return of(halves[0]) + of(halves[1])


def row_sum_one(halves):
    far = row_chunk(halves, 2).astype(bf16)
    if far.shape[0] == 2:
        return ring(far[0], "row", 1), ring(far[1], "row", -1)
    cut = far.shape[2] // 256 * 128
    return ring(far[0, :, :cut], "row", 1), ring(far[0, :, cut:], "row", -1)


def row_sum_two(halves, far):
    to_right, to_left = row_chunk(halves, 1), row_chunk(halves, 3)
    one, two = (part.astype(f32) for part in far)
    if to_right.shape[0] == 2:
        to_right = jnp.stack([to_right[0] + one, to_right[1]])
        to_left = jnp.stack([to_left[0], to_left[1] + two])
    else:
        cut = one.shape[1]
        to_right = jnp.concatenate([to_right[0, :, :cut] + one, to_right[0, :, cut:]], axis=1)[None]
        to_left = jnp.concatenate([to_left[0, :, :cut], to_left[0, :, cut:] + two], axis=1)[None]
    return ring(to_right.astype(bf16), "row", 1), ring(to_left.astype(bf16), "row", -1)


def row_sum_end(halves, near):
    return row_chunk(halves, 0) + near[0].astype(f32) + near[1].astype(f32)


def scatter_row(partial):
    chunks = partial.reshape(2, 4, partial.shape[0] // 8, partial.shape[1])
    return lax.psum_scatter(chunks, "row", scatter_dimension=1, tiled=False)


def scatter_plain(partial):
    return lax.psum_scatter(partial, ("seq", "row"), scatter_dimension=0, tiled=True).astype(f32)


def combine_axis(array, axis, join):
    total = array
    for shift in range(1, lax.axis_size(axis)):
        total = join(total, ring(array, axis, shift))
    return total


def on_device(
    tokens,
    prefix,
    ln1_gain,
    ln1_bias,
    w_qkv,
    b_qv,
    w_out,
    b_out,
    ln2_gain,
    ln2_bias,
    w_up,
    b_up,
    w_down,
    b_down,
    cotangent,
):
    seq_count = lax.axis_size("seq")
    row_count = lax.axis_size("row")
    col_count = lax.axis_size("col")
    fast = seq_count == 2 and row_count == 4
    seq_index = lax.axis_index("seq")
    row_index = lax.axis_index("row")
    col_index = lax.axis_index("col")
    x_bit = col_index // 2
    core_bit = col_index % 2
    span, part = tokens.shape[1], tokens.shape[2]
    full = part * col_count
    quarter = span // col_count
    fewer = H // col_count
    slots = fewer + 1
    width = slots * E
    spare = width - part

    def by_index(pieces):
        own, across, beside, other = pieces
        even = (jnp.where(core_bit == 0, own, beside), jnp.where(core_bit == 0, across, other))
        odd = (jnp.where(core_bit == 0, beside, own), jnp.where(core_bit == 0, other, across))
        return jnp.concatenate(
            [
                jnp.where(x_bit == 0, even[0], even[1]),
                jnp.where(x_bit == 0, odd[0], odd[1]),
                jnp.where(x_bit == 0, even[1], even[0]),
                jnp.where(x_bit == 0, odd[1], odd[0]),
            ],
            axis=1,
        )

    def first_head(device):
        return jnp.where(device == 0, 0, 1 + fewer * device)

    head_first = first_head(col_index)
    head_count = jnp.where(col_index == 0, fewer + 1, fewer)
    column_shift = head_first * E - col_index * part
    info = jnp.stack([prefix[0], seq_index * span]).astype(jnp.int32)
    order = jnp.stack([col_index, col_index ^ 2, col_index ^ 1, col_index ^ 3]).astype(jnp.int32)

    x_shard = tokens[0].T
    dy_shard = cotangent[0].T
    part_rows = w_qkv.shape[0]
    w_flat = w_qkv.reshape(part_rows, 3 * part)

    def own_rows(array):
        return lax.dynamic_slice_in_dim(array, col_index * part, part, 0)

    vectors = jnp.stack(
        [ln1_gain, ln1_bias, ln2_gain, ln2_bias, b_qv[0], b_qv[1], own_rows(b_out)], axis=1
    )
    x_sent = jnp.concatenate([x_shard, jnp.pad(vectors, ((0, 0), (0, 121))), dy_shard], axis=1)

    slot_column = lax.broadcasted_iota(jnp.int32, (1, 3 * width), 1)
    slot_part, slot_index = slot_column // width, slot_column % width
    slot_source = jnp.where(slot_index < head_count * E, slot_index + column_shift, -1)
    own_row = lax.broadcasted_iota(jnp.int32, (3 * part, 1), 0)
    pick_own = ((own_row // part == slot_part) & (own_row % part == slot_source)).astype(bf16)
    next_row = lax.broadcasted_iota(jnp.int32, (3 * spare, 1), 0)
    pick_next = (
        (next_row // spare == slot_part) & (next_row % spare + part == slot_source)
    ).astype(bf16)
    next_to_here = [(i + 1, i) for i in range(col_count - 1)]
    here_to_next = [(i, i + 1) for i in range(col_count - 1)]

    def edge_of(array):
        return jnp.concatenate([array[:, p * part : p * part + spare] for p in range(3)], axis=1)

    where = jnp.stack([seq_index, head_first * E]).astype(jnp.int32)
    core = core_bit[None].astype(jnp.int32)
    if fast:
        w_sent = jnp.concatenate(
            [w_flat, lax.dynamic_slice_in_dim(w_out, col_index * part, part, 1)], axis=1
        )
        left = ring(w_sent, "row", 1)
        right = ring(w_sent, "row", -1)
        x_before = lax.ppermute(x_shard, "seq", [(0, 1)])
        w_order = ((row_index - jnp.arange(4, dtype=jnp.int32)) % 4).astype(jnp.int32)
        near = near_rows(w_order, [w_sent, after(left, x_before), right], pick_own)
        x_pieces = gather_rest(x_sent, after(swap_x(x_sent), near[2]))
        x_full, normed_one, stats_one, columns, dy_full = first_norm(order, x_pieces, span)
        x_across = swap_x(after(x_before, x_pieces[1]))
        cut = part_rows // 32 * 16 + 16
        far_a = ring(left[:cut], "row", 1)
        far_b = ring(right[cut:], "row", -1)
        w_base, edges, out_mine = far_rows(w_order, near, [far_a, far_b], pick_own, normed_one)
        edges = lax.ppermute(edges, "col", next_to_here)
        some, give = 176, 96
        w_down_rows = w_down.T
        up_piece = jnp.concatenate(
            [lax.dynamic_slice_in_dim(w, seq_index * give, some, 0) for w in (w_up, w_down_rows)]
        )
        up_piece = after(up_piece, out_mine)
        up_left = ring(up_piece, "row", 1)
        up_right = ring(up_piece, "row", -1)

        before_pieces = gather_rest(x_before, after(x_across, out_mine))
        _, normed_before, _ = first_norm(order, before_pieces, span, columns)
        out_across = swap_x(after(out_mine, edges))
        queries, kv_all, w_heads = project(
            where, w_base, after(edges, normed_before), pick_next, columns, normed_one, normed_before
        )
        attn_one = attn_fwd(info, queries, kv_all, slots, 0)
        attn_across_one = swap_x(attn_one[0])
        out_pieces = gather_rest(out_mine, after(out_across, attn_one[3]))
        up_left, up_right = after_all((up_left, up_right), attn_one[3])
        lacked = (seq_index * (some - give))[None].astype(jnp.int32)
        near_given, up_on, down_on = given_rows(lacked, up_left, up_right, give)
        near_theirs = swap_seq(near_given)
        far_mine = (ring(up_on, "row", 1), ring(down_on, "row", -1))
        attn_two = attn_fwd(info, after(queries, attn_one[3], near_given), kv_all, slots, 1)
        attn_across_two = swap_x(attn_two[0])
        far_mine = after_all(far_mine, attn_two[3], attn_across_one)
        attn_pieces_one = gather_rest(attn_one[0], after(attn_across_one, attn_two[3]))
        w_out_t, w_out_all = assemble(
            (order * part).astype(jnp.int32),
            after_all(out_pieces, attn_two[3]),
            [(n, 0, part, n) for n in range(4)],
            full,
            E,
            True,
        )
        far_theirs = swap_seq(given_rows(lacked, *far_mine, give)[0])
        def weight(shard, which):
            starts = [row_index * part_rows]
            plan = [(0, 0, part_rows, 0)]
            pieces = [shard, up_left, up_right, far_mine[which], near_theirs, far_theirs]
            mine_at, theirs_at = seq_index * give, (1 - seq_index) * some
            for piece, start, length, away, at in (
                (1, which * some, some, 1, mine_at),
                (2, which * some, some, 3, mine_at),
                (3, 0, some, 2, mine_at),
                (4, which * give, give, 1, theirs_at),
                (4, (2 + which) * give, give, 3, theirs_at),
                (5, which * give, give, 2, theirs_at),
            ):
                plan.append((piece, start, length, len(starts)))
                starts.append((row_index - away) % 4 * part_rows + at)
            return assemble(jnp.stack(starts).astype(jnp.int32), pieces, plan, full)

    else:
        x_pieces = gather_col(x_sent)
        x_full, normed_one, stats_one, columns, dy_full = first_norm(order, x_pieces, span)
        w_all = lax.all_gather(w_flat, "row", axis=0, tiled=True)
        edges = lax.ppermute(edge_of(w_all), "col", next_to_here)
        w_heads = (dot_nn(w_all, pick_own) + dot_nn(edges, pick_next)).astype(bf16)
        bias = lax.dynamic_slice_in_dim(columns, head_first * E, width, 0)
        projected = dot_tn(w_heads, normed_one)
        queries = (
            (projected[:width] + bias[:, 4:5]).astype(bf16) * E ** (-0.5)
        ).astype(bf16)
        keyvals = jnp.concatenate(
            [projected[width : 2 * width], projected[2 * width :] + bias[:, 5:6]]
        ).astype(bf16)
        kv_all = lax.all_gather(keyvals, "seq", axis=1, tiled=True)
        attn_one = attn_fwd(info, queries, kv_all, slots, 0)
        attn_two = attn_fwd(info, queries, kv_all, slots, 1)
        attn_pieces_one = gather_col(attn_one[0])
        attn_pieces_two = gather_col(attn_two[0])
        w_out_all = jnp.pad(lax.all_gather(w_out, "row", axis=0, tiled=True), ((0, E), (0, 0)))
        w_out_t = w_out_all[:full].T
        w_up_all = lax.all_gather(w_up, "row", axis=0, tiled=True)
        w_down_t = lax.all_gather(w_down.T, "row", axis=0, tiled=True)

    head_rows = (first_head(order) * E).astype(jnp.int32)
    normal_one = out_norm(head_rows, attn_pieces_one, w_out_t, x_full, columns, 0)
    if fast:
        attn_pieces_two = gather_rest(attn_two[0], after(attn_across_two, normal_one[2]))
    normal_two = out_norm(head_rows, attn_pieces_two, w_out_t, x_full, columns, 1)
    if fast:
        far_theirs = after(far_theirs, normal_two[2])
        w_up_all = weight(w_up, 0)
        w_down_t = weight(w_down_rows, 1)

    def joined(index):
        return jnp.concatenate([normal_one[index], normal_two[index]], axis=1)

    after_attn, normed_two, stats_two, attn_all = (joined(i) for i in range(4))
    exact = jnp.concatenate([attn_one[1], attn_two[1]], axis=1)
    lse = jnp.concatenate([attn_one[2], attn_two[2]], axis=1)
    tops = jnp.max(jnp.maximum(attn_one[3], attn_two[3]), axis=1)

    slot_head = jnp.arange(slots, dtype=jnp.int32)
    head_ids = jnp.arange(H, dtype=jnp.int32)
    my_top = jnp.where(slot_head < head_count, tops[:slots], neg_fill)
    placed_top = jnp.max(
        jnp.where(head_ids[None] == (head_first + slot_head)[:, None], my_top[:, None], neg_fill),
        axis=0,
    )
    placed_top = jnp.pad(placed_top, (0, full - H))

    act, grad_pre, back_theirs, back_mine, bup_sums = feed(
        core, normed_two, dy_full, w_up_all, w_down_t, b_up.astype(f32)[:, None]
    )
    back_core = swap_core(back_theirs)
    back_sent = (
        lax.dynamic_index_in_dim(back_mine, 1 - x_bit, 0, keepdims=False).astype(f32)
        + lax.dynamic_index_in_dim(back_core, 1 - x_bit, 0, keepdims=False).astype(f32)
    ).astype(bf16)
    back_got = swap_x(back_sent)
    up_partial = product(normed_two, after(grad_pre, back_sent))
    down_partial = product(dy_full, after(act, back_sent))

    branch_rows, row_sums = second_back(
        jnp.stack([col_index, x_bit]).astype(jnp.int32),
        back_mine,
        back_core,
        after(back_got, up_partial, down_partial),
        after_attn,
        dy_full,
        stats_two,
        columns,
    )
    branch_across = swap_x(branch_rows)
    if fast:
        down_chunks = down_partial.reshape(2, 4, full // 8, full)

        def down_chunk(offset):
            return lax.dynamic_index_in_dim(down_chunks, (row_index + offset) % 4, 1, keepdims=False)

        down_far = down_chunk(2)
        down_far = ring(down_far[0], "row", 1), ring(down_far[1], "row", -1)
    else:
        down_far = ()
    down = dot_nn(w_down_t, after(act, branch_rows)).astype(bf16).reshape(col_count, part, span)
    head_info = jnp.concatenate([jnp.stack([head_first * E, head_count * E]), order]).astype(jnp.int32)
    branch_pieces = gather_rest(branch_rows, after(branch_across, down, *down_far))
    branch, grad_attn = attn_grad(head_info, branch_pieces, w_out_all, width)
    middle = jnp.concatenate([row_sums[:, :3].T, placed_top[None]])

    def join(one, two):
        return jnp.concatenate([one[:3] + two[:3], jnp.maximum(one[3:4], two[3:4]), one[4:] + two[4:]])

    middle = after(middle, grad_attn)
    middle = join(middle, swap_x(middle))
    middle = join(middle, swap_core(middle))

    branch_own = own_rows(branch)
    out_partial = dot_nt(attn_all, branch_own).astype(bf16)
    if fast:

        def halves_of(partial):
            chunks = partial.reshape(2, 4, partial.shape[0] // 8, partial.shape[1])
            return [
                lax.dynamic_index_in_dim(chunks, i, 0, keepdims=False) for i in (1 - seq_index, seq_index)
            ]

        feed_halves = seq_halves([halves_of(up_partial)])
        down_far = after_all(down_far, *branch_pieces[2:])
        to_right, to_left = down_chunk(1).astype(f32), down_chunk(3).astype(f32)
        to_right = jnp.stack([to_right[0] + down_far[0].astype(f32), to_right[1]]).astype(bf16)
        to_left = jnp.stack([to_left[0], to_left[1] + down_far[1].astype(f32)]).astype(bf16)
        down_near = ring(to_right, "row", 1), ring(to_left, "row", -1)
        out_chunks = halves_of(out_partial)
        down_mine, down_got = scatter_col(down, x_bit, core_bit)
        dq_one, dkv_one = attn_bwd(
            info, after(queries, out_partial), kv_all, grad_attn, exact, lse, None, slots, 0, False
        )
        dkv_there = lax.ppermute(dkv_one, "seq", [(1, 0)])
        dq, dkv_two = attn_bwd(
            info,
            after(queries, dq_one, down_got, middle),
            kv_all,
            grad_attn,
            exact,
            lse,
            dq_one,
            slots,
            1,
            True,
        )
        feed_halves = (feed_halves[0], after(feed_halves[1], dq))
        feed_far = row_sum_one(feed_halves)
        chunks = weight_grad(where, normed_one, normed_before, dq, dkv_one, dkv_two)
        halves = seq_halves([[jnp.concatenate(pair, axis=2) for pair in zip(chunks, out_chunks)]])
        one_theirs, one_mine = one_back(
            jnp.stack([core_bit, seq_index]).astype(jnp.int32),
            w_heads,
            dq,
            dkv_one,
            dkv_there,
            dkv_two,
            chunks[0],
        )
        feed_near = row_sum_two(feed_halves, after_all(feed_far, one_theirs))
        down_sums = down_chunk(0).astype(f32) + sum(p.astype(f32) for p in after_all(down_near, dq))
        down_sent = lax.dynamic_index_in_dim(down_sums, 1 - seq_index, 0, keepdims=False).astype(bf16)
        down_sent = swap_seq(after(down_sent, halves[1]))
        down_sums = lax.dynamic_index_in_dim(down_sums, seq_index, 0, keepdims=False)
        one_core = after(swap_core(one_theirs), halves[1])
        one_mine, one_got = across_sum(one_mine, one_core, x_bit)
        last_far = row_sum_one(halves)
        feed_sums = row_sum_end(feed_halves, feed_near)
        last_far = after_all(last_far, down_sent, *feed_near)
        grad_w_up = feed_sums[0]
        grad_w_down = (down_sums + down_sent.astype(f32)).T
        last_near = row_sum_two(halves, last_far)
        last = row_sum_end(halves, after_all(last_near, one_got))[0]
        summed, out_columns = last[:, : 3 * width], last[:, 3 * width :].astype(bf16)
        middle = after(middle, *last_far)
        head_sums = jnp.sum(dq.astype(f32), axis=1), (
            jnp.sum(dkv_one[width:].astype(f32), axis=1) + jnp.sum(dkv_two[width:].astype(f32), axis=1)
        )
    else:
        grad_w_up = scatter_plain(up_partial)
        grad_w_down = scatter_plain(down_partial).T
        out_columns = scatter_plain(out_partial).astype(bf16)
        dq, pieces = None, []
        for segment in range(seq_count):
            dq, dkv_one = attn_bwd(
                info, queries, kv_all, grad_attn, exact, lse, dq, slots, segment, segment == seq_count - 1
            )
            pieces.append(dkv_one)
        dkv = lax.psum_scatter(
            jnp.concatenate(pieces, axis=1), "seq", scatter_dimension=1, tiled=True
        )
        heads_grad = jnp.concatenate([dq, dkv])
        one_parts = dot_nn(w_heads, heads_grad).astype(bf16).reshape(col_count, part, span)
        one_mine, one_got = scatter_col(one_parts, x_bit, core_bit)
        summed = scatter_plain(dot_nt(normed_one, heads_grad).astype(bf16))
        head_sums = jnp.sum(dq.astype(f32), axis=1), jnp.sum(dkv[width:].astype(f32), axis=1)
        down_mine, down_got = scatter_col(down, x_bit, core_bit)
    summed = summed.reshape(-1, 3, width)
    grad_w_out = by_index(gather_col(out_columns)).astype(f32)
    block_out = (
        own_rows(after_attn) + down_mine + down_got.astype(f32) + b_down.astype(f32)[:, None]
    ).astype(bf16)

    def to_owner(array):
        wide_array = jnp.pad(array, ((0, 0), (0, 0), (spare, 0)))
        shifted = wide_array[:, :, spare : spare + width]
        for shift in range(1, col_count):
            amount = 1 + fewer * shift
            offset = amount * E - shift * part
            shifted = jnp.where(
                col_index == shift, wide_array[:, :, spare - offset : spare - offset + width], shifted
            )
        sent = lax.ppermute(shifted[:, :, part:].reshape(-1, 3 * spare), "col", here_to_next)
        return shifted[:, :, :part] + jnp.pad(
            sent.reshape(-1, 3, spare), ((0, 0), (0, 0), (0, part - spare))
        )

    head_sums = jnp.stack(head_sums)
    head_sums = lax.dynamic_update_slice_in_dim(
        jnp.zeros((2, full + E), f32), head_sums, head_first * E, 1
    )[:, :full]

    back_one = one_mine + one_got.astype(f32)
    unit_one = (x_shard.astype(f32) - stats_one[0:1]) * stats_one[1:2]
    unit_grad = back_one * ln1_gain.astype(f32)[:, None]
    sums = jnp.stack([jnp.sum(unit_grad, axis=0), jnp.sum(unit_grad * unit_one, axis=0)])
    sums = jnp.concatenate([jnp.pad(sums, ((0, 0), (0, full - span))) if full > span else sums, head_sums])
    sums = sums + swap_x(sums)
    sums = sums + swap_core(sums)
    bias_grads = lax.dynamic_slice_in_dim(sums[2:], col_index * part, part, 1)
    sums = sums[:2, :span] / full
    grad_tokens = own_rows(branch).astype(f32) + stats_one[1:2] * (
        unit_grad - sums[0:1] - unit_one * sums[1:2]
    )

    small = jnp.concatenate(
        [
            jnp.sum(back_one * unit_one, axis=1),
            jnp.sum(back_one, axis=1),
            jnp.sum(dy_shard.astype(f32), axis=1),
            jnp.zeros((part,), f32),
        ]
    )
    middle = jnp.concatenate(
        [
            middle,
            bup_sums[:, 0][None],
            small[None],
            jnp.pad(bias_grads.reshape(1, -1), ((0, 0), (0, full - 2 * part))),
        ]
    )
    middle = combine_axis(middle, "seq", join)
    grad_w_qkv = to_owner(after(summed, middle))
    middle = combine_axis(middle, "row", join)
    row_vectors, head_max, grad_b_up = middle[:3], middle[3, :H], middle[4]
    own_vectors = lax.dynamic_slice_in_dim(row_vectors, col_index * part, part, 1)

    def piece(start, length):
        return middle[5, start : start + length]

    root_clip = jnp.sqrt(clip_limit / jnp.maximum(head_max, clip_limit))
    column_head = (col_index * part + jnp.arange(part, dtype=jnp.int32)) // E
    one_hot = (column_head[:, None] == head_ids[None, :]).astype(f32)
    column_root = jnp.sum(one_hot * root_clip[None, :], axis=1)
    scale_three = jnp.stack([column_root, column_root, jnp.ones_like(column_root)])
    clipped_qkv = w_qkv.astype(f32) * scale_three[None]
    return (
        block_out.T[None],
        grad_tokens.T[None],
        piece(0, part),
        piece(part, part),
        grad_w_qkv,
        middle[6, : 2 * part].reshape(2, part),
        grad_w_out,
        row_vectors[2],
        own_vectors[0],
        own_vectors[1],
        grad_w_up,
        grad_b_up,
        grad_w_down,
        piece(2 * part, part),
        clipped_qkv,
        head_max,
    )


def solution(mesh):
    placed = (
        P("row", "seq", "col"),
        P("row"),
        P("col"),
        P("col"),
        P("row", None, "col"),
        P(None, "col"),
        P("row", None),
        P(),
        P("col"),
        P("col"),
        P("row", "col"),
        P("col"),
        P("col", "row"),
        P("col"),
        P("row", "seq", "col"),
    )
    return jax.shard_map(
        on_device,
        mesh=mesh,
        in_specs=placed,
        out_specs=(
            P("row", "seq", "col"),
            P("row", "seq", "col"),
            P("col"),
            P("col"),
            P(("seq", "row"), None, "col"),
            P(None, "col"),
            P(("seq", "row"), None),
            P(),
            P("col"),
            P("col"),
            P(("seq", "row"), "col"),
            P("col"),
            P("col", ("seq", "row")),
            P("col"),
            P("row", None, "col"),
            P(),
        ),
        check_vma=False,
    )
```
